32 devices in a mesh: view: 8 (over z, y), plane: 4 (over x, core).
Axes of the slice: x: 2, y: 2, z: 4, core: 2. Of those that a mesh axis runs over, the one named last changes fastest.
Arguments:
- features: bfloat16 [32, 32, 512], P('view'), may hold values from -6 to 6
- sources: int32 [32, 10], replicated, may hold values from 0 to 31, as said below
- warp_weights: bfloat16 [48, 512, 512], P('plane'), may hold values from -0.25 to 0.25
- view_gate: float32 [8], replicated, may hold values from -6 to 6
- depth_kernel: float32 [3, 8, 8], replicated, may hold values from -4 to 4
- cotangent: bfloat16 [32, 48, 8, 512], P('view', 'plane'), may hold values from -6 to 6
Outputs:
- regular: bfloat16 [32, 48, 8, 512], P('view', 'plane')
- feature_grads: float32 [32, 32, 512], P('view')
The draws below stay inside these ranges and needn't reach their ends.
Inputs may be any that keep to these rules, and one draw needn't show every extreme that they name: `sources`: view v is owned by the device at index v // 4 of view. Among the 40 entries of the rows of one device (rows i * 4 to i * 4 + 3), at most 10 name views of any one owner, and for each device some owner is named exactly 10 times.
All inputs are finite; a program needn't handle non-finite values.
Results may differ from the reference program's by a relative error of at most 0.0038.
Values may be sent and summed in bfloat16 or wider, within the bound.
No kernel may reach another device: no remote copies, remote signals or barrier semaphores. Data moves between devices by JAX's collectives and lax.ppermute only.
A program may use at most 128 MiB of HBM per device.

```python
import jax
import jax.numpy as jnp
from jax import lax

C = 32
G = 8
GC = 4
D = 48
S = 10
VIEWS_DEV = 4
PIX = 512
NV = 32
CAP = 10


def draw_sources(key, part):
    blocks = NV // VIEWS_DEV
    requests = VIEWS_DEV * S
    slot_total = blocks * CAP

    def one_block(block_key):
        first, second, third, fourth = jax.random.split(block_key, 4)
        busiest = jax.random.randint(first, (), 0, blocks)
        order = jax.random.permutation(second, slot_total)
        owners = order // CAP
        sort_key = jnp.where(owners == busiest, 0, slot_total) + jnp.arange(slot_total)
        chosen = owners[jnp.argsort(sort_key)][:requests]
        chosen = chosen[jax.random.permutation(third, requests)]
        local_pick = jax.random.randint(fourth, (requests,), 0, VIEWS_DEV)
        return (chosen * VIEWS_DEV + local_pick).reshape(VIEWS_DEV, S)
    block_keys = jax.random.split(jax.random.fold_in(key, 17), blocks)
    return jax.vmap(one_block)(block_keys).reshape(NV, S).astype(jnp.int32)


def level_of(stream_key, shape, cuts, least, top_value):
    def one(axis_at, blocks):
        steps = jax.random.uniform(jax.random.fold_in(jax.random.fold_in(stream_key, 6), axis_at), (blocks,), jnp.float32, least / len(cuts), top_value / len(cuts))
        return jnp.repeat(jnp.exp(steps), shape[axis_at] // blocks).reshape((-1,) + (1,) * (len(shape) - axis_at - 1))

    factor_of = one(*cuts[0])
    for cut in cuts[1:]:
        factor_of = factor_of * one(*cut)
    return factor_of


def centred(own_key, dims, deviation, bound, shards=(), kind=jnp.bfloat16):
    entries = jax.random.normal(own_key, dims, jnp.float32) * deviation
    if len(shards) > 0:
        entries = level_of(own_key, dims, shards, -0.22, 0.18) * entries
    return jnp.clip(entries, min=-bound, max=bound).astype(kind)


def setup_inputs(seed: int = 0) -> dict:
    splits = jax.random.split(jax.random.key(seed), 7)
    return {
        "features": centred(splits[0], (NV, C, PIX), 1.0, 6.0, ((0, 8),)),
        "sources": draw_sources(jax.random.fold_in(splits[6], 71), 0),
        "warp_weights": centred(splits[2], (D, PIX, PIX), PIX ** -0.5, 0.25, ((0, 4),)),
        "view_gate": centred(splits[3], (G,), 2.0, 6.0, (), jnp.float32),
        "depth_kernel": centred(splits[4], (3, G, G), 1.0, 4.0, (), jnp.float32),
        "cotangent": centred(splits[5], (NV, D, G, PIX), 1.0, 6.0, ((0, 8), (1, 4))),
    }


def aggregate(ref_map, warped, view_gate):
    src_count = warped.shape[0]
    plane_count = warped.shape[1]
    product = ref_map[None, None] * warped
    correlation = lax.optimization_barrier(jnp.sum(product.reshape(src_count, plane_count, G, GC, product.shape[-1]), axis=3)) / GC
    logits = lax.optimization_barrier(jnp.sum(correlation * view_gate[None, None, :, None], axis=2))
    visible = 0.5 + jax.nn.sigmoid(logits)
    weighted = lax.optimization_barrier(jnp.sum(visible[:, :, None, :] * correlation, axis=0))
    return weighted / lax.optimization_barrier(jnp.sum(visible, axis=0))[:, None, :]

def warp_planes(src_maps, warp_weights):
    return jnp.einsum('scy,dxy->sdcx', src_maps.astype(jnp.float32), warp_weights.astype(jnp.float32), precision=lax.Precision.HIGHEST)

def depth_conv(cost_volume, depth_kernel):
    planes = cost_volume.shape[1]
    padded = jnp.pad(cost_volume, ((0, 0), (1, 1), (0, 0), (0, 0)))
    result = jnp.zeros(cost_volume.shape, jnp.float32)
    for offset in range(3):
        result = result + jnp.einsum('og,rdgx->rdox', depth_kernel[offset], padded[:, offset:offset + planes], precision=lax.Precision.HIGHEST)
    return result

def reference(features, sources, warp_weights, view_gate, depth_kernel, cotangent):

    def forward_one(index):
        ref_map = features[index].astype(jnp.float32)
        src_maps = features[sources[index]]
        return aggregate(ref_map, warp_planes(src_maps, warp_weights), view_gate)
    cost_volume = lax.map(forward_one, jnp.arange(NV))
    pre_act, conv_vjp = jax.vjp(lambda volume: depth_conv(volume, depth_kernel), cost_volume)
    regular = jax.nn.silu(pre_act).astype(jnp.bfloat16)
    sigmoid_pre = jax.nn.sigmoid(pre_act)
    pre_grad = cotangent.astype(jnp.float32) * (sigmoid_pre * (1.0 + pre_act * (1.0 - sigmoid_pre)))
    cost_grad = conv_vjp(pre_grad)[0]

    def backward_one(index):
        ref_map = features[index].astype(jnp.float32)
        src_maps = features[sources[index]]
        warped = warp_planes(src_maps, warp_weights)
        unused, agg_vjp = jax.vjp(lambda first, second: aggregate(first, second, view_gate), ref_map, warped)
        ref_grad, warp_grad = agg_vjp(cost_grad[index])
        warp_round = lax.optimization_barrier(warp_grad.astype(jnp.bfloat16))
        src_grad = jnp.einsum('sdcx,dxy->scy', warp_round.astype(jnp.float32), warp_weights.astype(jnp.float32), precision=lax.Precision.HIGHEST)
        return (ref_grad, src_grad)
    ref_grad, src_grad = lax.map(backward_one, jnp.arange(NV))
    summed = jax.ops.segment_sum(src_grad.reshape(NV * S, C, PIX), sources.reshape(NV * S), num_segments=NV)
    return (regular, ref_grad + summed)
```

```python
import functools

import jax
import jax.numpy as jnp
from jax import lax
from jax.experimental import pallas as pl
from jax.experimental.pallas import tpu as pltpu
from jax.sharding import PartitionSpec as P

G = 8
GC = 4
SUB = 8
LANE = 128
VMEM_LIMIT = 48 * 1024 * 1024
NT = (((1,), (1,)), ((), ()))


def params(**extra):
    return pltpu.CompilerParams(vmem_limit_bytes=VMEM_LIMIT, **extra)


def low_half():
    return lax.broadcasted_iota(jnp.int32, (SUB, LANE), 0) < SUB // 2


def swap_halves(tile):
    return pltpu.roll(tile, SUB // 2, 0)


def spread(tile, half, low):
    other = swap_halves(tile)
    return jnp.where(low, tile, other) if half == 0 else jnp.where(low, other, tile)


def assemble_kernel(src_ref, all_ref, own_ref, rows_ref, refx_ref, scratch):
    local_views, per_view = src_ref.shape
    channels = own_ref.shape[1]
    pairs = local_views * per_view
    for pair in range(pairs):
        view = src_ref[pair % local_views, pair // local_views]
        for tile in range(scratch.shape[0]):
            scratch[tile, pl.ds(pair, channels, stride=pairs), :] = all_ref[
                view, :, pl.ds(tile * LANE, LANE)
            ].astype(jnp.float32)
    for tile in range(scratch.shape[0]):
        lanes = pl.ds(tile * LANE, LANE)
        rows_ref[:, lanes] = scratch[tile].astype(jnp.bfloat16)
        for view in range(local_views):
            own = own_ref[view, :, lanes].astype(jnp.float32)
            for copy in range(SUB // local_views):
                refx_ref[tile, pl.ds(copy * local_views + view, channels, stride=SUB), :] = own


def forward_kernel(
    gate_ref, rows_ref, refx_ref, w_ref, warped_ref, corr_ref, sig_ref, rden_ref, cost_ref, *chunks
):
    pairs = corr_ref.shape[2]
    groups = corr_ref.shape[1]
    tiles = pairs // SUB
    low = low_half()
    width = 2 * LANE
    for index, chunk in enumerate(chunks):
        chunk[...] = lax.dot_general(
            rows_ref[...],
            w_ref[0, index * width : (index + 1) * width, :],
            NT,
            preferred_element_type=jnp.float32,
        )
    for index, chunk in enumerate(chunks):
        warped_ref[0, :, index * width : (index + 1) * width] = chunk[...].astype(jnp.bfloat16)
        cost_pair = []
        for half in range(2):
            inner = pl.ds(half * LANE, LANE)
            lanes = pl.ds(index * width + half * LANE, LANE)
            logits = jnp.zeros((tiles, SUB, LANE), jnp.float32)
            for g in range(groups):
                total = None
                for j in range(GC):
                    c = g * GC + j
                    part = (
                        chunk[pl.ds(c * pairs, pairs), inner].reshape(tiles, SUB, LANE)
                        * refx_ref[2 * index + half, pl.ds(c * SUB, SUB), :][None]
                    )
                    total = part if total is None else total + part
                corr = total * (1.0 / GC)
                corr_ref[0, g, :, lanes] = corr.reshape(pairs, LANE)
                logits = logits + corr * gate_ref[g]
            sig = jax.nn.sigmoid(logits)
            sig_ref[0, :, lanes] = sig.reshape(pairs, LANE)
            visible = 0.5 + sig
            den = jnp.sum(visible, axis=0)
            rden = 1.0 / (den + swap_halves(den))
            rden_ref[0, :, lanes] = rden
            costs = []
            for g in range(groups):
                num = jnp.sum(
                    visible * corr_ref[0, g, :, lanes].reshape(tiles, SUB, LANE), axis=0
                )
                costs.append((num + swap_halves(num)) * rden)
            cost_pair.append(costs)
        for g in range(groups):
            cost_ref[0, pl.ds(g * SUB, SUB), pl.ds(index * LANE, LANE)] = jnp.where(
                low, cost_pair[0][g], cost_pair[1][g]
            )


def conv_kernel(taps_ref, cost_ref, cot_ref, regular_ref, grad_ref, slope):
    planes = regular_ref.shape[0]
    width = cost_ref.shape[2]

    def forward_plane(plane, carry):
        for lane in range(0, width, LANE):
            lanes = pl.ds(lane, LANE)
            inputs = [
                [cost_ref[plane + k, pl.ds(g * SUB, SUB), lanes] for g in range(G)]
                for k in range(3)
            ]
            pres = []
            for o in range(G):
                total = None
                for k in range(3):
                    for g in range(G):
                        part = inputs[k][g] * taps_ref[k, o, g]
                        total = part if total is None else total + part
                pres.append(total)
            pre = jnp.concatenate(pres, axis=0)
            sig = jax.nn.sigmoid(pre)
            cot = cot_ref[plane, :, lanes].astype(jnp.float32)
            slope[plane, :, lanes] = cot * (sig * (1.0 + pre * (1.0 - sig)))

            @pl.when((plane >= 1) & (plane <= planes))
            def _():
                regular_ref[plane - 1, :, lanes] = (pre * sig).astype(jnp.bfloat16)

        return carry

    lax.fori_loop(0, planes + 2, forward_plane, 0)

    def backward_plane(plane, carry):
        for lane in range(0, width, LANE):
            lanes = pl.ds(lane, LANE)
            inputs = [
                [slope[plane + 2 - k, pl.ds(o * SUB, SUB), lanes] for o in range(G)]
                for k in range(3)
            ]
            for g in range(G):
                total = None
                for k in range(3):
                    for o in range(G):
                        part = inputs[k][o] * taps_ref[k, o, g]
                        total = part if total is None else total + part
                grad_ref[plane, pl.ds(g * SUB, SUB), lanes] = total
        return carry

    lax.fori_loop(0, planes, backward_plane, 0)


def backward_kernel(
    gate_ref,
    src_ref,
    place_ref,
    refx_ref,
    w_ref,
    warped_ref,
    corr_ref,
    sig_ref,
    rden_ref,
    cost_ref,
    grad_ref,
    keep_ref,
    send_ref,
    rows,
    acc,
    dref,
    dense,
):
    step = pl.program_id(0)
    pairs = corr_ref.shape[2]
    groups = corr_ref.shape[1]
    tiles = pairs // SUB
    pixels = corr_ref.shape[3]
    local_views, per_view = src_ref.shape
    channels = groups * GC
    low = low_half()

    @pl.when(step == 0)
    def _():
        acc[...] = jnp.zeros_like(acc)
        dref[...] = jnp.zeros_like(dref)

    for tile in range(pixels // LANE):
        lanes = pl.ds(tile * LANE, LANE)
        packed = pl.ds((tile // 2) * LANE, LANE)
        half = tile % 2
        rden = rden_ref[0, :, lanes]
        mixed = None
        num_grads = []
        for g in range(groups):
            grad = grad_ref[0, pl.ds(g * SUB, SUB), packed]
            part = grad * cost_ref[0, pl.ds(g * SUB, SUB), packed]
            mixed = part if mixed is None else mixed + part
            num_grads.append(spread(grad, half, low) * rden)
        den_grad = spread(mixed, half, low) * rden
        vis_grad = -den_grad[None]
        for g in range(groups):
            vis_grad = vis_grad + num_grads[g][None] * corr_ref[0, g, :, lanes].reshape(
                tiles, SUB, LANE
            )
        sig = sig_ref[0, :, lanes].reshape(tiles, SUB, LANE)
        logit_grad = vis_grad * (sig * (1.0 - sig)) * (1.0 / GC)
        visible = (0.5 + sig) * (1.0 / GC)
        for g in range(groups):
            corr_grad = visible * num_grads[g][None] + logit_grad * gate_ref[g]
            for j in range(0, GC, 2):
                c = g * GC + j
                span = pl.ds(c * pairs, 2 * pairs)
                both = jnp.concatenate(
                    [
                        (corr_grad * refx_ref[tile, pl.ds((c + i) * SUB, SUB), :][None]).reshape(
                            pairs, LANE
                        )
                        for i in range(2)
                    ],
                    axis=0,
                )
                rows[span, lanes] = both.astype(jnp.bfloat16)
                warped = (
                    warped_ref[0, span, lanes].astype(jnp.float32).reshape(2, tiles, SUB, LANE)
                )
                for i in range(2):
                    dref[tile, pl.ds((c + i) * SUB, SUB), :] += jnp.sum(
                        corr_grad * warped[i], axis=0
                    )
    for index in range(pixels // (2 * LANE)):
        product = jnp.dot(
            rows[...],
            w_ref[0, :, pl.ds(index * 2 * LANE, 2 * LANE)],
            preferred_element_type=jnp.float32,
        )
        for half in range(2):
            acc[2 * index + half] += product[:, half * LANE : (half + 1) * LANE]

    @pl.when(step == pl.num_programs(0) - 1)
    def _():
        own_index = place_ref[0]
        parity = place_ref[1]
        dense[...] = jnp.zeros_like(dense)
        for tile in range(pixels // LANE):
            lanes = pl.ds(tile * LANE, LANE)
            for view in range(local_views):
                total = dref[tile, pl.ds(view, channels, stride=SUB), :]
                for copy in range(1, SUB // local_views):
                    first = copy * local_views + view
                    total = total + dref[tile, pl.ds(first, channels, stride=SUB), :]
                dense[own_index * local_views + view, :, lanes] = total
        for pair in range(pairs):
            view = src_ref[pair % local_views, pair // local_views]
            for tile in range(pixels // LANE):
                dense[view, :, pl.ds(tile * LANE, LANE)] += acc[
                    tile, pl.ds(pair, channels, stride=pairs), :
                ]
        blocks = keep_ref.shape[1]
        share = keep_ref.shape[2]

        def one_view(view, carry):
            kept = []
            sent = []
            for block in range(blocks):
                mine = pl.multiple_of((2 * block + parity) * share, share)
                theirs = pl.multiple_of((2 * block + 1 - parity) * share, share)
                keep_ref[view, block] = dense[view, pl.ds(mine, share), :]
                sent.append(dense[view, pl.ds(theirs, share), :])
            send_ref[view] = jnp.concatenate(sent, axis=0).astype(jnp.bfloat16)
            return carry

        lax.fori_loop(0, dense.shape[0], one_view, 0)


def whole(array):
    rank = len(array.shape)
    return pl.BlockSpec(array.shape, lambda d: (0,) * rank)


def per_plane(shape):
    rank = len(shape)
    return pl.BlockSpec((1,) + tuple(shape[1:]), lambda d: (d,) + (0,) * (rank - 1))


SMEM = functools.partial(pl.BlockSpec, memory_space=pltpu.SMEM)


def shards(features, sources, warp_weights, view_gate, depth_kernel, cotangent):
    view_count = lax.axis_size("view")
    plane_count = lax.axis_size("plane")
    own_index = lax.axis_index("view")
    plane_index = lax.axis_index("plane")
    local_views, channels, pixels = features.shape
    all_views, per_view = sources.shape
    pairs = local_views * per_view
    planes = warp_weights.shape[0]
    share = channels // plane_count
    blocks = plane_count // 2
    parity = plane_index % 2
    packed_rows = G * SUB
    packed_width = pixels // 2
    f32 = jnp.float32
    bf16 = jnp.bfloat16
    swap = [(i, i ^ 1) for i in range(plane_count)]
    up = [(i, i + 1) for i in range(plane_count - 1)]
    down = [(i + 1, i) for i in range(plane_count - 1)]

    halves = features.reshape(local_views, blocks, 2, share, pixels)
    mine = lax.dynamic_index_in_dim(halves, parity, 2, keepdims=False).reshape(
        local_views, channels // 2, pixels
    )
    gathered = lax.all_gather(mine, "view", axis=0, tiled=True)
    other = lax.ppermute(gathered, "plane", swap)
    shape5 = (all_views, blocks, 1, share, pixels)
    first = jnp.where(parity == 0, gathered, other).reshape(shape5)
    second = jnp.where(parity == 0, other, gathered).reshape(shape5)
    all_maps = jnp.concatenate([first, second], axis=2).reshape(all_views, channels, pixels)

    cot = cotangent.reshape(local_views, planes, G, pixels // (2 * LANE), 2, LANE)
    cot = cot.transpose(1, 2, 4, 0, 3, 5).reshape(planes, packed_rows, packed_width)
    cot_ext = jnp.concatenate(
        [
            lax.ppermute(cot[planes - 1 :], "plane", up),
            cot,
            lax.ppermute(cot[:1], "plane", down),
        ],
        axis=0,
    )

    src_own = lax.dynamic_slice_in_dim(sources, own_index * local_views, local_views, 0)
    rows, refx = pl.pallas_call(
        assemble_kernel,
        out_shape=(
            jax.ShapeDtypeStruct((channels * pairs, pixels), bf16),
            jax.ShapeDtypeStruct((pixels // LANE, channels * SUB, LANE), f32),
        ),
        in_specs=[SMEM(), pl.BlockSpec(), pl.BlockSpec()],
        scratch_shapes=[pltpu.VMEM((pixels // LANE, channels * pairs, LANE), f32)],
        compiler_params=params(),
        name="assemble",
    )(src_own, all_maps, features)

    warped_s = jax.ShapeDtypeStruct((planes, channels * pairs, pixels), bf16)
    corr_s = jax.ShapeDtypeStruct((planes, G, pairs, pixels), f32)
    sig_s = jax.ShapeDtypeStruct((planes, pairs, pixels), f32)
    rden_s = jax.ShapeDtypeStruct((planes, SUB, pixels), f32)
    cost_s = jax.ShapeDtypeStruct((planes, packed_rows, packed_width), f32)
    saved = (warped_s, corr_s, sig_s, rden_s, cost_s)
    warped, corr, sig, rden, cost = pl.pallas_call(
        forward_kernel,
        out_shape=saved,
        grid=(planes,),
        in_specs=[SMEM(), whole(rows), whole(refx), per_plane(warp_weights.shape)],
        out_specs=tuple(per_plane(s.shape) for s in saved),
        scratch_shapes=[
            pltpu.VMEM((channels * pairs, 2 * LANE), f32) for _ in range(pixels // (2 * LANE))
        ],
        compiler_params=params(),
        name="forward",
    )(view_gate, rows, refx, warp_weights)

    cost_ext = jnp.concatenate(
        [
            lax.ppermute(cost[planes - 2 :], "plane", up),
            cost,
            lax.ppermute(cost[:2], "plane", down),
        ],
        axis=0,
    )
    regular, cost_grad = pl.pallas_call(
        conv_kernel,
        out_shape=(
            jax.ShapeDtypeStruct((planes, packed_rows, packed_width), bf16),
            jax.ShapeDtypeStruct((planes, packed_rows, packed_width), f32),
        ),
        in_specs=[SMEM(), pl.BlockSpec(), pl.BlockSpec()],
        scratch_shapes=[pltpu.VMEM((planes + 2, packed_rows, packed_width), f32)],
        compiler_params=params(),
        name="depth_conv",
    )(depth_kernel, cost_ext, cot_ext)
    regular = (
        regular.reshape(planes, G, 2, local_views, pixels // (2 * LANE), LANE)
        .transpose(3, 0, 1, 4, 2, 5)
        .reshape(local_views, planes, G, pixels)
    )

    place = jnp.stack([own_index, parity]).astype(jnp.int32)
    keep, send = pl.pallas_call(
        backward_kernel,
        out_shape=(
            jax.ShapeDtypeStruct((all_views, blocks, share, pixels), f32),
            jax.ShapeDtypeStruct((all_views, blocks * share, pixels), bf16),
        ),
        grid=(planes,),
        in_specs=[SMEM(), SMEM(), SMEM(), whole(refx), per_plane(warp_weights.shape)]
        + [per_plane(s.shape) for s in saved]
        + [per_plane(cost_grad.shape)],
        out_specs=(
            pl.BlockSpec((all_views, blocks, share, pixels), lambda d: (0, 0, 0, 0)),
            pl.BlockSpec((all_views, blocks * share, pixels), lambda d: (0, 0, 0)),
        ),
        scratch_shapes=[
            pltpu.VMEM((channels * pairs, pixels), bf16),
            pltpu.VMEM((pixels // LANE, channels * pairs, LANE), f32),
            pltpu.VMEM((pixels // LANE, channels * SUB, LANE), f32),
            pltpu.VMEM((all_views, channels, pixels), f32),
        ],
        compiler_params=params(),
        name="backward",
    )(view_gate, src_own, place, refx, warp_weights, warped, corr, sig, rden, cost, cost_grad)

    received = lax.ppermute(send, "plane", swap)
    paired = keep + received.reshape(keep.shape).astype(f32)
    outbound = (
        paired.reshape(view_count, local_views, blocks, share, pixels)
        .transpose(0, 2, 1, 3, 4)
        .reshape(view_count * blocks, local_views, share, pixels)
        .astype(bf16)
    )
    fellows = [
        [v * plane_count + 2 * b + side for v in range(view_count) for b in range(blocks)]
        for side in range(2)
    ]
    inbound = lax.all_to_all(
        outbound, ("view", "plane"), 0, 0, axis_index_groups=fellows, tiled=True
    )
    own_share = jnp.sum(inbound.astype(f32), axis=0)
    return (regular, lax.all_gather(own_share, "plane", axis=1, tiled=True))


def solution(mesh):
    in_specs = (
        P("view", None, None),
        P(),
        P("plane", None, None),
        P(),
        P(),
        P("view", "plane", None, None),
    )
    out_specs = (P("view", "plane", None, None), P("view", None, None))
    return jax.shard_map(shards, mesh=mesh, in_specs=in_specs, out_specs=out_specs, check_vma=False)
```

```python
import functools

import jax
import jax.numpy as jnp
from jax import lax
from jax.experimental import pallas as pl
from jax.experimental.pallas import tpu as pltpu
from jax.sharding import PartitionSpec as P

G = 8
GC = 4
SUB = 8
LANE = 128
VMEM_LIMIT = 48 * 1024 * 1024
NT = (((1,), (1,)), ((), ()))


def params(**extra):
    return pltpu.CompilerParams(vmem_limit_bytes=VMEM_LIMIT, **extra)


def low_half():
    return lax.broadcasted_iota(jnp.int32, (SUB, LANE), 0) < SUB // 2


def swap_halves(tile):
    return pltpu.roll(tile, SUB // 2, 0)


def spread(tile, half, low):
    other = swap_halves(tile)
    return jnp.where(low, tile, other) if half == 0 else jnp.where(low, other, tile)


def assemble_kernel(src_ref, place_ref, mine_ref, other_ref, own_ref, rows_ref, refx_ref, scratch):
    local_views, per_view = src_ref.shape
    channels = own_ref.shape[1]
    tiles, _, _ = scratch.shape
    pairs = local_views * per_view
    share = SUB
    blocks = mine_ref.shape[1] // share
    own_index = place_ref[0]
    parity = place_ref[1]
    for pair in range(pairs):
        view = src_ref[pair % local_views, pair // local_views]
        slot = ((view // local_views) ^ own_index) * local_views + view % local_views
        for tile in range(tiles):
            lanes = pl.ds(tile * LANE, LANE)
            for side, ref in ((parity, mine_ref), (1 - parity, other_ref)):
                maps = ref[slot, :, lanes].astype(jnp.float32)
                for block in range(blocks):
                    first = (2 * block + side) * (share * pairs) + pair
                    scratch[tile, pl.ds(first, share, stride=pairs), :] = maps[
                        block * share : (block + 1) * share
                    ]
    for tile in range(tiles):
        lanes = pl.ds(tile * LANE, LANE)
        rows_ref[:, lanes] = scratch[tile].astype(jnp.bfloat16)
        for view in range(local_views):
            own = own_ref[view, :, lanes].astype(jnp.float32)
            for copy in range(SUB // local_views):
                refx_ref[tile, pl.ds(copy * local_views + view, channels, stride=SUB), :] = own


def forward_body(
    gate_ref, rows_ref, refx_ref, w_ref, warped_ref, corr_ref, sig_ref, rden_ref, cost_ref, chunks
):
    pairs = corr_ref.shape[2]
    groups = corr_ref.shape[1]
    tiles = pairs // SUB
    low = low_half()
    width = 2 * LANE
    for index, chunk in enumerate(chunks):
        chunk[...] = lax.dot_general(
            rows_ref[...],
            w_ref[0, index * width : (index + 1) * width, :],
            NT,
            preferred_element_type=jnp.float32,
        )
    for index, chunk in enumerate(chunks):
        warped_ref[0, :, index * width : (index + 1) * width] = chunk[...].astype(jnp.bfloat16)
        cost_pair = []
        for half in range(2):
            inner = pl.ds(half * LANE, LANE)
            lanes = pl.ds(index * width + half * LANE, LANE)
            logits = jnp.zeros((tiles, SUB, LANE), jnp.float32)
            for g in range(groups):
                total = None
                for j in range(GC):
                    c = g * GC + j
                    part = (
                        chunk[pl.ds(c * pairs, pairs), inner].reshape(tiles, SUB, LANE)
                        * refx_ref[2 * index + half, pl.ds(c * SUB, SUB), :][None]
                    )
                    total = part if total is None else total + part
                corr = total * (1.0 / GC)
                corr_ref[0, g, :, lanes] = corr.reshape(pairs, LANE)
                logits = logits + corr * gate_ref[g]
            sig = jax.nn.sigmoid(logits)
            sig_ref[0, :, lanes] = sig.reshape(pairs, LANE)
            visible = 0.5 + sig
            den = jnp.sum(visible, axis=0)
            rden = 1.0 / (den + swap_halves(den))
            rden_ref[0, :, lanes] = rden
            costs = []
            for g in range(groups):
                num = jnp.sum(
                    visible * corr_ref[0, g, :, lanes].reshape(tiles, SUB, LANE), axis=0
                )
                costs.append((num + swap_halves(num)) * rden)
            cost_pair.append(costs)
        for g in range(groups):
            cost_ref[0, index, pl.ds(g * SUB, SUB), :] = jnp.where(
                low, cost_pair[0][g], cost_pair[1][g]
            )


def pack_planes(array_ref, plane, out_ref, slot):
    local_views, _, groups, pixels = array_ref.shape
    for view in range(local_views):
        for tile in range(pixels // LANE):
            first = (tile % 2) * local_views + view
            out_ref[slot, tile // 2, pl.ds(first, groups, stride=SUB), :] = array_ref[
                view, plane, :, pl.ds(tile * LANE, LANE)
            ].astype(jnp.float32)


def edge_kernel(
    gate_ref,
    rows_ref,
    refx_ref,
    w_ref,
    cot_ref,
    warped_ref,
    corr_ref,
    sig_ref,
    rden_ref,
    up_ref,
    down_ref,
    *scratch,
):
    cost, *chunks = scratch
    step = pl.program_id(0)
    last = cot_ref.shape[1] - 1
    forward_body(
        gate_ref, rows_ref, refx_ref, w_ref, warped_ref, corr_ref, sig_ref, rden_ref, cost, chunks
    )

    @pl.when(step < 2)
    def _():
        down_ref[step] = cost[0]

    @pl.when(step >= 2)
    def _():
        up_ref[step - 2] = cost[0]

    @pl.when(step == 0)
    def _():
        pack_planes(cot_ref, 0, down_ref, 2)
        pack_planes(cot_ref, last, up_ref, 2)


def inner_kernel(
    gate_ref,
    rows_ref,
    refx_ref,
    w_ref,
    warped_in,
    corr_in,
    sig_in,
    rden_in,
    warped_ref,
    corr_ref,
    sig_ref,
    rden_ref,
    cost_ref,
    *chunks,
):
    forward_body(
        gate_ref,
        rows_ref,
        refx_ref,
        w_ref,
        warped_ref,
        corr_ref,
        sig_ref,
        rden_ref,
        cost_ref,
        chunks,
    )


def conv_kernel(
    taps_ref,
    below_ref,
    down_ref,
    inner_ref,
    up_ref,
    above_ref,
    cot_ref,
    regular_ref,
    cost_ref,
    grad_ref,
    cost,
    cot,
    slope,
    smooth,
):
    planes = grad_ref.shape[0]
    local_views, _, groups, pixels = cot_ref.shape
    cost[0:2] = below_ref[0:2]
    cost[2:4] = down_ref[0:2]
    cost[4:planes] = inner_ref[...]
    cost[planes : planes + 2] = up_ref[0:2]
    cost[planes + 2 : planes + 4] = above_ref[0:2]
    cost_ref[...] = cost[2 : planes + 2]
    cot[0] = below_ref[2]
    cot[planes + 1] = above_ref[2]

    def pack_one(plane, carry):
        pack_planes(cot_ref, plane, cot, plane + 1)
        return carry

    lax.fori_loop(0, planes, pack_one, 0)

    def mix(source, tap):
        results = []
        for a in range(G):
            total = None
            for k in range(3):
                for b in range(G):
                    part = source(k, b) * tap(k, a, b)
                    total = part if total is None else total + part
            results.append(total)
        return jnp.concatenate(results, axis=1)

    def forward_plane(plane, carry):
        pre = mix(
            lambda k, g: cost[plane + k, :, pl.ds(g * SUB, SUB), :],
            lambda k, o, g: taps_ref[k, o, g],
        )
        sig = jax.nn.sigmoid(pre)
        slope[plane] = cot[plane] * (sig * (1.0 + pre * (1.0 - sig)))
        smooth[plane] = pre * sig
        return carry

    lax.fori_loop(0, planes + 2, forward_plane, 0)

    def backward_plane(plane, carry):
        grad_ref[plane] = mix(
            lambda k, o: slope[plane + 2 - k, :, pl.ds(o * SUB, SUB), :],
            lambda k, g, o: taps_ref[k, o, g],
        )
        for view in range(local_views):
            for tile in range(pixels // LANE):
                first = (tile % 2) * local_views + view
                regular_ref[view, plane, :, pl.ds(tile * LANE, LANE)] = smooth[
                    plane + 1, tile // 2, pl.ds(first, groups, stride=SUB), :
                ].astype(jnp.bfloat16)
        return carry

    lax.fori_loop(0, planes, backward_plane, 0)


def backward_kernel(
    gate_ref,
    src_ref,
    place_ref,
    refx_ref,
    w_ref,
    warped_ref,
    corr_ref,
    sig_ref,
    rden_ref,
    cost_ref,
    grad_ref,
    keep_ref,
    send_ref,
    rows,
    acc,
    dref,
    dense,
):
    step = pl.program_id(0)
    pairs = corr_ref.shape[2]
    groups = corr_ref.shape[1]
    tiles = pairs // SUB
    pixels = corr_ref.shape[3]
    local_views, per_view = src_ref.shape
    channels = groups * GC
    low = low_half()

    @pl.when(step == 0)
    def _():
        acc[...] = jnp.zeros_like(acc)
        dref[...] = jnp.zeros_like(dref)

    for tile in range(pixels // LANE):
        lanes = pl.ds(tile * LANE, LANE)
        pack = tile // 2
        half = tile % 2
        rden = rden_ref[0, :, lanes]
        mixed = None
        num_grads = []
        for g in range(groups):
            grad = grad_ref[0, pack, pl.ds(g * SUB, SUB), :]
            part = grad * cost_ref[0, pack, pl.ds(g * SUB, SUB), :]
            mixed = part if mixed is None else mixed + part
            num_grads.append(spread(grad, half, low) * rden)
        den_grad = spread(mixed, half, low) * rden
        vis_grad = -den_grad[None]
        for g in range(groups):
            vis_grad = vis_grad + num_grads[g][None] * corr_ref[0, g, :, lanes].reshape(
                tiles, SUB, LANE
            )
        sig = sig_ref[0, :, lanes].reshape(tiles, SUB, LANE)
        logit_grad = vis_grad * (sig * (1.0 - sig)) * (1.0 / GC)
        visible = (0.5 + sig) * (1.0 / GC)
        for g in range(groups):
            corr_grad = visible * num_grads[g][None] + logit_grad * gate_ref[g]
            for j in range(0, GC, 2):
                c = g * GC + j
                span = pl.ds(c * pairs, 2 * pairs)
                both = jnp.concatenate(
                    [
                        (corr_grad * refx_ref[tile, pl.ds((c + i) * SUB, SUB), :][None]).reshape(
                            pairs, LANE
                        )
                        for i in range(2)
                    ],
                    axis=0,
                )
                rows[span, lanes] = both.astype(jnp.bfloat16)
                warped = (
                    warped_ref[0, span, lanes].astype(jnp.float32).reshape(2, tiles, SUB, LANE)
                )
                for i in range(2):
                    dref[tile, pl.ds((c + i) * SUB, SUB), :] += jnp.sum(
                        corr_grad * warped[i], axis=0
                    )
    for index in range(pixels // (2 * LANE)):
        product = jnp.dot(
            rows[...],
            w_ref[0, :, pl.ds(index * 2 * LANE, 2 * LANE)],
            preferred_element_type=jnp.float32,
        )
        for half in range(2):
            acc[2 * index + half] += product[:, half * LANE : (half + 1) * LANE]

    @pl.when(step == pl.num_programs(0) - 1)
    def _():
        own_index = place_ref[0]
        parity = place_ref[1]
        dense[...] = jnp.zeros_like(dense)
        for tile in range(pixels // LANE):
            lanes = pl.ds(tile * LANE, LANE)
            for view in range(local_views):
                total = dref[tile, pl.ds(view, channels, stride=SUB), :]
                for copy in range(1, SUB // local_views):
                    first = copy * local_views + view
                    total = total + dref[tile, pl.ds(first, channels, stride=SUB), :]
                dense[view, :, lanes] = total
        for pair in range(pairs):
            view = src_ref[pair % local_views, pair // local_views]
            slot = ((view // local_views) ^ own_index) * local_views + view % local_views
            for tile in range(pixels // LANE):
                dense[slot, :, pl.ds(tile * LANE, LANE)] += acc[
                    tile, pl.ds(pair, channels, stride=pairs), :
                ]
        share = SUB
        blocks = keep_ref.shape[1] // share

        def one_view(view, carry):
            kept = []
            sent = []
            for block in range(blocks):
                mine = pl.multiple_of((2 * block + parity) * share, share)
                theirs = pl.multiple_of((2 * block + 1 - parity) * share, share)
                kept.append(dense[view, pl.ds(mine, share), :])
                sent.append(dense[view, pl.ds(theirs, share), :])
            keep_ref[view] = jnp.concatenate(kept, axis=0)
            send_ref[view] = jnp.concatenate(sent, axis=0).astype(jnp.bfloat16)
            return carry

        lax.fori_loop(0, dense.shape[0], one_view, 0)


def combine_kernel(keep_ref, received_ref, own_ref, *out_refs):
    local_views = own_ref.shape[0]
    own_ref[...] = keep_ref[0:local_views] + received_ref[0:local_views].astype(jnp.float32)
    for index, out_ref in enumerate(out_refs):
        span = pl.ds((index + 1) * local_views, local_views)
        out_ref[...] = (keep_ref[span] + received_ref[span].astype(jnp.float32)).astype(
            jnp.bfloat16
        )


def per_plane(shape, plane):
    rank = len(shape)
    return pl.BlockSpec((1,) + tuple(shape[1:]), lambda d: (plane(d),) + (0,) * (rank - 1))


def fixed(shape):
    rank = len(shape)
    return pl.BlockSpec(tuple(shape), lambda d: (0,) * rank)


SMEM = functools.partial(pl.BlockSpec, memory_space=pltpu.SMEM)


def shards(features, sources, warp_weights, view_gate, depth_kernel, cotangent):
    view_count = lax.axis_size("view")
    plane_count = lax.axis_size("plane")
    own_index = lax.axis_index("view")
    plane_index = lax.axis_index("plane")
    local_views, channels, pixels = features.shape
    all_views, per_view = sources.shape
    pairs = local_views * per_view
    planes = warp_weights.shape[0]
    share = channels // plane_count
    blocks = plane_count // 2
    parity = plane_index % 2
    f32 = jnp.float32
    bf16 = jnp.bfloat16
    near = [(i, i ^ 1) for i in range(plane_count)]
    far = [(i, i ^ 2) for i in range(plane_count)]
    up = [(i, i + 1) for i in range(plane_count - 1)]
    down = [(i + 1, i) for i in range(plane_count - 1)]
    shape = jax.ShapeDtypeStruct

    halves = features.reshape(local_views, blocks, 2, share, pixels)
    mine = lax.dynamic_index_in_dim(halves, parity, 2, keepdims=False).reshape(
        local_views, channels // 2, pixels
    )

    def over_view(array, k):
        return lax.ppermute(array, "view", [(i, i ^ k) for i in range(view_count)])

    mine_all = jnp.concatenate(
        [mine] + [over_view(mine, k) for k in range(1, view_count)], axis=0
    )
    other_all = lax.ppermute(mine_all, "plane", near)

    src_own = lax.dynamic_slice_in_dim(sources, own_index * local_views, local_views, 0)
    place = jnp.stack([own_index, parity]).astype(jnp.int32)
    rows, refx = pl.pallas_call(
        assemble_kernel,
        out_shape=(
            shape((channels * pairs, pixels), bf16),
            shape((pixels // LANE, channels * SUB, LANE), f32),
        ),
        in_specs=[SMEM(), SMEM(), pl.BlockSpec(), pl.BlockSpec(), pl.BlockSpec()],
        scratch_shapes=[pltpu.VMEM((pixels // LANE, channels * pairs, LANE), f32)],
        compiler_params=params(),
        name="assemble",
    )(src_own, place, mine_all, other_all, features)

    packed = (pixels // (2 * LANE), G * SUB, LANE)
    saved = (
        shape((planes, channels * pairs, pixels), bf16),
        shape((planes, G, pairs, pixels), f32),
        shape((planes, pairs, pixels), f32),
        shape((planes, SUB, pixels), f32),
    )
    chunks = [
        pltpu.VMEM((channels * pairs, 2 * LANE), f32) for _ in range(pixels // (2 * LANE))
    ]

    def edge(d):
        return jnp.where(d < 2, d, planes - 4 + d)

    def inner(d):
        return d + 2

    fixed_specs = [SMEM(), fixed(rows.shape), fixed(refx.shape)]
    *edge_saved, up_load, down_load = pl.pallas_call(
        edge_kernel,
        out_shape=saved + (shape((3,) + packed, f32),) * 2,
        grid=(4,),
        in_specs=fixed_specs + [per_plane(warp_weights.shape, edge), fixed(cotangent.shape)],
        out_specs=tuple(per_plane(s.shape, edge) for s in saved) + (fixed((3,) + packed),) * 2,
        scratch_shapes=[pltpu.VMEM((1,) + packed, f32)] + chunks,
        compiler_params=params(),
        name="forward_edge",
    )(view_gate, rows, refx, warp_weights, cotangent)
    below = lax.ppermute(up_load, "plane", up)
    above = lax.ppermute(down_load, "plane", down)
    *saved_values, inner_cost = pl.pallas_call(
        inner_kernel,
        out_shape=saved + (shape((planes - 4,) + packed, f32),),
        grid=(planes - 4,),
        in_specs=fixed_specs
        + [per_plane(warp_weights.shape, inner)]
        + [pl.BlockSpec(memory_space=pl.ANY)] * 4,
        out_specs=tuple(per_plane(s.shape, inner) for s in saved)
        + (per_plane((planes - 4,) + packed, lambda d: d),),
        scratch_shapes=chunks,
        input_output_aliases={4: 0, 5: 1, 6: 2, 7: 3},
        compiler_params=params(),
        cost_estimate=pl.CostEstimate(
            flops=2 * channels * pairs * pixels * pixels * (planes - 4),
            bytes_accessed=40 * 1024 * 1024,
            transcendentals=0,
        ),
        name="forward_inner",
    )(view_gate, rows, refx, warp_weights, *edge_saved)

    regular, cost, cost_grad = pl.pallas_call(
        conv_kernel,
        out_shape=(
            shape(cotangent.shape, bf16),
            shape((planes,) + packed, f32),
            shape((planes,) + packed, f32),
        ),
        in_specs=[SMEM()] + [pl.BlockSpec()] * 6,
        scratch_shapes=[
            pltpu.VMEM((planes + 4,) + packed, f32),
            pltpu.VMEM((planes + 2,) + packed, f32),
            pltpu.VMEM((planes + 2,) + packed, f32),
            pltpu.VMEM((planes + 2,) + packed, f32),
        ],
        compiler_params=params(),
        name="depth_conv",
    )(depth_kernel, below, down_load, inner_cost, up_load, above, cotangent)

    def same(d):
        return d

    returned = (all_views, channels // 2, pixels)
    keep, send = pl.pallas_call(
        backward_kernel,
        out_shape=(shape(returned, f32), shape(returned, bf16)),
        grid=(planes,),
        in_specs=[SMEM(), SMEM(), SMEM(), fixed(refx.shape), per_plane(warp_weights.shape, same)]
        + [per_plane(s.shape, same) for s in saved]
        + [per_plane(cost.shape, same), per_plane(cost_grad.shape, same)],
        out_specs=(fixed(returned), fixed(returned)),
        scratch_shapes=[
            pltpu.VMEM((channels * pairs, pixels), bf16),
            pltpu.VMEM((pixels // LANE, channels * pairs, LANE), f32),
            pltpu.VMEM((pixels // LANE, channels * SUB, LANE), f32),
            pltpu.VMEM((all_views, channels, pixels), f32),
        ],
        compiler_params=params(),
        name="backward",
    )(view_gate, src_own, place, refx, warp_weights, *saved_values, cost, cost_grad)

    received = lax.ppermute(send, "plane", near)
    piece = (local_views, channels // 2, pixels)
    total, *pieces = pl.pallas_call(
        combine_kernel,
        out_shape=(shape(piece, f32),) + (shape(piece, bf16),) * (view_count - 1),
        compiler_params=params(),
        name="combine",
    )(keep, received)
    for k, part in enumerate(pieces):
        total = total + over_view(part, k + 1).astype(f32)
    total = total + lax.ppermute(total, "plane", far)
    other = lax.ppermute(total, "plane", near)
    cut = (local_views, blocks, 1, share, pixels)
    first = jnp.where(parity == 0, total, other).reshape(cut)
    second = jnp.where(parity == 0, other, total).reshape(cut)
    feature_grads = jnp.concatenate([first, second], axis=2).reshape(features.shape)
    return (regular, feature_grads)


def solution(mesh):
    in_specs = (
        P("view", None, None),
        P(),
        P("plane", None, None),
        P(),
        P(),
        P("view", "plane", None, None),
    )
    out_specs = (P("view", "plane", None, None), P("view", None, None))
    return jax.shard_map(shards, mesh=mesh, in_specs=in_specs, out_specs=out_specs, check_vma=False)
```

```python
import functools

import jax
import jax.numpy as jnp
from jax import lax
from jax.experimental import pallas as pl
from jax.experimental.pallas import tpu as pltpu
from jax.sharding import PartitionSpec as P

G = 8
GC = 4
SUB = 8
LANE = 128
VMEM_LIMIT = 48 * 1024 * 1024
NT = (((1,), (1,)), ((), ()))


def params():
    return pltpu.CompilerParams(vmem_limit_bytes=VMEM_LIMIT)


def low_half():
    return lax.broadcasted_iota(jnp.int32, (SUB, LANE), 0) < SUB // 2


def swap_halves(tile):
    return pltpu.roll(tile, SUB // 2, 0)


def spread(tile, half, low):
    other = swap_halves(tile)
    return jnp.where(low, tile, other) if half == 0 else jnp.where(low, other, tile)


def pack_planes(array_ref, plane, out_ref, slot):
    local_views, _, groups, pixels = array_ref.shape
    for view in range(local_views):
        for tile in range(pixels // LANE):
            first = (tile % 2) * local_views + view
            out_ref[slot, tile // 2, pl.ds(first, groups, stride=SUB), :] = array_ref[
                view, plane, :, pl.ds(tile * LANE, LANE)
            ].astype(jnp.float32)


def prep_kernel(gate_ref, own_ref, cot_ref, refx_ref, gates_ref, cot_out):
    local_views, channels, pixels = own_ref.shape
    for tile in range(pixels // LANE):
        for view in range(local_views):
            own = own_ref[view, :, pl.ds(tile * LANE, LANE)].astype(jnp.float32)
            for copy in range(SUB // local_views):
                refx_ref[tile, pl.ds(copy * local_views + view, channels, stride=SUB), :] = own
    for g in range(gates_ref.shape[0]):
        gates_ref[g] = jnp.full((SUB, LANE), gate_ref[g], jnp.float32)

    def pack_one(plane, carry):
        pack_planes(cot_ref, plane, cot_out, plane)
        return carry

    lax.fori_loop(0, cot_out.shape[0], pack_one, 0)


def position(view, own_index, local_views, view_count):
    distance = (view // local_views) ^ own_index
    place = distance // 2 + (distance % 2) * (view_count // 2)
    return place * local_views + view % local_views


def assemble_kernel(src_ref, place_ref, even_ref, odd_ref, even_far, odd_far, rows_ref, scratch):
    local_views, per_view = src_ref.shape
    tiles = scratch.shape[0]
    pairs = local_views * per_view
    half_views = even_ref.shape[0]
    blocks = even_ref.shape[1] // SUB
    own_index = place_ref[0]
    parity = place_ref[1]
    for pair in range(pairs):
        view = src_ref[pair % local_views, pair // local_views]
        slot = position(view, own_index, local_views, 2 * half_views // local_views)
        odd = slot >= half_views
        index = jnp.where(odd, slot - half_views, slot)
        for tile in range(tiles):
            lanes = pl.ds(tile * LANE, LANE)
            for side, even, other in ((parity, even_ref, odd_ref), (1 - parity, even_far, odd_far)):
                maps = jnp.where(odd, other[index, :, lanes], even[index, :, lanes]).astype(
                    jnp.float32
                )
                for block in range(blocks):
                    first = (2 * block + side) * (SUB * pairs) + pair
                    scratch[tile, pl.ds(first, SUB, stride=pairs), :] = maps[
                        block * SUB : (block + 1) * SUB
                    ]
    for tile in range(tiles):
        rows_ref[:, pl.ds(tile * LANE, LANE)] = scratch[tile].astype(jnp.bfloat16)


def forward_vector(gates_ref, refx_ref, chunk, first_tile, half, outs):
    warped_ref, corr_ref, sig_ref, rden_ref = outs
    groups, pairs = corr_ref.shape[1:3]
    tiles = pairs // SUB
    lanes = pl.ds(half * LANE, LANE)
    logits = None
    for g in range(groups):
        total = None
        for j in range(0, GC, 2):
            c = g * GC + j
            span = pl.ds(c * pairs, 2 * pairs)
            both = chunk[span, lanes]
            warped_ref[0, span, lanes] = both.astype(jnp.bfloat16)
            both = both.reshape(2, tiles, SUB, LANE)
            for i in range(2):
                part = both[i] * refx_ref[first_tile + half, pl.ds((c + i) * SUB, SUB), :][None]
                total = part if total is None else total + part
        corr = total * (1.0 / GC)
        corr_ref[0, g, :, lanes] = corr.reshape(pairs, LANE)
        part = corr * gates_ref[g][None]
        logits = part if logits is None else logits + part
    sig = jax.nn.sigmoid(logits)
    sig_ref[0, :, lanes] = sig.reshape(pairs, LANE)
    visible = 0.5 + sig
    den = jnp.sum(visible, axis=0)
    rden = 1.0 / (den + swap_halves(den))
    rden_ref[0, :, lanes] = rden
    costs = []
    for g in range(groups):
        num = jnp.sum(visible * corr_ref[0, g, :, lanes].reshape(tiles, SUB, LANE), axis=0)
        costs.append((num + swap_halves(num)) * rden)
    return costs


def forward_dot(rows_ref, w_ref, chunk, part, parts):
    count = rows_ref.shape[0] // parts
    span = pl.ds(part * count, count)
    chunk[span, :] = lax.dot_general(
        rows_ref[span, :], w_ref[0], NT, preferred_element_type=jnp.float32
    )


def forward_body(gates_ref, rows_ref, refx_ref, w0_ref, w1_ref, outs, cost_ref, chunks):
    step = pl.program_id(0)
    count = pl.num_programs(0) - 1
    low = low_half()

    def vector(index, plane, matmul):
        costs = []
        for half in range(2):
            if matmul is not None:
                matmul(half)
            costs.append(
                forward_vector(
                    gates_ref, refx_ref, chunks[index], 2 * index, half, outs[4 * index : 4 * index + 4]
                )
            )
        for g in range(G):
            cost_ref[plane, index, pl.ds(g * SUB, SUB), :] = jnp.where(
                low, costs[0][g], costs[1][g]
            )

    @pl.when(step < count)
    def _():
        vector(
            1,
            jnp.maximum(step - 1, 0),
            lambda part: forward_dot(rows_ref, w0_ref, chunks[0], part, 2),
        )
        vector(0, step, lambda part: forward_dot(rows_ref, w1_ref, chunks[1], part, 2))

    @pl.when(step == count)
    def _():
        vector(1, step - 1, None)


def edge_kernel(gates_ref, rows_ref, refx_ref, w0_ref, w1_ref, cot_ref, *rest):
    outs = rest[:8]
    up_ref, down_ref, cost, *chunks = rest[8:]
    forward_body(gates_ref, rows_ref, refx_ref, w0_ref, w1_ref, outs, cost, chunks)

    @pl.when(pl.program_id(0) == pl.num_programs(0) - 1)
    def _():
        down_ref[0:2] = cost[0:2]
        up_ref[0:2] = cost[2:4]
        down_ref[2] = cot_ref[0]
        up_ref[2] = cot_ref[cot_ref.shape[0] - 1]


def inner_kernel(gates_ref, rows_ref, refx_ref, w0_ref, w1_ref, *rest):
    outs = rest[8:16]
    cost_ref, *chunks = rest[16:]
    forward_body(gates_ref, rows_ref, refx_ref, w0_ref, w1_ref, outs, cost_ref, chunks)


def conv_kernel(
    taps_ref,
    below_ref,
    down_ref,
    inner_ref,
    up_ref,
    above_ref,
    cot_ref,
    regular_ref,
    cost_ref,
    grad_ref,
    cost,
    slope,
    smooth,
):
    planes = grad_ref.shape[0]
    local_views, _, groups, pixels = regular_ref.shape
    cost[0:2] = below_ref[0:2]
    cost[2:4] = down_ref[0:2]
    cost[4:planes] = inner_ref[...]
    cost[planes : planes + 2] = up_ref[0:2]
    cost[planes + 2 : planes + 4] = above_ref[0:2]
    cost_ref[...] = cost[2 : planes + 2]
    slope[0] = below_ref[2]
    slope[1 : planes + 1] = cot_ref[...]
    slope[planes + 1] = above_ref[2]

    def mix(source, tap):
        totals = [None] * G
        for k in range(3):
            for b in range(G):
                value = source(k, b)
                for a in range(G):
                    part = value * tap(k, a, b)
                    totals[a] = part if totals[a] is None else totals[a] + part
        return totals

    def forward_planes(index, carry):
        plane = 2 * index
        pres = mix(
            lambda k, g: cost[pl.ds(plane + k, 2), :, pl.ds(g * SUB, SUB), :],
            lambda k, o, g: taps_ref[k, o, g],
        )
        for o in range(G):
            pre = pres[o]
            rows = pl.ds(o * SUB, SUB)
            sig = jax.nn.sigmoid(pre)
            both = pl.ds(plane, 2)
            slope[both, :, rows, :] = slope[both, :, rows, :] * (sig * (1.0 + pre * (1.0 - sig)))
            smooth[both, :, rows, :] = pre * sig
        return carry

    lax.fori_loop(0, (planes + 2) // 2, forward_planes, 0)

    def backward_planes(index, carry):
        plane = 2 * index
        grads = mix(
            lambda k, o: slope[pl.ds(plane + 2 - k, 2), :, pl.ds(o * SUB, SUB), :],
            lambda k, g, o: taps_ref[k, o, g],
        )
        for g in range(G):
            grad_ref[pl.ds(plane, 2), :, pl.ds(g * SUB, SUB), :] = grads[g]
        for view in range(local_views):
            for tile in range(pixels // LANE):
                first = (tile % 2) * local_views + view
                for i in range(2):
                    regular_ref[view, plane + i, :, pl.ds(tile * LANE, LANE)] = smooth[
                        plane + i + 1, tile // 2, pl.ds(first, groups, stride=SUB), :
                    ].astype(jnp.bfloat16)
        return carry

    lax.fori_loop(0, planes // 2, backward_planes, 0)


def backward_kernel(src_ref, place_ref, gates_ref, refx_ref, w_ref, *rest):
    saved = (rest[0:4], rest[4:8])
    cost_ref, grad_ref, keep_ref, send_ref = rest[8:12]
    rows_lo, rows_hi, acc, dref, logit, w_prev, dense = rest[12:]
    step = pl.program_id(0)
    count = pl.num_programs(0) - 1
    groups, pairs = saved[0][1].shape[1:3]
    tiles = pairs // SUB
    lane_tiles = dref.shape[0]
    local_views = src_ref.shape[0]
    channels = groups * GC
    half_rows = rows_lo.shape[0]
    low = low_half()

    def vector(tile, upper, target):
        _, corr_ref, sig_ref, rden_ref = saved[tile // 2]
        warped_ref = saved[tile // 2][0]
        lanes = pl.ds((tile % 2) * LANE, LANE)
        full = pl.ds(tile * LANE, LANE)
        pack = tile // 2
        half = tile % 2
        rden = rden_ref[0, :, lanes]
        sig = sig_ref[0, :, lanes].reshape(tiles, SUB, LANE)
        wanted = range(groups // 2, groups) if upper else range(groups)
        num_grads = {}
        for g in wanted:
            grad = grad_ref[0, pack, pl.ds(g * SUB, SUB), :]
            num_grads[g] = spread(grad, half, low) * rden
        if upper:
            logit_grad = logit[:, full].reshape(tiles, SUB, LANE)
        else:
            mixed = None
            for g in range(groups):
                rows = pl.ds(g * SUB, SUB)
                part = grad_ref[0, pack, rows, :] * cost_ref[0, pack, rows, :]
                mixed = part if mixed is None else mixed + part
            vis_grad = -(spread(mixed, half, low) * rden)[None]
            for g in range(groups):
                vis_grad = vis_grad + num_grads[g][None] * corr_ref[0, g, :, lanes].reshape(
                    tiles, SUB, LANE
                )
            logit_grad = vis_grad * (sig * (1.0 - sig)) * (1.0 / GC)
            logit[:, full] = logit_grad.reshape(pairs, LANE)
        visible = (0.5 + sig) * (1.0 / GC)
        base = groups // 2 if upper else 0
        for g in range(base, base + groups // 2):
            corr_grad = visible * num_grads[g][None] + logit_grad * gates_ref[g][None]
            for j in range(0, GC, 2):
                c = g * GC + j
                local = (c - base * GC) * pairs
                both = jnp.concatenate(
                    [
                        (corr_grad * refx_ref[tile, pl.ds((c + i) * SUB, SUB), :][None]).reshape(
                            pairs, LANE
                        )
                        for i in range(2)
                    ],
                    axis=0,
                )
                target[pl.ds(local, 2 * pairs), full] = both.astype(jnp.bfloat16)
                warped = (
                    warped_ref[0, pl.ds(c * pairs, 2 * pairs), lanes]
                    .astype(jnp.float32)
                    .reshape(2, tiles, SUB, LANE)
                )
                for i in range(2):
                    dref[tile, pl.ds((c + i) * SUB, SUB), :] += jnp.sum(
                        corr_grad * warped[i], axis=0
                    )

    def matmul(rows, weights, base, index):
        product = jnp.dot(
            rows[...],
            weights(pl.ds(index * 2 * LANE, 2 * LANE)),
            preferred_element_type=jnp.float32,
        )
        for half in range(2):
            acc[2 * index + half, pl.ds(base, half_rows), :] += product[
                :, half * LANE : (half + 1) * LANE
            ]

    @pl.when(step == 0)
    def _():
        acc[...] = jnp.zeros_like(acc)
        dref[...] = jnp.zeros_like(dref)
        rows_hi[...] = jnp.zeros_like(rows_hi)
        w_prev[...] = jnp.zeros_like(w_prev)

    @pl.when(step < count)
    def _():
        for tile in range(lane_tiles):
            if tile % 2 == 0:
                matmul(rows_hi, lambda lanes: w_prev[:, lanes], half_rows, tile // 2)
            vector(tile, False, rows_lo)
        w_prev[...] = w_ref[0]
        for tile in range(lane_tiles):
            if tile % 2 == 0:
                matmul(rows_lo, lambda lanes: w_ref[0, :, lanes], 0, tile // 2)
            vector(tile, True, rows_hi)

    @pl.when(step == count)
    def _():
        for index in range(lane_tiles // 2):
            matmul(rows_hi, lambda lanes: w_prev[:, lanes], half_rows, index)
        own_index = place_ref[0]
        parity = place_ref[1]
        dense[...] = jnp.zeros_like(dense)
        for tile in range(lane_tiles):
            lanes = pl.ds(tile * LANE, LANE)
            for view in range(local_views):
                total = dref[tile, pl.ds(view, channels, stride=SUB), :]
                for copy in range(1, SUB // local_views):
                    first = copy * local_views + view
                    total = total + dref[tile, pl.ds(first, channels, stride=SUB), :]
                dense[view, :, lanes] = total
        for pair in range(pairs):
            view = src_ref[pair % local_views, pair // local_views]
            slot = position(view, own_index, local_views, dense.shape[0] // local_views)
            for tile in range(lane_tiles):
                dense[slot, :, pl.ds(tile * LANE, LANE)] += acc[
                    tile, pl.ds(pair, channels, stride=pairs), :
                ]
        blocks = keep_ref.shape[1] // SUB

        def one_view(view, carry):
            kept = []
            sent = []
            for block in range(blocks):
                mine = pl.multiple_of((2 * block + parity) * SUB, SUB)
                theirs = pl.multiple_of((2 * block + 1 - parity) * SUB, SUB)
                kept.append(dense[view, pl.ds(mine, SUB), :])
                sent.append(dense[view, pl.ds(theirs, SUB), :])
            keep_ref[view] = jnp.concatenate(kept, axis=0)
            send_ref[view] = jnp.concatenate(sent, axis=0).astype(jnp.bfloat16)
            return carry

        lax.fori_loop(0, dense.shape[0], one_view, 0)


def split_kernel(keep_ref, received_ref, even_ref, near_ref, far_ref):
    near = near_ref.shape[0]
    half = even_ref.shape[0]
    even_ref[...] = keep_ref[0:half] + received_ref[0:half].astype(jnp.float32)
    for out_ref, first, count in ((near_ref, half, near), (far_ref, half + near, half - near)):
        span = pl.ds(first, count)
        out_ref[...] = (keep_ref[span] + received_ref[span].astype(jnp.float32)).astype(
            jnp.bfloat16
        )


def spread_kernel(first, even_ref, received_ref, *out_refs):
    size = out_refs[0].shape[0]
    for index, out_ref in enumerate(out_refs):
        span = pl.ds(first + index * size, size)
        out_ref[...] = (
            even_ref[span] + received_ref[pl.ds(index * size, size)].astype(jnp.float32)
        ).astype(out_ref.dtype)


def per_plane(shape, plane):
    rank = len(shape)
    return pl.BlockSpec((1,) + tuple(shape[1:]), lambda d: (plane(d),) + (0,) * (rank - 1))


def fixed(shape):
    rank = len(shape)
    return pl.BlockSpec(tuple(shape), lambda d: (0,) * rank)


SMEM = functools.partial(pl.BlockSpec, memory_space=pltpu.SMEM)


def shards(features, sources, warp_weights, view_gate, depth_kernel, cotangent):
    view_count = lax.axis_size("view")
    plane_count = lax.axis_size("plane")
    own_index = lax.axis_index("view")
    plane_index = lax.axis_index("plane")
    local_views, channels, pixels = features.shape
    all_views, per_view = sources.shape
    pairs = local_views * per_view
    planes = warp_weights.shape[0]
    share = channels // plane_count
    blocks = plane_count // 2
    parity = plane_index % 2
    f32 = jnp.float32
    bf16 = jnp.bfloat16
    near = [(i, i ^ 1) for i in range(plane_count)]
    far = [(i, i ^ 2) for i in range(plane_count)]
    up = [(i, i + 1) for i in range(plane_count - 1)]
    down = [(i + 1, i) for i in range(plane_count - 1)]
    shape = jax.ShapeDtypeStruct

    halves = features.reshape(local_views, blocks, 2, share, pixels)
    mine = lax.dynamic_index_in_dim(halves, parity, 2, keepdims=False).reshape(
        local_views, channels // 2, pixels
    )

    def over_view(array, k):
        return lax.ppermute(array, "view", [(i, i ^ k) for i in range(view_count)])

    evens = range(2, view_count, 2)
    even = jnp.concatenate([mine] + [over_view(mine, k) for k in evens], axis=0)
    odd = over_view(even, 1)
    even_far = lax.ppermute(even, "plane", near)
    odd_far = lax.ppermute(odd, "plane", near)

    packed = (pixels // (2 * LANE), G * SUB, LANE)
    refx, gates, cot = pl.pallas_call(
        prep_kernel,
        out_shape=(
            shape((pixels // LANE, channels * SUB, LANE), f32),
            shape((G, SUB, LANE), f32),
            shape((planes,) + packed, f32),
        ),
        in_specs=[SMEM(), pl.BlockSpec(), pl.BlockSpec()],
        compiler_params=params(),
        name="prep",
    )(view_gate, features, cotangent)

    src_own = lax.dynamic_slice_in_dim(sources, own_index * local_views, local_views, 0)
    place = jnp.stack([own_index, parity]).astype(jnp.int32)
    rows = pl.pallas_call(
        assemble_kernel,
        out_shape=shape((channels * pairs, pixels), bf16),
        in_specs=[SMEM(), SMEM()] + [pl.BlockSpec()] * 4,
        scratch_shapes=[pltpu.VMEM((pixels // LANE, channels * pairs, LANE), f32)],
        compiler_params=params(),
        name="assemble",
    )(src_own, place, even, odd, even_far, odd_far)

    width = 2 * LANE
    saved = (
        shape((planes, channels * pairs, width), bf16),
        shape((planes, G, pairs, width), f32),
        shape((planes, pairs, width), f32),
        shape((planes, SUB, width), f32),
    )
    chunks = [pltpu.VMEM((channels * pairs, width), f32)] * 2

    def edge(d):
        return jnp.where(d < 2, d, planes - 4 + d)

    def inner(d):
        return d + 2

    def lane_half(index, plane, count):
        if index == 0:
            return lambda d: plane(jnp.minimum(d, count - 1))
        return lambda d: plane(jnp.maximum(d - 1, 0))

    def forward_specs(plane, count):
        ins = [fixed(gates.shape), fixed(rows.shape), fixed(refx.shape)] + [
            pl.BlockSpec(
                (1, width, pixels),
                lambda d, index=index: (plane(jnp.minimum(d, count - 1)), index, 0),
            )
            for index in range(2)
        ]
        outs = [
            per_plane(s.shape, lane_half(index, plane, count)) for index in range(2) for s in saved
        ]
        return ins, outs

    edge_ins, edge_outs = forward_specs(edge, 4)
    *edge_saved, up_load, down_load = pl.pallas_call(
        edge_kernel,
        out_shape=saved * 2 + (shape((3,) + packed, f32),) * 2,
        grid=(5,),
        in_specs=edge_ins + [fixed(cot.shape)],
        out_specs=tuple(edge_outs) + (fixed((3,) + packed),) * 2,
        scratch_shapes=[pltpu.VMEM((4,) + packed, f32)] + chunks,
        compiler_params=params(),
        name="forward_edge",
    )(gates, rows, refx, warp_weights, warp_weights, cot)
    below = lax.ppermute(up_load, "plane", up)
    above = lax.ppermute(down_load, "plane", down)
    inner_ins, inner_outs = forward_specs(inner, planes - 4)
    *saved_values, inner_cost = pl.pallas_call(
        inner_kernel,
        out_shape=saved * 2 + (shape((planes - 4,) + packed, f32),),
        grid=(planes - 3,),
        in_specs=inner_ins + [pl.BlockSpec(memory_space=pl.ANY)] * 8,
        out_specs=tuple(inner_outs) + (fixed((planes - 4,) + packed),),
        scratch_shapes=chunks,
        input_output_aliases={5 + i: i for i in range(8)},
        compiler_params=params(),
        cost_estimate=pl.CostEstimate(
            flops=2 * channels * pairs * pixels * pixels * (planes - 4),
            bytes_accessed=40 * 1024 * 1024,
            transcendentals=0,
        ),
        name="forward_inner",
    )(gates, rows, refx, warp_weights, warp_weights, *edge_saved)

    regular, cost, cost_grad = pl.pallas_call(
        conv_kernel,
        out_shape=(
            shape(cotangent.shape, bf16),
            shape((planes,) + packed, f32),
            shape((planes,) + packed, f32),
        ),
        in_specs=[SMEM()] + [pl.BlockSpec()] * 6,
        scratch_shapes=[
            pltpu.VMEM((planes + 4,) + packed, f32),
            pltpu.VMEM((planes + 2,) + packed, f32),
            pltpu.VMEM((planes + 2,) + packed, f32),
        ],
        compiler_params=params(),
        name="depth_conv",
    )(depth_kernel, below, down_load, inner_cost, up_load, above, cot)

    def clamped(d):
        return jnp.minimum(d, planes - 1)

    returned = (all_views, channels // 2, pixels)
    keep, send = pl.pallas_call(
        backward_kernel,
        out_shape=(shape(returned, f32), shape(returned, bf16)),
        grid=(planes + 1,),
        in_specs=[SMEM(), SMEM(), fixed(gates.shape), fixed(refx.shape)]
        + [per_plane(warp_weights.shape, clamped)]
        + [per_plane(s.shape, clamped) for s in saved * 2]
        + [per_plane(cost.shape, clamped), per_plane(cost_grad.shape, clamped)],
        out_specs=(fixed(returned), fixed(returned)),
        scratch_shapes=[
            pltpu.VMEM((channels * pairs // 2, pixels), bf16),
            pltpu.VMEM((channels * pairs // 2, pixels), bf16),
            pltpu.VMEM((pixels // LANE, channels * pairs, LANE), f32),
            pltpu.VMEM((pixels // LANE, channels * SUB, LANE), f32),
            pltpu.VMEM((pairs, pixels), f32),
            pltpu.VMEM((pixels, pixels), bf16),
            pltpu.VMEM((all_views, channels, pixels), f32),
        ],
        compiler_params=params(),
        name="backward",
    )(src_own, place, gates, refx, warp_weights, *saved_values, cost, cost_grad)

    received = lax.ppermute(send, "plane", near)
    half_views = all_views // 2
    close = half_views // 2
    piece = (local_views, channels // 2, pixels)
    even_sum, send_close, send_away = pl.pallas_call(
        split_kernel,
        out_shape=(
            shape((half_views,) + piece[1:], f32),
            shape((close,) + piece[1:], bf16),
            shape((half_views - close,) + piece[1:], bf16),
        ),
        compiler_params=params(),
        name="split",
    )(keep, received)
    away = over_view(send_away, 1)
    closer = over_view(send_close, 1)
    count = close // local_views
    away_parts = pl.pallas_call(
        functools.partial(spread_kernel, close),
        out_shape=(shape(piece, bf16),) * (view_count // 2 - count),
        compiler_params=params(),
        name="spread_away",
    )(even_sum, away)
    total, *close_parts = pl.pallas_call(
        functools.partial(spread_kernel, 0),
        out_shape=(shape(piece, f32),) + (shape(piece, bf16),) * (count - 1),
        compiler_params=params(),
        name="spread_close",
    )(even_sum, closer)
    for index, part in enumerate(away_parts):
        total = total + over_view(part, 2 * (count + index)).astype(f32)
    for index, part in enumerate(close_parts):
        total = total + over_view(part, 2 * (index + 1)).astype(f32)
    total = total + lax.ppermute(total, "plane", far)
    other = lax.ppermute(total, "plane", near)
    cut = (local_views, blocks, 1, share, pixels)
    first = jnp.where(parity == 0, total, other).reshape(cut)
    second = jnp.where(parity == 0, other, total).reshape(cut)
    feature_grads = jnp.concatenate([first, second], axis=2).reshape(features.shape)
    return (regular, feature_grads)


def solution(mesh):
    in_specs = (
        P("view", None, None),
        P(),
        P("plane", None, None),
        P(),
        P(),
        P("view", "plane", None, None),
    )
    out_specs = (P("view", "plane", None, None), P("view", None, None))
    return jax.shard_map(shards, mesh=mesh, in_specs=in_specs, out_specs=out_specs, check_vma=False)
```

```python
import functools

import jax
import jax.numpy as jnp
from jax import lax
from jax.experimental import pallas as pl
from jax.experimental.pallas import tpu as pltpu
from jax.sharding import PartitionSpec as P

G = 8
GC = 4
SUB = 8
LANE = 128
MIB = 1024 * 1024
NT = (((1,), (1,)), ((), ()))


def params(mib=16):
    return pltpu.CompilerParams(vmem_limit_bytes=mib * MIB)


def low_half():
    return lax.broadcasted_iota(jnp.int32, (SUB, LANE), 0) < SUB // 2


def swap_halves(tile):
    return pltpu.roll(tile, SUB // 2, 0)


def spread(tile, half, low):
    other = swap_halves(tile)
    return jnp.where(low, tile, other) if half == 0 else jnp.where(low, other, tile)


def pack_planes(array_ref, plane, out_ref, slot):
    local_views, _, groups, pixels = array_ref.shape
    for view in range(local_views):
        for tile in range(pixels // LANE):
            first = (tile % 2) * local_views + view
            out_ref[slot, tile // 2, pl.ds(first, groups, stride=SUB), :] = array_ref[
                view, plane, :, pl.ds(tile * LANE, LANE)
            ].astype(jnp.float32)


def prep_kernel(gate_ref, own_ref, cot_ref, refx_ref, gates_ref, cot_out):
    local_views, channels, pixels = own_ref.shape
    for tile in range(pixels // LANE):
        for view in range(local_views):
            own = own_ref[view, :, pl.ds(tile * LANE, LANE)].astype(jnp.float32)
            for copy in range(SUB // local_views):
                refx_ref[tile, pl.ds(copy * local_views + view, channels, stride=SUB), :] = own
    for g in range(gates_ref.shape[0]):
        gates_ref[g] = jnp.full((SUB, LANE), gate_ref[g], jnp.float32)

    def pack_one(plane, carry):
        pack_planes(cot_ref, plane, cot_out, plane)
        return carry

    lax.fori_loop(0, cot_out.shape[0], pack_one, 0)


def position(view, own_index, local_views, view_count):
    distance = (view // local_views) ^ own_index
    place = distance // 2 + (distance % 2) * (view_count // 2)
    return place * local_views + view % local_views


def assemble_kernel(src_ref, place_ref, *rest):
    *map_refs, rows_ref, maps, scratch = rest
    local_views, per_view = src_ref.shape
    tiles = scratch.shape[0]
    pairs = local_views * per_view
    view_count = maps.shape[1] // local_views
    blocks = maps.shape[2] // SUB
    own_index = place_ref[0]
    parity = place_ref[1]
    half = len(map_refs) // 2
    for side in range(2):
        first = 0
        for ref in map_refs[side * half : (side + 1) * half]:
            maps[side, first : first + ref.shape[0]] = ref[...]
            first += ref.shape[0]
    for pair in range(pairs):
        view = src_ref[pair % local_views, pair // local_views]
        slot = position(view, own_index, local_views, view_count)
        for tile in range(tiles):
            for side in range(2):
                values = maps[side, slot, :, pl.ds(tile * LANE, LANE)].astype(jnp.float32)
                held = parity if side == 0 else 1 - parity
                for block in range(blocks):
                    first = (2 * block + held) * (SUB * pairs) + pair
                    scratch[tile, pl.ds(first, SUB, stride=pairs), :] = values[
                        block * SUB : (block + 1) * SUB
                    ]
    for tile in range(tiles):
        rows_ref[:, pl.ds(tile * LANE, LANE)] = scratch[tile].astype(jnp.bfloat16)


def forward_vector(gates_ref, refx_ref, chunk, first_tile, half, outs):
    warped_ref, corr_ref, sig_ref, rden_ref = outs
    groups, pairs = corr_ref.shape[1:3]
    tiles = pairs // SUB
    lanes = pl.ds(half * LANE, LANE)
    logits = None
    for g in range(groups):
        total = None
        for j in range(0, GC, 2):
            c = g * GC + j
            span = pl.ds(c * pairs, 2 * pairs)
            both = chunk[span, lanes]
            warped_ref[0, span, lanes] = both.astype(jnp.bfloat16)
            both = both.reshape(2, tiles, SUB, LANE)
            for i in range(2):
                part = both[i] * refx_ref[first_tile + half, pl.ds((c + i) * SUB, SUB), :][None]
                total = part if total is None else total + part
        corr = total * (1.0 / GC)
        corr_ref[0, g, :, lanes] = corr.reshape(pairs, LANE)
        part = corr * gates_ref[g][None]
        logits = part if logits is None else logits + part
    sig = jax.nn.sigmoid(logits)
    sig_ref[0, :, lanes] = sig.reshape(pairs, LANE)
    visible = 0.5 + sig
    den = jnp.sum(visible, axis=0)
    rden = 1.0 / (den + swap_halves(den))
    rden_ref[0, :, lanes] = rden
    costs = []
    for g in range(groups):
        num = jnp.sum(visible * corr_ref[0, g, :, lanes].reshape(tiles, SUB, LANE), axis=0)
        costs.append((num + swap_halves(num)) * rden)
    return costs


def forward_dot(rows_ref, w_ref, chunk, part, parts):
    count = rows_ref.shape[0] // parts
    span = pl.ds(part * count, count)
    chunk[span, :] = lax.dot_general(
        rows_ref[span, :], w_ref[0], NT, preferred_element_type=jnp.float32
    )


def forward_body(gates_ref, rows_ref, refx_ref, w0_ref, w1_ref, outs, cost_ref, chunks):
    step = pl.program_id(0)
    count = pl.num_programs(0) - 1
    low = low_half()

    def vector(index, plane, matmul):
        costs = []
        for half in range(2):
            if matmul is not None:
                matmul(half)
            costs.append(
                forward_vector(
                    gates_ref, refx_ref, chunks[index], 2 * index, half, outs[4 * index : 4 * index + 4]
                )
            )
        for g in range(G):
            cost_ref[plane, index, pl.ds(g * SUB, SUB), :] = jnp.where(
                low, costs[0][g], costs[1][g]
            )

    @pl.when(step < count)
    def _():
        vector(
            1,
            jnp.maximum(step - 1, 0),
            lambda part: forward_dot(rows_ref, w0_ref, chunks[0], part, 2),
        )
        vector(0, step, lambda part: forward_dot(rows_ref, w1_ref, chunks[1], part, 2))

    @pl.when(step == count)
    def _():
        vector(1, step - 1, None)


def edge_kernel(gates_ref, rows_ref, refx_ref, w0_ref, w1_ref, cot_ref, *rest):
    outs = rest[:8]
    up_ref, down_ref, cost, *chunks = rest[8:]
    forward_body(gates_ref, rows_ref, refx_ref, w0_ref, w1_ref, outs, cost, chunks)

    @pl.when(pl.program_id(0) == pl.num_programs(0) - 1)
    def _():
        down_ref[0:2] = cost[0:2]
        up_ref[0:2] = cost[2:4]
        down_ref[2] = cot_ref[0]
        up_ref[2] = cot_ref[cot_ref.shape[0] - 1]


def inner_kernel(gates_ref, rows_ref, refx_ref, w0_ref, w1_ref, *rest):
    outs = rest[8:16]
    cost_ref, *chunks = rest[16:]
    forward_body(gates_ref, rows_ref, refx_ref, w0_ref, w1_ref, outs, cost_ref, chunks)


def conv_kernel(
    taps_ref,
    below_ref,
    down_ref,
    inner_ref,
    up_ref,
    above_ref,
    cot_ref,
    regular_ref,
    cost_ref,
    grad_ref,
    cost,
    slope,
    smooth,
):
    planes = grad_ref.shape[0]
    local_views, _, groups, pixels = regular_ref.shape
    cost[0:2] = below_ref[0:2]
    cost[2:4] = down_ref[0:2]
    cost[4:planes] = inner_ref[...]
    cost[planes : planes + 2] = up_ref[0:2]
    cost[planes + 2 : planes + 4] = above_ref[0:2]
    cost_ref[...] = cost[2 : planes + 2]
    slope[0] = below_ref[2]
    slope[1 : planes + 1] = cot_ref[...]
    slope[planes + 1] = above_ref[2]

    def mix(source, tap):
        totals = [None] * G
        for k in range(3):
            for b in range(G):
                value = source(k, b)
                for a in range(G):
                    part = value * tap(k, a, b)
                    totals[a] = part if totals[a] is None else totals[a] + part
        return totals

    def forward_planes(index, carry):
        plane = 2 * index
        pres = mix(
            lambda k, g: cost[pl.ds(plane + k, 2), :, pl.ds(g * SUB, SUB), :],
            lambda k, o, g: taps_ref[k, o, g],
        )
        for o in range(G):
            pre = pres[o]
            rows = pl.ds(o * SUB, SUB)
            sig = jax.nn.sigmoid(pre)
            both = pl.ds(plane, 2)
            slope[both, :, rows, :] = slope[both, :, rows, :] * (sig * (1.0 + pre * (1.0 - sig)))
            smooth[both, :, rows, :] = pre * sig
        return carry

    lax.fori_loop(0, (planes + 2) // 2, forward_planes, 0)

    def backward_planes(index, carry):
        plane = 2 * index
        grads = mix(
            lambda k, o: slope[pl.ds(plane + 2 - k, 2), :, pl.ds(o * SUB, SUB), :],
            lambda k, g, o: taps_ref[k, o, g],
        )
        for g in range(G):
            grad_ref[pl.ds(plane, 2), :, pl.ds(g * SUB, SUB), :] = grads[g]
        for view in range(local_views):
            for tile in range(pixels // LANE):
                first = (tile % 2) * local_views + view
                for i in range(2):
                    regular_ref[view, plane + i, :, pl.ds(tile * LANE, LANE)] = smooth[
                        plane + i + 1, tile // 2, pl.ds(first, groups, stride=SUB), :
                    ].astype(jnp.bfloat16)
        return carry

    lax.fori_loop(0, planes // 2, backward_planes, 0)


def backward_kernel(src_ref, place_ref, gates_ref, refx_ref, w_ref, *rest):
    saved = (rest[0:4], rest[4:8])
    cost_ref, grad_ref, keep_ref, send_ref = rest[8:12]
    rows_lo, rows_hi, acc, dref, logit, w_prev, dense = rest[12:]
    step = pl.program_id(0)
    count = pl.num_programs(0) - 1
    groups, pairs = saved[0][1].shape[1:3]
    tiles = pairs // SUB
    lane_tiles = dref.shape[0]
    local_views = src_ref.shape[0]
    channels = groups * GC
    half_rows = rows_lo.shape[0]
    low = low_half()

    def vector(tile, upper, target):
        _, corr_ref, sig_ref, rden_ref = saved[tile // 2]
        warped_ref = saved[tile // 2][0]
        lanes = pl.ds((tile % 2) * LANE, LANE)
        full = pl.ds(tile * LANE, LANE)
        pack = tile // 2
        half = tile % 2
        rden = rden_ref[0, :, lanes]
        sig = sig_ref[0, :, lanes].reshape(tiles, SUB, LANE)
        wanted = range(groups // 2, groups) if upper else range(groups)
        num_grads = {}
        for g in wanted:
            grad = grad_ref[0, pack, pl.ds(g * SUB, SUB), :]
            num_grads[g] = spread(grad, half, low) * rden
        if upper:
            logit_grad = logit[:, full].reshape(tiles, SUB, LANE)
        else:
            mixed = None
            for g in range(groups):
                rows = pl.ds(g * SUB, SUB)
                part = grad_ref[0, pack, rows, :] * cost_ref[0, pack, rows, :]
                mixed = part if mixed is None else mixed + part
            vis_grad = -(spread(mixed, half, low) * rden)[None]
            for g in range(groups):
                vis_grad = vis_grad + num_grads[g][None] * corr_ref[0, g, :, lanes].reshape(
                    tiles, SUB, LANE
                )
            logit_grad = vis_grad * (sig * (1.0 - sig)) * (1.0 / GC)
            logit[:, full] = logit_grad.reshape(pairs, LANE)
        visible = (0.5 + sig) * (1.0 / GC)
        base = groups // 2 if upper else 0
        for g in range(base, base + groups // 2):
            corr_grad = visible * num_grads[g][None] + logit_grad * gates_ref[g][None]
            for j in range(0, GC, 2):
                c = g * GC + j
                local = (c - base * GC) * pairs
                both = jnp.concatenate(
                    [
                        (corr_grad * refx_ref[tile, pl.ds((c + i) * SUB, SUB), :][None]).reshape(
                            pairs, LANE
                        )
                        for i in range(2)
                    ],
                    axis=0,
                )
                target[pl.ds(local, 2 * pairs), full] = both.astype(jnp.bfloat16)
                warped = (
                    warped_ref[0, pl.ds(c * pairs, 2 * pairs), lanes]
                    .astype(jnp.float32)
                    .reshape(2, tiles, SUB, LANE)
                )
                for i in range(2):
                    dref[tile, pl.ds((c + i) * SUB, SUB), :] += jnp.sum(
                        corr_grad * warped[i], axis=0
                    )

    def matmul(rows, weights, base, index):
        product = jnp.dot(
            rows[...],
            weights(pl.ds(index * 2 * LANE, 2 * LANE)),
            preferred_element_type=jnp.float32,
        )
        for half in range(2):
            acc[2 * index + half, pl.ds(base, half_rows), :] += product[
                :, half * LANE : (half + 1) * LANE
            ]

    @pl.when(step == 0)
    def _():
        acc[...] = jnp.zeros_like(acc)
        dref[...] = jnp.zeros_like(dref)
        rows_hi[...] = jnp.zeros_like(rows_hi)
        w_prev[...] = jnp.zeros_like(w_prev)

    @pl.when(step < count)
    def _():
        for tile in range(lane_tiles):
            if tile % 2 == 0:
                matmul(rows_hi, lambda lanes: w_prev[:, lanes], half_rows, tile // 2)
            vector(tile, False, rows_lo)
        w_prev[...] = w_ref[0]
        for tile in range(lane_tiles):
            if tile % 2 == 0:
                matmul(rows_lo, lambda lanes: w_ref[0, :, lanes], 0, tile // 2)
            vector(tile, True, rows_hi)

    @pl.when(step == count)
    def _():
        for index in range(lane_tiles // 2):
            matmul(rows_hi, lambda lanes: w_prev[:, lanes], half_rows, index)
        own_index = place_ref[0]
        parity = place_ref[1]
        dense[...] = jnp.zeros_like(dense)
        for tile in range(lane_tiles):
            lanes = pl.ds(tile * LANE, LANE)
            for view in range(local_views):
                total = dref[tile, pl.ds(view, channels, stride=SUB), :]
                for copy in range(1, SUB // local_views):
                    first = copy * local_views + view
                    total = total + dref[tile, pl.ds(first, channels, stride=SUB), :]
                dense[view, :, lanes] = total
        for pair in range(pairs):
            view = src_ref[pair % local_views, pair // local_views]
            slot = position(view, own_index, local_views, dense.shape[0] // local_views)
            for tile in range(lane_tiles):
                dense[slot, :, pl.ds(tile * LANE, LANE)] += acc[
                    tile, pl.ds(pair, channels, stride=pairs), :
                ]
        blocks = keep_ref.shape[1] // SUB

        def one_view(view, carry):
            kept = []
            sent = []
            for block in range(blocks):
                mine = pl.multiple_of((2 * block + parity) * SUB, SUB)
                theirs = pl.multiple_of((2 * block + 1 - parity) * SUB, SUB)
                kept.append(dense[view, pl.ds(mine, SUB), :])
                sent.append(dense[view, pl.ds(theirs, SUB), :])
            keep_ref[view] = jnp.concatenate(kept, axis=0)
            send_ref[view] = jnp.concatenate(sent, axis=0).astype(jnp.bfloat16)
            return carry

        lax.fori_loop(0, dense.shape[0], one_view, 0)


def split_kernel(keep_ref, received_ref, even_ref, near_ref, far_ref):
    near = near_ref.shape[0]
    half = even_ref.shape[0]
    even_ref[...] = keep_ref[0:half] + received_ref[0:half].astype(jnp.float32)
    for out_ref, first, count in ((near_ref, half, near), (far_ref, half + near, half - near)):
        span = pl.ds(first, count)
        out_ref[...] = (keep_ref[span] + received_ref[span].astype(jnp.float32)).astype(
            jnp.bfloat16
        )


def spread_kernel(first, even_ref, received_ref, after_ref, *out_refs):
    size = out_refs[0].shape[0]
    for index, out_ref in enumerate(out_refs):
        span = pl.ds(first + index * size, size)
        out_ref[...] = (
            even_ref[span] + received_ref[pl.ds(index * size, size)].astype(jnp.float32)
        ).astype(out_ref.dtype)


def per_plane(shape, plane):
    rank = len(shape)
    return pl.BlockSpec((1,) + tuple(shape[1:]), lambda d: (plane(d),) + (0,) * (rank - 1))


def fixed(shape):
    rank = len(shape)
    return pl.BlockSpec(tuple(shape), lambda d: (0,) * rank)


SMEM = functools.partial(pl.BlockSpec, memory_space=pltpu.SMEM)


def shards(features, sources, warp_weights, view_gate, depth_kernel, cotangent):
    view_count = lax.axis_size("view")
    plane_count = lax.axis_size("plane")
    own_index = lax.axis_index("view")
    plane_index = lax.axis_index("plane")
    local_views, channels, pixels = features.shape
    all_views, per_view = sources.shape
    pairs = local_views * per_view
    planes = warp_weights.shape[0]
    share = channels // plane_count
    blocks = plane_count // 2
    parity = plane_index % 2
    f32 = jnp.float32
    bf16 = jnp.bfloat16
    near = [(i, i ^ 1) for i in range(plane_count)]
    far = [(i, i ^ 2) for i in range(plane_count)]
    up = [(i, i + 1) for i in range(plane_count - 1)]
    down = [(i + 1, i) for i in range(plane_count - 1)]
    shape = jax.ShapeDtypeStruct

    halves = features.reshape(local_views, blocks, 2, share, pixels)
    mine = lax.dynamic_index_in_dim(halves, parity, 2, keepdims=False).reshape(
        local_views, channels // 2, pixels
    )

    def over_view(array, k):
        return lax.ppermute(array, "view", [(i, i ^ k) for i in range(view_count)])

    quarter = max(view_count // 4, 1)
    even = [mine] + [over_view(mine, k) for k in range(2, view_count, 2)]
    near_even = jnp.concatenate(even[:quarter], axis=0)
    far_even = jnp.concatenate(even[quarter:], axis=0)
    maps = [near_even, far_even, over_view(near_even, 1), over_view(far_even, 1)]
    maps = maps + [lax.ppermute(part, "plane", near) for part in maps]

    packed = (pixels // (2 * LANE), G * SUB, LANE)
    refx, gates, cot = pl.pallas_call(
        prep_kernel,
        out_shape=(
            shape((pixels // LANE, channels * SUB, LANE), f32),
            shape((G, SUB, LANE), f32),
            shape((planes,) + packed, f32),
        ),
        in_specs=[SMEM(), pl.BlockSpec(), pl.BlockSpec()],
        compiler_params=params(),
        cost_estimate=pl.CostEstimate(flops=10**9, bytes_accessed=4 * MIB, transcendentals=0),
        name="prep",
    )(view_gate, features, cotangent)

    src_own = lax.dynamic_slice_in_dim(sources, own_index * local_views, local_views, 0)
    place = jnp.stack([own_index, parity]).astype(jnp.int32)
    rows = pl.pallas_call(
        assemble_kernel,
        out_shape=shape((channels * pairs, pixels), bf16),
        in_specs=[SMEM(), SMEM()] + [pl.BlockSpec()] * len(maps),
        scratch_shapes=[
            pltpu.VMEM((2, all_views, channels // 2, pixels), bf16),
            pltpu.VMEM((pixels // LANE, channels * pairs, LANE), f32),
        ],
        compiler_params=params(24),
        name="assemble",
    )(src_own, place, *maps)

    width = 2 * LANE
    saved = (
        shape((planes, channels * pairs, width), bf16),
        shape((planes, G, pairs, width), f32),
        shape((planes, pairs, width), f32),
        shape((planes, SUB, width), f32),
    )
    chunks = [pltpu.VMEM((channels * pairs, width), f32)] * 2

    def edge(d):
        return jnp.where(d < 2, d, planes - 4 + d)

    def inner(d):
        return d + 2

    def lane_half(index, plane, count):
        if index == 0:
            return lambda d: plane(jnp.minimum(d, count - 1))
        return lambda d: plane(jnp.maximum(d - 1, 0))

    def forward_specs(plane, count):
        ins = [fixed(gates.shape), fixed(rows.shape), fixed(refx.shape)] + [
            pl.BlockSpec(
                (1, width, pixels),
                lambda d, index=index: (plane(jnp.minimum(d, count - 1)), index, 0),
            )
            for index in range(2)
        ]
        outs = [
            per_plane(s.shape, lane_half(index, plane, count)) for index in range(2) for s in saved
        ]
        return ins, outs

    edge_ins, edge_outs = forward_specs(edge, 4)
    *edge_saved, up_load, down_load = pl.pallas_call(
        edge_kernel,
        out_shape=saved * 2 + (shape((3,) + packed, f32),) * 2,
        grid=(5,),
        in_specs=edge_ins + [fixed(cot.shape)],
        out_specs=tuple(edge_outs) + (fixed((3,) + packed),) * 2,
        scratch_shapes=[pltpu.VMEM((4,) + packed, f32)] + chunks,
        compiler_params=params(20),
        name="forward_edge",
    )(gates, rows, refx, warp_weights, warp_weights, cot)
    below = lax.ppermute(up_load, "plane", up)
    above = lax.ppermute(down_load, "plane", down)
    inner_ins, inner_outs = forward_specs(inner, planes - 4)
    *saved_values, inner_cost = pl.pallas_call(
        inner_kernel,
        out_shape=saved * 2 + (shape((planes - 4,) + packed, f32),),
        grid=(planes - 3,),
        in_specs=inner_ins + [pl.BlockSpec(memory_space=pl.ANY)] * 8,
        out_specs=tuple(inner_outs) + (fixed((planes - 4,) + packed),),
        scratch_shapes=chunks,
        input_output_aliases={5 + i: i for i in range(8)},
        compiler_params=params(20),
        cost_estimate=pl.CostEstimate(
            flops=2 * channels * pairs * pixels * pixels * (planes - 4),
            bytes_accessed=40 * 1024 * 1024,
            transcendentals=0,
        ),
        name="forward_inner",
    )(gates, rows, refx, warp_weights, warp_weights, *edge_saved)

    regular, cost, cost_grad = pl.pallas_call(
        conv_kernel,
        out_shape=(
            shape(cotangent.shape, bf16),
            shape((planes,) + packed, f32),
            shape((planes,) + packed, f32),
        ),
        in_specs=[SMEM()] + [pl.BlockSpec()] * 6,
        scratch_shapes=[
            pltpu.VMEM((planes + 4,) + packed, f32),
            pltpu.VMEM((planes + 2,) + packed, f32),
            pltpu.VMEM((planes + 2,) + packed, f32),
        ],
        compiler_params=params(),
        name="depth_conv",
    )(depth_kernel, below, down_load, inner_cost, up_load, above, cot)

    def clamped(d):
        return jnp.minimum(d, planes - 1)

    returned = (all_views, channels // 2, pixels)
    keep, send = pl.pallas_call(
        backward_kernel,
        out_shape=(shape(returned, f32), shape(returned, bf16)),
        grid=(planes + 1,),
        in_specs=[SMEM(), SMEM(), fixed(gates.shape), fixed(refx.shape)]
        + [per_plane(warp_weights.shape, clamped)]
        + [per_plane(s.shape, clamped) for s in saved * 2]
        + [per_plane(cost.shape, clamped), per_plane(cost_grad.shape, clamped)],
        out_specs=(fixed(returned), fixed(returned)),
        scratch_shapes=[
            pltpu.VMEM((channels * pairs // 2, pixels), bf16),
            pltpu.VMEM((channels * pairs // 2, pixels), bf16),
            pltpu.VMEM((pixels // LANE, channels * pairs, LANE), f32),
            pltpu.VMEM((pixels // LANE, channels * SUB, LANE), f32),
            pltpu.VMEM((pairs, pixels), f32),
            pltpu.VMEM((pixels, pixels), bf16),
            pltpu.VMEM((all_views, channels, pixels), f32),
        ],
        compiler_params=params(16 + 14 * all_views * channels * pixels // MIB),
        name="backward",
    )(src_own, place, gates, refx, warp_weights, *saved_values, cost, cost_grad)

    received = lax.ppermute(send, "plane", near)
    half_views = all_views // 2
    close = half_views // 2
    piece = (local_views, channels // 2, pixels)
    even_sum, send_close, send_away = pl.pallas_call(
        split_kernel,
        out_shape=(
            shape((half_views,) + piece[1:], f32),
            shape((close,) + piece[1:], bf16),
            shape((half_views - close,) + piece[1:], bf16),
        ),
        compiler_params=params(32),
        name="split",
    )(keep, received)
    away = over_view(send_away, 1)
    closer = over_view(send_close, 1)
    count = close // local_views
    away_parts = pl.pallas_call(
        functools.partial(spread_kernel, close),
        out_shape=(shape(piece, bf16),) * (view_count // 2 - count),
        in_specs=[pl.BlockSpec(), pl.BlockSpec(), pl.BlockSpec(memory_space=pl.ANY)],
        compiler_params=params(32),
        name="spread_away",
    )(even_sum, away, away)
    total, *close_parts = pl.pallas_call(
        functools.partial(spread_kernel, 0),
        out_shape=(shape(piece, f32),) + (shape(piece, bf16),) * (count - 1),
        in_specs=[pl.BlockSpec(), pl.BlockSpec(), pl.BlockSpec(memory_space=pl.ANY)],
        compiler_params=params(32),
        name="spread_close",
    )(even_sum, closer, away_parts[0])
    for index, part in enumerate(away_parts):
        total = total + over_view(part, 2 * (count + index)).astype(f32)
    for index, part in enumerate(close_parts):
        total = total + over_view(part, 2 * (index + 1)).astype(f32)
    total = total + lax.ppermute(total, "plane", far)
    other = lax.ppermute(total, "plane", near)
    cut = (local_views, blocks, 1, share, pixels)
    first = jnp.where(parity == 0, total, other).reshape(cut)
    second = jnp.where(parity == 0, other, total).reshape(cut)
    feature_grads = jnp.concatenate([first, second], axis=2).reshape(features.shape)
    return (regular, feature_grads)


def solution(mesh):
    in_specs = (
        P("view", None, None),
        P(),
        P("plane", None, None),
        P(),
        P(),
        P("view", "plane", None, None),
    )
    out_specs = (P("view", "plane", None, None), P("view", None, None))
    return jax.shard_map(shards, mesh=mesh, in_specs=in_specs, out_specs=out_specs, check_vma=False)
```

```python
import functools

import jax
import jax.numpy as jnp
from jax import lax
from jax.experimental import pallas as pl
from jax.experimental.pallas import tpu as pltpu
from jax.sharding import PartitionSpec as P

G = 8
GC = 4
SUB = 8
LANE = 128
MIB = 1024 * 1024
NT = (((1,), (1,)), ((), ()))


def params(mib=16):
    return pltpu.CompilerParams(vmem_limit_bytes=mib * MIB)


def low_half():
    return lax.broadcasted_iota(jnp.int32, (SUB, LANE), 0) < SUB // 2


def swap_halves(tile):
    return pltpu.roll(tile, SUB // 2, 0)


def spread(tile, half, low):
    other = swap_halves(tile)
    return jnp.where(low, tile, other) if half == 0 else jnp.where(low, other, tile)


def pack_planes(array_ref, plane, out_ref, slot):
    local_views, _, groups, pixels = array_ref.shape
    for view in range(local_views):
        for tile in range(pixels // LANE):
            first = (tile % 2) * local_views + view
            out_ref[slot, tile // 2, pl.ds(first, groups, stride=SUB), :] = array_ref[
                view, plane, :, pl.ds(tile * LANE, LANE)
            ].astype(jnp.float32)


def prep_kernel(gate_ref, own_ref, cot_ref, refx_ref, gates_ref, cot_out):
    local_views, channels, pixels = own_ref.shape
    for tile in range(pixels // LANE):
        for view in range(local_views):
            own = own_ref[view, :, pl.ds(tile * LANE, LANE)].astype(jnp.float32)
            for copy in range(SUB // local_views):
                refx_ref[tile, pl.ds(copy * local_views + view, channels, stride=SUB), :] = own
    for g in range(gates_ref.shape[0]):
        gates_ref[g] = jnp.full((SUB, LANE), gate_ref[g], jnp.float32)

    def pack_one(plane, carry):
        pack_planes(cot_ref, plane, cot_out, plane)
        return carry

    lax.fori_loop(0, cot_out.shape[0], pack_one, 0)


def position(view, own_index, local_views, view_count):
    distance = (view // local_views) ^ own_index
    place = distance // 2 + (distance % 2) * (view_count // 2)
    return place * local_views + view % local_views


def assemble_kernel(src_ref, place_ref, *rest):
    *map_refs, rows_ref, maps, scratch = rest
    local_views, per_view = src_ref.shape
    tiles = scratch.shape[0]
    pairs = local_views * per_view
    view_count = maps.shape[1] // local_views
    blocks = maps.shape[2] // SUB
    own_index = place_ref[0]
    parity = place_ref[1]
    half = len(map_refs) // 2
    for side in range(2):
        first = 0
        for ref in map_refs[side * half : (side + 1) * half]:
            maps[side, first : first + ref.shape[0]] = ref[...]
            first += ref.shape[0]
    for pair in range(pairs):
        view = src_ref[pair % local_views, pair // local_views]
        slot = position(view, own_index, local_views, view_count)
        for tile in range(tiles):
            for side in range(2):
                values = maps[side, slot, :, pl.ds(tile * LANE, LANE)].astype(jnp.float32)
                held = parity if side == 0 else 1 - parity
                for block in range(blocks):
                    first = (2 * block + held) * (SUB * pairs) + pair
                    scratch[tile, pl.ds(first, SUB, stride=pairs), :] = values[
                        block * SUB : (block + 1) * SUB
                    ]
    for tile in range(tiles):
        rows_ref[:, pl.ds(tile * LANE, LANE)] = scratch[tile].astype(jnp.bfloat16)


def forward_vector(gates_ref, refx_ref, chunk, tile, outs):
    warped_ref, corr_ref, sig_ref, rden_ref = outs
    pairs = sig_ref.shape[1]
    tiles = pairs // SUB
    lanes = pl.ds((tile % 2) * LANE, LANE)
    logits = None
    corrs = []
    for g in range(G):
        total = None
        for j in range(0, GC, 2):
            c = g * GC + j
            span = pl.ds(c * pairs, 2 * pairs)
            both = chunk[span, lanes]
            warped_ref[0, span, lanes] = both.astype(jnp.bfloat16)
            both = both.reshape(2, tiles, SUB, LANE)
            for i in range(2):
                part = both[i] * refx_ref[tile, pl.ds((c + i) * SUB, SUB), :][None]
                total = part if total is None else total + part
        corr = total * (1.0 / GC)
        corrs.append(corr)
        part = corr * gates_ref[g][None]
        logits = part if logits is None else logits + part
        if g % 2 == 1:
            both = jnp.concatenate([item.reshape(pairs, LANE) for item in corrs[-2:]], axis=0)
            corr_ref[0, pl.ds((g - 1) * pairs, 2 * pairs), lanes] = both.astype(jnp.bfloat16)
    sig = jax.nn.sigmoid(logits)
    sig_ref[0, :, lanes] = sig.reshape(pairs, LANE)
    visible = 0.5 + sig
    den = jnp.sum(visible, axis=0)
    rden = 1.0 / (den + swap_halves(den))
    rden_ref[0, :, lanes] = rden
    costs = []
    for g in range(G):
        num = jnp.sum(visible * corrs[g], axis=0)
        costs.append((num + swap_halves(num)) * rden)
    return costs


def weight_copy(w_ref, held, sems, plane, slot):
    return pltpu.make_async_copy(w_ref.at[plane], held.at[slot], sems.at[slot])


def forward_body(plane_of, gates_ref, rows_ref, refx_ref, w_ref, outs, cost_ref, scratch):
    held, sems, *chunks = scratch
    step = pl.program_id(0)
    count = pl.num_programs(0) - 1
    slot = lax.rem(step, 2)
    low = low_half()

    def matmul(index, part):
        rows = pl.ds(part * (rows_ref.shape[0] // 2), rows_ref.shape[0] // 2)
        chunks[index][rows, :] = lax.dot_general(
            rows_ref[rows, :],
            held[slot, pl.ds(index * 2 * LANE, 2 * LANE), :],
            NT,
            preferred_element_type=jnp.float32,
        )

    def vector(index, plane, beside):
        costs = []
        for half in range(2):
            if beside is not None:
                matmul(beside, half)
            costs.append(
                forward_vector(
                    gates_ref,
                    refx_ref,
                    chunks[index],
                    2 * index + half,
                    outs[4 * index : 4 * index + 4],
                )
            )
        for g in range(G):
            cost_ref[plane, index, pl.ds(g * SUB, SUB), :] = jnp.where(
                low, costs[0][g], costs[1][g]
            )

    @pl.when(step == 0)
    def _():
        weight_copy(w_ref, held, sems, plane_of(0), 0).start()

    @pl.when(step + 1 < count)
    def _():
        weight_copy(w_ref, held, sems, plane_of(step + 1), 1 - slot).start()

    @pl.when(step < count)
    def _():
        weight_copy(w_ref, held, sems, plane_of(step), slot).wait()
        vector(1, jnp.maximum(step - 1, 0), 0)
        vector(0, step, 1)

    @pl.when(step == count)
    def _():
        vector(1, step - 1, None)


def edge_plane(planes, index):
    return jnp.where(index < 2, index, planes - 4 + index)


def edge_kernel(gates_ref, rows_ref, refx_ref, w_ref, cot_ref, *rest):
    up_ref, down_ref, cost, *scratch = rest[8:]
    planes = w_ref.shape[0]
    forward_body(
        functools.partial(edge_plane, planes),
        gates_ref,
        rows_ref,
        refx_ref,
        w_ref,
        rest[:8],
        cost,
        scratch,
    )

    @pl.when(pl.program_id(0) == pl.num_programs(0) - 1)
    def _():
        down_ref[0:2] = cost[0:2]
        up_ref[0:2] = cost[2:4]
        down_ref[2] = cot_ref[0]
        up_ref[2] = cot_ref[planes - 1]


def inner_kernel(gates_ref, rows_ref, refx_ref, w_ref, *rest):
    cost_ref, *scratch = rest[8:]
    forward_body(
        lambda index: index + 2, gates_ref, rows_ref, refx_ref, w_ref, rest[:8], cost_ref, scratch
    )


def depth_conv(
    taps_ref,
    below_ref,
    down_ref,
    inner_ref,
    up_ref,
    above_ref,
    cot_ref,
    regular_ref,
    cost,
    grad_ref,
    slope,
    smooth,
):
    planes = grad_ref.shape[0]
    local_views, _, groups, pixels = regular_ref.shape
    cost[0:2] = below_ref[0:2]
    cost[2:4] = down_ref[0:2]
    cost[4:planes] = inner_ref[...]
    cost[planes : planes + 2] = up_ref[0:2]
    cost[planes + 2 : planes + 4] = above_ref[0:2]
    slope[0] = below_ref[2]
    slope[1 : planes + 1] = cot_ref[...]
    slope[planes + 1] = above_ref[2]

    def mix(source, tap):
        totals = [None] * G
        for k in range(3):
            for b in range(G):
                value = source(k, b)
                for a in range(G):
                    part = value * tap(k, a, b)
                    totals[a] = part if totals[a] is None else totals[a] + part
        return totals

    def forward_planes(index, carry):
        plane = 2 * index
        pres = mix(
            lambda k, g: cost[pl.ds(plane + k, 2), :, pl.ds(g * SUB, SUB), :],
            lambda k, o, g: taps_ref[k, o, g],
        )
        for o in range(G):
            pre = pres[o]
            rows = pl.ds(o * SUB, SUB)
            sig = jax.nn.sigmoid(pre)
            both = pl.ds(plane, 2)
            slope[both, :, rows, :] = slope[both, :, rows, :] * (sig * (1.0 + pre * (1.0 - sig)))
            smooth[both, :, rows, :] = pre * sig
        return carry

    lax.fori_loop(0, (planes + 2) // 2, forward_planes, 0)

    def backward_planes(index, carry):
        plane = 2 * index
        grads = mix(
            lambda k, o: slope[pl.ds(plane + 2 - k, 2), :, pl.ds(o * SUB, SUB), :],
            lambda k, g, o: taps_ref[k, o, g],
        )
        for g in range(G):
            grad_ref[pl.ds(plane, 2), :, pl.ds(g * SUB, SUB), :] = grads[g]
        for view in range(local_views):
            for tile in range(pixels // LANE):
                first = (tile % 2) * local_views + view
                for i in range(2):
                    regular_ref[view, plane + i, :, pl.ds(tile * LANE, LANE)] = smooth[
                        plane + i + 1, tile // 2, pl.ds(first, groups, stride=SUB), :
                    ].astype(jnp.bfloat16)
        return carry

    lax.fori_loop(0, planes // 2, backward_planes, 0)


def backward_kernel(src_ref, place_ref, taps_ref, gates_ref, refx_ref, w_ref, *rest):
    halo_refs = rest[:6]
    inner_saved = (rest[6:10], rest[10:14])
    edge_saved = (rest[14:18], rest[18:22])
    regular_ref, keep_ref, send_ref = rest[22:25]
    cost, grad_ref, slope, smooth, rows_lo, rows_hi, acc, dref, logit, held, sems, dense = rest[25:]
    step = pl.program_id(0)
    count = pl.num_programs(0) - 1
    pairs = logit.shape[0]
    tiles = pairs // SUB
    lane_tiles = dref.shape[0]
    local_views = src_ref.shape[0]
    channels = G * GC
    half_rows = rows_lo.shape[0]
    low = low_half()
    inner_count = count - 4

    def plane_of(index):
        return jnp.where(index < inner_count, index + 2, edge_plane(count, index - inner_count))

    plane = plane_of(step)
    slot = lax.rem(step, 3)
    slot_before = lax.rem(step + 2, 3)

    def vector(saved, tile, upper, target):
        warped_ref, corr_ref, sig_ref, rden_ref = saved[tile // 2]
        lanes = pl.ds((tile % 2) * LANE, LANE)
        full = pl.ds(tile * LANE, LANE)
        pack = tile // 2
        half = tile % 2
        rden = rden_ref[0, :, lanes]
        sig = sig_ref[0, :, lanes].reshape(tiles, SUB, LANE)
        wanted = range(G // 2, G) if upper else range(G)
        num_grads = {}
        for g in wanted:
            grad = grad_ref[plane, pack, pl.ds(g * SUB, SUB), :]
            num_grads[g] = spread(grad, half, low) * rden
        if upper:
            logit_grad = logit[:, full].reshape(tiles, SUB, LANE)
        else:
            mixed = None
            for g in range(G):
                rows = pl.ds(g * SUB, SUB)
                part = grad_ref[plane, pack, rows, :] * cost[plane + 2, pack, rows, :]
                mixed = part if mixed is None else mixed + part
            vis_grad = -(spread(mixed, half, low) * rden)[None]
            for g in range(0, G, 2):
                corr = (
                    corr_ref[0, pl.ds(g * pairs, 2 * pairs), lanes]
                    .astype(jnp.float32)
                    .reshape(2, tiles, SUB, LANE)
                )
                vis_grad = vis_grad + num_grads[g][None] * corr[0]
                vis_grad = vis_grad + num_grads[g + 1][None] * corr[1]
            logit_grad = vis_grad * (sig * (1.0 - sig)) * (1.0 / GC)
            logit[:, full] = logit_grad.reshape(pairs, LANE)
        visible = (0.5 + sig) * (1.0 / GC)
        base = G // 2 if upper else 0
        for g in range(base, base + G // 2):
            corr_grad = visible * num_grads[g][None] + logit_grad * gates_ref[g][None]
            for j in range(0, GC, 2):
                c = g * GC + j
                local = (c - base * GC) * pairs
                both = jnp.concatenate(
                    [
                        (corr_grad * refx_ref[tile, pl.ds((c + i) * SUB, SUB), :][None]).reshape(
                            pairs, LANE
                        )
                        for i in range(2)
                    ],
                    axis=0,
                )
                target[pl.ds(local, 2 * pairs), full] = both.astype(jnp.bfloat16)
                warped = (
                    warped_ref[0, pl.ds(c * pairs, 2 * pairs), lanes]
                    .astype(jnp.float32)
                    .reshape(2, tiles, SUB, LANE)
                )
                for i in range(2):
                    dref[tile, pl.ds((c + i) * SUB, SUB), :] += jnp.sum(
                        corr_grad * warped[i], axis=0
                    )

    def matmul(rows, where, base, index):
        product = jnp.dot(
            rows[...],
            held[where, :, pl.ds(index * 2 * LANE, 2 * LANE)],
            preferred_element_type=jnp.float32,
        )
        for half in range(2):
            acc[2 * index + half, pl.ds(base, half_rows), :] += product[
                :, half * LANE : (half + 1) * LANE
            ]

    def one_plane(saved):
        weight_copy(w_ref, held, sems, plane, slot).wait()
        for tile in range(lane_tiles):
            if tile % 2 == 0:
                matmul(rows_hi, slot_before, half_rows, tile // 2)
            vector(saved, tile, False, rows_lo)
        for tile in range(lane_tiles):
            if tile % 2 == 0:
                matmul(rows_lo, slot, 0, tile // 2)
            vector(saved, tile, True, rows_hi)

    @pl.when(step == 0)
    def _():
        weight_copy(w_ref, held, sems, plane_of(0), 0).start()
        acc[...] = jnp.zeros_like(acc)
        dref[...] = jnp.zeros_like(dref)
        rows_hi[...] = jnp.zeros_like(rows_hi)
        held[2] = jnp.zeros_like(held[2])
        depth_conv(taps_ref, *halo_refs, regular_ref, cost, grad_ref, slope, smooth)

    @pl.when(step + 1 < count)
    def _():
        weight_copy(w_ref, held, sems, plane_of(step + 1), lax.rem(step + 1, 3)).start()

    @pl.when(step < inner_count)
    def _():
        one_plane(inner_saved)

    @pl.when((step >= inner_count) & (step < count))
    def _():
        one_plane(edge_saved)

    @pl.when(step == count)
    def _():
        for index in range(lane_tiles // 2):
            matmul(rows_hi, slot_before, half_rows, index)
        own_index = place_ref[0]
        parity = place_ref[1]
        dense[...] = jnp.zeros_like(dense)
        for tile in range(lane_tiles):
            lanes = pl.ds(tile * LANE, LANE)
            for view in range(local_views):
                total = dref[tile, pl.ds(view, channels, stride=SUB), :]
                for copy in range(1, SUB // local_views):
                    first = copy * local_views + view
                    total = total + dref[tile, pl.ds(first, channels, stride=SUB), :]
                dense[view, :, lanes] = total
        for pair in range(pairs):
            view = src_ref[pair % local_views, pair // local_views]
            slot = position(view, own_index, local_views, dense.shape[0] // local_views)
            for tile in range(lane_tiles):
                dense[slot, :, pl.ds(tile * LANE, LANE)] += acc[
                    tile, pl.ds(pair, channels, stride=pairs), :
                ]
        blocks = keep_ref.shape[1] // SUB

        def one_view(view, carry):
            kept = []
            sent = []
            for block in range(blocks):
                mine = pl.multiple_of((2 * block + parity) * SUB, SUB)
                theirs = pl.multiple_of((2 * block + 1 - parity) * SUB, SUB)
                kept.append(dense[view, pl.ds(mine, SUB), :])
                sent.append(dense[view, pl.ds(theirs, SUB), :])
            keep_ref[view] = jnp.concatenate(kept, axis=0)
            send_ref[view] = jnp.concatenate(sent, axis=0).astype(jnp.bfloat16)
            return carry

        lax.fori_loop(0, dense.shape[0], one_view, 0)


def split_kernel(first, keep_ref, received_ref, after_ref, even_ref, send_ref):
    count = even_ref.shape[0]
    half = keep_ref.shape[0] // 2
    for out_ref, start in ((even_ref, first), (send_ref, half + first)):
        span = pl.ds(start, count)
        out_ref[...] = (keep_ref[span] + received_ref[span].astype(jnp.float32)).astype(
            out_ref.dtype
        )


def spread_kernel(even_ref, received_ref, *out_refs):
    size = out_refs[0].shape[0]
    for index, out_ref in enumerate(out_refs):
        span = pl.ds(index * size, size)
        out_ref[...] = (even_ref[span] + received_ref[span].astype(jnp.float32)).astype(
            out_ref.dtype
        )


def per_plane(shape, plane):
    rank = len(shape)
    return pl.BlockSpec((1,) + tuple(shape[1:]), lambda d: (plane(d),) + (0,) * (rank - 1))


def fixed(shape):
    rank = len(shape)
    return pl.BlockSpec(tuple(shape), lambda d: (0,) * rank, pipeline_mode=pl.Buffered(1))


SMEM = functools.partial(pl.BlockSpec, memory_space=pltpu.SMEM)


def shards(features, sources, warp_weights, view_gate, depth_kernel, cotangent):
    view_count = lax.axis_size("view")
    plane_count = lax.axis_size("plane")
    own_index = lax.axis_index("view")
    plane_index = lax.axis_index("plane")
    local_views, channels, pixels = features.shape
    all_views, per_view = sources.shape
    pairs = local_views * per_view
    planes = warp_weights.shape[0]
    share = channels // plane_count
    blocks = plane_count // 2
    parity = plane_index % 2
    f32 = jnp.float32
    bf16 = jnp.bfloat16
    near = [(i, i ^ 1) for i in range(plane_count)]
    far = [(i, i ^ 2) for i in range(plane_count)]
    up = [(i, i + 1) for i in range(plane_count - 1)]
    down = [(i + 1, i) for i in range(plane_count - 1)]
    shape = jax.ShapeDtypeStruct

    halves = features.reshape(local_views, blocks, 2, share, pixels)
    mine = lax.dynamic_index_in_dim(halves, parity, 2, keepdims=False).reshape(
        local_views, channels // 2, pixels
    )

    def over_view(array, k):
        return lax.ppermute(array, "view", [(i, i ^ k) for i in range(view_count)])

    quarter = max(view_count // 4, 1)
    even = [mine] + [over_view(mine, k) for k in range(2, view_count, 2)]
    near_even = jnp.concatenate(even[:quarter], axis=0)
    far_even = jnp.concatenate(even[quarter:], axis=0)
    packed = (pixels // (2 * LANE), G * SUB, LANE)
    refx, gates, cot = pl.pallas_call(
        prep_kernel,
        out_shape=(
            shape((pixels // LANE, channels * SUB, LANE), f32),
            shape((G, SUB, LANE), f32),
            shape((planes,) + packed, f32),
        ),
        in_specs=[SMEM(), pl.BlockSpec(), pl.BlockSpec()],
        compiler_params=params(),
        cost_estimate=pl.CostEstimate(flops=10**9, bytes_accessed=4 * MIB, transcendentals=0),
        name="prep",
    )(view_gate, features, cotangent)
    near_even, refx, gates, cot = lax.optimization_barrier((near_even, refx, gates, cot))
    maps = [near_even, far_even, over_view(near_even, 1), over_view(far_even, 1)]
    maps = maps + [lax.ppermute(part, "plane", near) for part in maps]

    src_own = lax.dynamic_slice_in_dim(sources, own_index * local_views, local_views, 0)
    place = jnp.stack([own_index, parity]).astype(jnp.int32)
    rows = pl.pallas_call(
        assemble_kernel,
        out_shape=shape((channels * pairs, pixels), bf16),
        in_specs=[SMEM(), SMEM()] + [pl.BlockSpec()] * len(maps),
        scratch_shapes=[
            pltpu.VMEM((2, all_views, channels // 2, pixels), bf16),
            pltpu.VMEM((pixels // LANE, channels * pairs, LANE), f32),
        ],
        compiler_params=params(24),
        name="assemble",
    )(src_own, place, *maps)

    width = 2 * LANE

    def saved_shapes(count):
        one = (
            shape((count, channels * pairs, width), bf16),
            shape((count, G * pairs, width), bf16),
            shape((count, pairs, width), f32),
            shape((count, SUB, width), f32),
        )
        return one * 2

    def saved_specs(count):
        specs = []
        for index, item in enumerate(saved_shapes(count)):
            if index < 4:
                specs.append(per_plane(item.shape, lambda d: jnp.minimum(d, count - 1)))
            else:
                specs.append(per_plane(item.shape, lambda d: jnp.maximum(d - 1, 0)))
        return specs

    hbm = pl.BlockSpec(memory_space=pltpu.HBM)
    fixed_specs = [fixed(gates.shape), fixed(rows.shape), fixed(refx.shape), hbm]
    scratch = [
        pltpu.VMEM((2, pixels, pixels), bf16),
        pltpu.SemaphoreType.DMA((2,)),
        pltpu.VMEM((channels * pairs, width), f32),
        pltpu.VMEM((channels * pairs, width), f32),
    ]
    inner_count = planes - 4
    load = (3,) + packed
    *edge_saved, up_load, down_load = pl.pallas_call(
        edge_kernel,
        out_shape=saved_shapes(4) + (shape(load, f32),) * 2,
        grid=(5,),
        in_specs=fixed_specs + [fixed(cot.shape)],
        out_specs=tuple(saved_specs(4)) + (fixed(load),) * 2,
        scratch_shapes=[pltpu.VMEM((4,) + packed, f32)] + scratch,
        compiler_params=params(14),
        name="forward_edge",
    )(gates, rows, refx, warp_weights, cot)
    below = lax.ppermute(up_load, "plane", up)
    above = lax.ppermute(down_load, "plane", down)
    *inner_saved, inner_cost = pl.pallas_call(
        inner_kernel,
        out_shape=saved_shapes(inner_count) + (shape((inner_count,) + packed, f32),),
        grid=(inner_count + 1,),
        in_specs=fixed_specs,
        out_specs=tuple(saved_specs(inner_count)) + (fixed((inner_count,) + packed),),
        scratch_shapes=scratch,
        compiler_params=params(14),
        cost_estimate=pl.CostEstimate(
            flops=2 * channels * pairs * pixels * pixels * inner_count,
            bytes_accessed=40 * MIB,
            transcendentals=0,
        ),
        name="forward_inner",
    )(gates, rows, refx, warp_weights)

    halo = (below, down_load, inner_cost, up_load, above, cot)
    returned = (all_views, channels // 2, pixels)
    regular, keep, send = pl.pallas_call(
        backward_kernel,
        out_shape=(shape(cotangent.shape, bf16), shape(returned, f32), shape(returned, bf16)),
        grid=(planes + 1,),
        in_specs=[SMEM()] * 3
        + [fixed(gates.shape), fixed(refx.shape), hbm]
        + [fixed(item.shape) for item in halo]
        + [
            per_plane(item.shape, lambda d: jnp.minimum(d, inner_count - 1))
            for item in inner_saved
        ]
        + [
            per_plane(item.shape, lambda d: jnp.clip(d - inner_count, 0, 3))
            for item in edge_saved
        ],
        out_specs=(fixed(cotangent.shape), fixed(returned), fixed(returned)),
        scratch_shapes=[
            pltpu.VMEM((planes + 4,) + packed, f32),
            pltpu.VMEM((planes,) + packed, f32),
            pltpu.VMEM((planes + 2,) + packed, f32),
            pltpu.VMEM((planes + 2,) + packed, f32),
            pltpu.VMEM((channels * pairs // 2, pixels), bf16),
            pltpu.VMEM((channels * pairs // 2, pixels), bf16),
            pltpu.VMEM((pixels // LANE, channels * pairs, LANE), f32),
            pltpu.VMEM((pixels // LANE, channels * SUB, LANE), f32),
            pltpu.VMEM((pairs, pixels), f32),
            pltpu.VMEM((3, pixels, pixels), bf16),
            pltpu.SemaphoreType.DMA((3,)),
            pltpu.VMEM((all_views, channels, pixels), f32),
        ],
        compiler_params=params(15 + 14 * all_views * channels * pixels // MIB),
        name="backward",
    )(
        src_own,
        place,
        depth_kernel,
        gates,
        refx,
        warp_weights,
        *halo,
        *inner_saved,
        *edge_saved,
    )

    received = lax.ppermute(send, "plane", near)
    close = quarter * local_views
    piece = (local_views, channels // 2, pixels)
    anywhere = pl.BlockSpec(memory_space=pl.ANY)

    def stage(first, count, after, kind):
        even_sum, outgoing = pl.pallas_call(
            functools.partial(split_kernel, first),
            out_shape=(shape((count,) + piece[1:], f32), shape((count,) + piece[1:], bf16)),
            in_specs=[pl.BlockSpec(), pl.BlockSpec(), anywhere],
            compiler_params=params(32),
            name="split",
        )(keep, received, after)
        incoming = over_view(outgoing, 1)
        return pl.pallas_call(
            spread_kernel,
            out_shape=(shape(piece, kind),) + (shape(piece, bf16),) * (count // local_views - 1),
            compiler_params=params(32),
            name="spread",
        )(even_sum, incoming)

    away_parts = stage(close, all_views // 2 - close, received, bf16)
    total, *close_parts = stage(0, close, away_parts[0], f32)
    for index, part in enumerate(away_parts):
        total = total + over_view(part, 2 * (quarter + index)).astype(f32)
    for index, part in enumerate(close_parts):
        total = total + over_view(part, 2 * (index + 1)).astype(f32)
    total = total + lax.ppermute(total, "plane", far)
    other = lax.ppermute(total, "plane", near)
    cut = (local_views, blocks, 1, share, pixels)
    first = jnp.where(parity == 0, total, other).reshape(cut)
    second = jnp.where(parity == 0, other, total).reshape(cut)
    feature_grads = jnp.concatenate([first, second], axis=2).reshape(features.shape)
    return (regular, feature_grads)


def solution(mesh):
    in_specs = (
        P("view", None, None),
        P(),
        P("plane", None, None),
        P(),
        P(),
        P("view", "plane", None, None),
    )
    out_specs = (P("view", "plane", None, None), P("view", None, None))
    return jax.shard_map(shards, mesh=mesh, in_specs=in_specs, out_specs=out_specs, check_vma=False)
```

```python
import functools

import jax
import jax.numpy as jnp
from jax import lax
from jax.experimental import pallas as pl
from jax.experimental.pallas import tpu as pltpu
from jax.sharding import PartitionSpec as P

G = 8
GC = 4
SUB = 8
LANE = 128
MIB = 1024 * 1024
PARTS = 4
BACK_PARTS = 2
NT = (((1,), (1,)), ((), ()))


def params(mib=16):
    return pltpu.CompilerParams(vmem_limit_bytes=mib * MIB)


def low_half():
    return lax.broadcasted_iota(jnp.int32, (SUB, LANE), 0) < SUB // 2


def swap_halves(tile):
    return pltpu.roll(tile, SUB // 2, 0)


def spread(tile, half, low):
    other = swap_halves(tile)
    return jnp.where(low, tile, other) if half == 0 else jnp.where(low, other, tile)


def pack_planes(array_ref, plane, out_ref, slot):
    local_views, _, groups, pixels = array_ref.shape
    for view in range(local_views):
        for tile in range(pixels // LANE):
            first = (tile % 2) * local_views + view
            out_ref[slot, tile // 2, pl.ds(first, groups, stride=SUB), :] = array_ref[
                view, plane, :, pl.ds(tile * LANE, LANE)
            ].astype(jnp.float32)


def prep_kernel(
    gate_ref, own_hbm, cot_hbm, refx_ref, gates_ref, cot_out, own_ref, cot_ref, sems
):
    copies = [
        pltpu.make_async_copy(own_hbm, own_ref, sems.at[0]),
        pltpu.make_async_copy(cot_hbm, cot_ref, sems.at[1]),
    ]
    for copy in copies:
        copy.start()
    for copy in copies:
        copy.wait()
    local_views, channels, pixels = own_ref.shape
    for tile in range(pixels // LANE):
        for view in range(local_views):
            own = own_ref[view, :, pl.ds(tile * LANE, LANE)].astype(jnp.float32)
            for copied in range(SUB // local_views):
                first = copied * local_views + view
                refx_ref[tile, pl.ds(first, channels, stride=SUB), :] = own
    for g in range(gates_ref.shape[0]):
        gates_ref[g] = jnp.full((SUB, LANE), gate_ref[g], jnp.float32)

    def pack_one(plane, carry):
        pack_planes(cot_ref, plane, cot_out, plane)
        return carry

    lax.fori_loop(0, cot_out.shape[0], pack_one, 0)


def position(view, own_index, local_views, view_count):
    distance = (view // local_views) ^ own_index
    place = distance // 2 + (distance % 2) * (view_count // 2)
    return place * local_views + view % local_views


def assemble_kernel(src_ref, place_ref, *rest):
    *map_refs, rows_ref, maps, scratch = rest
    local_views, per_view = src_ref.shape
    tiles = scratch.shape[0]
    pairs = local_views * per_view
    view_count = maps.shape[1] // local_views
    blocks = maps.shape[2] // SUB
    own_index = place_ref[0]
    parity = place_ref[1]
    half = len(map_refs) // 2
    for side in range(2):
        first = 0
        for ref in map_refs[side * half : (side + 1) * half]:
            maps[side, first : first + ref.shape[0]] = ref[...]
            first += ref.shape[0]
    for pair in range(pairs):
        view = src_ref[pair % local_views, pair // local_views]
        slot = position(view, own_index, local_views, view_count)
        for tile in range(tiles):
            for side in range(2):
                values = maps[side, slot, :, pl.ds(tile * LANE, LANE)].astype(jnp.float32)
                held = parity if side == 0 else 1 - parity
                for block in range(blocks):
                    first = (2 * block + held) * (SUB * pairs) + pair
                    scratch[tile, pl.ds(first, SUB, stride=pairs), :] = values[
                        block * SUB : (block + 1) * SUB
                    ]
    for tile in range(tiles):
        rows_ref[:, pl.ds(tile * LANE, LANE)] = scratch[tile].astype(jnp.bfloat16)


def forward_vector(gates_ref, refx_ref, chunk, tile, outs, held_corr, tick):
    warped_ref, corr_ref, sig_ref, rden_ref = outs
    pairs = sig_ref.shape[1]
    tiles = pairs // SUB
    lanes = pl.ds((tile % 2) * LANE, LANE)
    logits = None
    corrs = []
    for g in range(G):
        tick()
        total = None
        for j in range(0, GC, 2):
            c = g * GC + j
            span = pl.ds(c * pairs, 2 * pairs)
            both = chunk[span, lanes]
            warped_ref[0, span, lanes] = both.astype(jnp.bfloat16)
            both = both.reshape(2, tiles, SUB, LANE)
            for i in range(2):
                part = both[i] * refx_ref[tile, pl.ds((c + i) * SUB, SUB), :][None]
                total = part if total is None else total + part
        corr = total * (1.0 / GC)
        corrs.append(corr)
        held_corr[pl.ds(g * pairs, pairs), :] = corr.reshape(pairs, LANE)
        part = corr * gates_ref[g][None]
        logits = part if logits is None else logits + part
        if g % 2 == 1:
            both = jnp.concatenate([item.reshape(pairs, LANE) for item in corrs[-2:]], axis=0)
            corr_ref[0, pl.ds((g - 1) * pairs, 2 * pairs), lanes] = both.astype(jnp.bfloat16)
    sig = jax.nn.sigmoid(logits)
    sig_ref[0, :, lanes] = sig.reshape(pairs, LANE)
    visible = 0.5 + sig
    den = jnp.sum(visible, axis=0)
    rden = 1.0 / (den + swap_halves(den))
    rden_ref[0, :, lanes] = rden
    costs = []
    for g in range(G):
        corr = held_corr[pl.ds(g * pairs, pairs), :].reshape(tiles, SUB, LANE)
        num = jnp.sum(visible * corr, axis=0)
        costs.append((num + swap_halves(num)) * rden)
    return costs


def ticker(thunks, ticks):
    state = [0, 0]

    def tick():
        state[0] += 1
        while state[1] * ticks < state[0] * len(thunks) and state[1] < len(thunks):
            thunks[state[1]]()
            state[1] += 1

    return tick


def weight_copy(w_ref, held, sems, plane, slot):
    return pltpu.make_async_copy(w_ref.at[plane], held.at[slot], sems.at[slot])


def forward_body(plane_of, gates_ref, rows_ref, refx_ref, w_ref, outs, cost_ref, scratch):
    held, sems, held_corr, *chunks = scratch
    step = pl.program_id(0)
    count = pl.num_programs(0) - 1
    slot = lax.rem(step, 2)
    low = low_half()

    def matmul(index, part):
        rows = pl.ds(part * (rows_ref.shape[0] // PARTS), rows_ref.shape[0] // PARTS)
        chunks[index][rows, :] = lax.dot_general(
            rows_ref[rows, :],
            held[slot, pl.ds(index * 2 * LANE, 2 * LANE), :],
            NT,
            preferred_element_type=jnp.float32,
        )

    def vector(index, plane, beside):
        costs = []
        thunks = []
        if beside is not None:
            thunks = [functools.partial(matmul, beside, part) for part in range(PARTS)]
        tick = ticker(thunks, 2 * G)
        for half in range(2):
            costs.append(
                forward_vector(
                    gates_ref,
                    refx_ref,
                    chunks[index],
                    2 * index + half,
                    outs[4 * index : 4 * index + 4],
                    held_corr,
                    tick,
                )
            )
        for g in range(G):
            cost_ref[plane, index, pl.ds(g * SUB, SUB), :] = jnp.where(
                low, costs[0][g], costs[1][g]
            )

    @pl.when(step == 0)
    def _():
        weight_copy(w_ref, held, sems, plane_of(0), 0).start()

    @pl.when(step + 1 < count)
    def _():
        weight_copy(w_ref, held, sems, plane_of(step + 1), 1 - slot).start()

    @pl.when(step < count)
    def _():
        weight_copy(w_ref, held, sems, plane_of(step), slot).wait()
        vector(1, jnp.maximum(step - 1, 0), 0)
        vector(0, step, 1)

    @pl.when(step == count)
    def _():
        vector(1, step - 1, None)


def edge_plane(planes, index):
    return jnp.where(index < 2, index, planes - 4 + index)


def edge_kernel(gates_ref, rows_ref, refx_ref, w_ref, cot_ref, *rest):
    up_ref, down_ref, cost, *scratch = rest[8:]
    planes = w_ref.shape[0]
    forward_body(
        functools.partial(edge_plane, planes),
        gates_ref,
        rows_ref,
        refx_ref,
        w_ref,
        rest[:8],
        cost,
        scratch,
    )

    @pl.when(pl.program_id(0) == pl.num_programs(0) - 1)
    def _():
        down_ref[0:2] = cost[0:2]
        up_ref[0:2] = cost[2:4]
        down_ref[2] = cot_ref[0]
        up_ref[2] = cot_ref[planes - 1]


def inner_kernel(gates_ref, rows_ref, refx_ref, w_ref, *rest):
    cost_ref, *scratch = rest[8:]
    forward_body(
        lambda index: index + 2, gates_ref, rows_ref, refx_ref, w_ref, rest[:8], cost_ref, scratch
    )


def depth_conv(
    taps_ref,
    below_ref,
    down_ref,
    inner_ref,
    up_ref,
    above_ref,
    cot_ref,
    regular_ref,
    cost,
    grad_ref,
    slope,
    smooth,
):
    planes = grad_ref.shape[0]
    local_views, _, groups, pixels = regular_ref.shape
    cost[0:2] = below_ref[0:2]
    cost[2:4] = down_ref[0:2]
    cost[4:planes] = inner_ref[...]
    cost[planes : planes + 2] = up_ref[0:2]
    cost[planes + 2 : planes + 4] = above_ref[0:2]
    slope[0] = below_ref[2]
    slope[1 : planes + 1] = cot_ref[...]
    slope[planes + 1] = above_ref[2]

    def mix(source, tap):
        totals = [None] * G
        for k in range(3):
            for b in range(G):
                value = source(k, b)
                for a in range(G):
                    part = value * tap(k, a, b)
                    totals[a] = part if totals[a] is None else totals[a] + part
        return totals

    def forward_planes(index, carry):
        plane = 2 * index
        pres = mix(
            lambda k, g: cost[pl.ds(plane + k, 2), :, pl.ds(g * SUB, SUB), :],
            lambda k, o, g: taps_ref[k, o, g],
        )
        for o in range(G):
            pre = pres[o]
            rows = pl.ds(o * SUB, SUB)
            sig = jax.nn.sigmoid(pre)
            both = pl.ds(plane, 2)
            slope[both, :, rows, :] = slope[both, :, rows, :] * (sig * (1.0 + pre * (1.0 - sig)))
            smooth[both, :, rows, :] = pre * sig
        return carry

    lax.fori_loop(0, (planes + 2) // 2, forward_planes, 0)

    def backward_planes(index, carry):
        plane = 2 * index
        grads = mix(
            lambda k, o: slope[pl.ds(plane + 2 - k, 2), :, pl.ds(o * SUB, SUB), :],
            lambda k, g, o: taps_ref[k, o, g],
        )
        for g in range(G):
            grad_ref[pl.ds(plane, 2), :, pl.ds(g * SUB, SUB), :] = grads[g]
        for view in range(local_views):
            for tile in range(pixels // LANE):
                first = (tile % 2) * local_views + view
                for i in range(2):
                    regular_ref[view, plane + i, :, pl.ds(tile * LANE, LANE)] = smooth[
                        plane + i + 1, tile // 2, pl.ds(first, groups, stride=SUB), :
                    ].astype(jnp.bfloat16)
        return carry

    lax.fori_loop(0, planes // 2, backward_planes, 0)


def backward_kernel(src_ref, place_ref, taps_ref, gates_ref, refx_ref, w_ref, *rest):
    halo_refs = rest[:6]
    inner_saved = (rest[6:10], rest[10:14])
    edge_saved = (rest[14:18], rest[18:22])
    regular_ref, keep_ref, send_ref = rest[22:25]
    cost, grad_ref, slope, smooth, rows_lo, rows_hi, acc, dref, logit, held, sems, dense = rest[25:]
    step = pl.program_id(0)
    count = pl.num_programs(0) - 1
    pairs = logit.shape[0]
    tiles = pairs // SUB
    lane_tiles = dref.shape[0]
    local_views = src_ref.shape[0]
    channels = G * GC
    half_rows = rows_lo.shape[0]
    low = low_half()
    inner_count = count - 4

    def plane_of(index):
        return jnp.where(index < inner_count, index + 2, edge_plane(count, index - inner_count))

    plane = plane_of(step)
    slot = lax.rem(step, 3)
    slot_before = lax.rem(step + 2, 3)

    def vector(saved, tile, upper, target, tick):
        warped_ref, corr_ref, sig_ref, rden_ref = saved[tile // 2]
        lanes = pl.ds((tile % 2) * LANE, LANE)
        full = pl.ds(tile * LANE, LANE)
        pack = tile // 2
        half = tile % 2
        rden = rden_ref[0, :, lanes]
        sig = sig_ref[0, :, lanes].reshape(tiles, SUB, LANE)
        wanted = range(G // 2, G) if upper else range(G)
        num_grads = {}
        for g in wanted:
            grad = grad_ref[plane, pack, pl.ds(g * SUB, SUB), :]
            num_grads[g] = spread(grad, half, low) * rden
        if upper:
            logit_grad = logit[:, full].reshape(tiles, SUB, LANE)
        else:
            mixed = None
            for g in range(G):
                rows = pl.ds(g * SUB, SUB)
                part = grad_ref[plane, pack, rows, :] * cost[plane + 2, pack, rows, :]
                mixed = part if mixed is None else mixed + part
            vis_grad = -(spread(mixed, half, low) * rden)[None]
            for g in range(0, G, 2):
                corr = (
                    corr_ref[0, pl.ds(g * pairs, 2 * pairs), lanes]
                    .astype(jnp.float32)
                    .reshape(2, tiles, SUB, LANE)
                )
                vis_grad = vis_grad + num_grads[g][None] * corr[0]
                vis_grad = vis_grad + num_grads[g + 1][None] * corr[1]
            logit_grad = vis_grad * (sig * (1.0 - sig)) * (1.0 / GC)
            logit[:, full] = logit_grad.reshape(pairs, LANE)
        visible = (0.5 + sig) * (1.0 / GC)
        base = G // 2 if upper else 0
        for g in range(base, base + G // 2):
            tick()
            corr_grad = visible * num_grads[g][None] + logit_grad * gates_ref[g][None]
            for j in range(0, GC, 2):
                c = g * GC + j
                local = (c - base * GC) * pairs
                both = jnp.concatenate(
                    [
                        (corr_grad * refx_ref[tile, pl.ds((c + i) * SUB, SUB), :][None]).reshape(
                            pairs, LANE
                        )
                        for i in range(2)
                    ],
                    axis=0,
                )
                target[pl.ds(local, 2 * pairs), full] = both.astype(jnp.bfloat16)
                warped = (
                    warped_ref[0, pl.ds(c * pairs, 2 * pairs), lanes]
                    .astype(jnp.float32)
                    .reshape(2, tiles, SUB, LANE)
                )
                for i in range(2):
                    dref[tile, pl.ds((c + i) * SUB, SUB), :] += jnp.sum(
                        corr_grad * warped[i], axis=0
                    )

    def matmul(rows, where, base, index, part):
        size = half_rows // BACK_PARTS
        product = jnp.dot(
            rows[pl.ds(part * size, size), :],
            held[where, :, pl.ds(index * 2 * LANE, 2 * LANE)],
            preferred_element_type=jnp.float32,
        )
        for half in range(2):
            acc[2 * index + half, pl.ds(base + part * size, size), :] += product[
                :, half * LANE : (half + 1) * LANE
            ]

    def matmuls(rows, where, base):
        return [
            functools.partial(matmul, rows, where, base, index, part)
            for index in range(lane_tiles // 2)
            for part in range(BACK_PARTS)
        ]

    def one_plane(saved):
        weight_copy(w_ref, held, sems, plane, slot).wait()
        tick = ticker(matmuls(rows_hi, slot_before, half_rows), lane_tiles * G // 2)
        for tile in range(lane_tiles):
            vector(saved, tile, False, rows_lo, tick)
        tick = ticker(matmuls(rows_lo, slot, 0), lane_tiles * G // 2)
        for tile in range(lane_tiles):
            vector(saved, tile, True, rows_hi, tick)

    @pl.when(step == 0)
    def _():
        weight_copy(w_ref, held, sems, plane_of(0), 0).start()
        acc[...] = jnp.zeros_like(acc)
        dref[...] = jnp.zeros_like(dref)
        rows_hi[...] = jnp.zeros_like(rows_hi)
        held[2] = jnp.zeros_like(held[2])
        depth_conv(taps_ref, *halo_refs, regular_ref, cost, grad_ref, slope, smooth)

    @pl.when(step + 1 < count)
    def _():
        weight_copy(w_ref, held, sems, plane_of(step + 1), lax.rem(step + 1, 3)).start()

    @pl.when(step < inner_count)
    def _():
        one_plane(inner_saved)

    @pl.when((step >= inner_count) & (step < count))
    def _():
        one_plane(edge_saved)

    @pl.when(step == count)
    def _():
        for thunk in matmuls(rows_hi, slot_before, half_rows):
            thunk()
        own_index = place_ref[0]
        parity = place_ref[1]
        dense[...] = jnp.zeros_like(dense)
        for tile in range(lane_tiles):
            lanes = pl.ds(tile * LANE, LANE)
            for view in range(local_views):
                total = dref[tile, pl.ds(view, channels, stride=SUB), :]
                for copy in range(1, SUB // local_views):
                    first = copy * local_views + view
                    total = total + dref[tile, pl.ds(first, channels, stride=SUB), :]
                dense[view, :, lanes] = total
        for pair in range(pairs):
            view = src_ref[pair % local_views, pair // local_views]
            slot = position(view, own_index, local_views, dense.shape[0] // local_views)
            for tile in range(lane_tiles):
                dense[slot, :, pl.ds(tile * LANE, LANE)] += acc[
                    tile, pl.ds(pair, channels, stride=pairs), :
                ]
        blocks = keep_ref.shape[1] // SUB

        def one_view(view, carry):
            kept = []
            sent = []
            for block in range(blocks):
                mine = pl.multiple_of((2 * block + parity) * SUB, SUB)
                theirs = pl.multiple_of((2 * block + 1 - parity) * SUB, SUB)
                kept.append(dense[view, pl.ds(mine, SUB), :])
                sent.append(dense[view, pl.ds(theirs, SUB), :])
            keep_ref[view] = jnp.concatenate(kept, axis=0)
            send_ref[view] = jnp.concatenate(sent, axis=0).astype(jnp.bfloat16)
            return carry

        lax.fori_loop(0, dense.shape[0], one_view, 0)


def split_kernel(first, keep_ref, received_ref, after_ref, even_ref, send_ref):
    count = even_ref.shape[0]
    half = keep_ref.shape[0] // 2
    for out_ref, start in ((even_ref, first), (send_ref, half + first)):
        span = pl.ds(start, count)
        out_ref[...] = (keep_ref[span] + received_ref[span].astype(jnp.float32)).astype(
            out_ref.dtype
        )


def spread_kernel(even_ref, received_ref, *out_refs):
    size = out_refs[0].shape[0]
    for index, out_ref in enumerate(out_refs):
        span = pl.ds(index * size, size)
        out_ref[...] = (even_ref[span] + received_ref[span].astype(jnp.float32)).astype(
            out_ref.dtype
        )


def per_plane(shape, plane):
    rank = len(shape)
    return pl.BlockSpec((1,) + tuple(shape[1:]), lambda d: (plane(d),) + (0,) * (rank - 1))


def fixed(shape):
    rank = len(shape)
    return pl.BlockSpec(tuple(shape), lambda d: (0,) * rank, pipeline_mode=pl.Buffered(1))


SMEM = functools.partial(pl.BlockSpec, memory_space=pltpu.SMEM)


def shards(features, sources, warp_weights, view_gate, depth_kernel, cotangent):
    view_count = lax.axis_size("view")
    plane_count = lax.axis_size("plane")
    own_index = lax.axis_index("view")
    plane_index = lax.axis_index("plane")
    local_views, channels, pixels = features.shape
    all_views, per_view = sources.shape
    pairs = local_views * per_view
    planes = warp_weights.shape[0]
    share = channels // plane_count
    blocks = plane_count // 2
    parity = plane_index % 2
    f32 = jnp.float32
    bf16 = jnp.bfloat16
    near = [(i, i ^ 1) for i in range(plane_count)]
    far = [(i, i ^ 2) for i in range(plane_count)]
    up = [(i, i + 1) for i in range(plane_count - 1)]
    down = [(i + 1, i) for i in range(plane_count - 1)]
    shape = jax.ShapeDtypeStruct

    halves = features.reshape(local_views, blocks, 2, share, pixels)
    mine = lax.dynamic_index_in_dim(halves, parity, 2, keepdims=False).reshape(
        local_views, channels // 2, pixels
    )

    def over_view(array, k):
        return lax.ppermute(array, "view", [(i, i ^ k) for i in range(view_count)])

    quarter = max(view_count // 4, 1)
    even = [mine] + [over_view(mine, k) for k in range(2, view_count, 2)]
    near_even = jnp.concatenate(even[:quarter], axis=0)
    far_even = jnp.concatenate(even[quarter:], axis=0)
    packed = (pixels // (2 * LANE), G * SUB, LANE)
    hbm = pl.BlockSpec(memory_space=pltpu.HBM)
    anywhere = pl.BlockSpec(memory_space=pl.ANY)
    weights = pltpu.with_memory_space_constraint(warp_weights, pltpu.HBM)
    refx, gates, cot = pl.pallas_call(
        prep_kernel,
        out_shape=(
            shape((pixels // LANE, channels * SUB, LANE), f32),
            shape((G, SUB, LANE), f32),
            shape((planes,) + packed, f32),
        ),
        in_specs=[SMEM(), hbm, hbm],
        scratch_shapes=[
            pltpu.VMEM(features.shape, bf16),
            pltpu.VMEM(cotangent.shape, bf16),
            pltpu.SemaphoreType.DMA((2,)),
        ],
        compiler_params=params(),
        cost_estimate=pl.CostEstimate(flops=10**9, bytes_accessed=4 * MIB, transcendentals=0),
        name="prep",
    )(
        pltpu.with_memory_space_constraint(view_gate, pltpu.HBM),
        pltpu.with_memory_space_constraint(features, pltpu.HBM),
        pltpu.with_memory_space_constraint(cotangent, pltpu.HBM),
    )
    far_even, refx, gates, cot = lax.optimization_barrier((far_even, refx, gates, cot))
    maps = [near_even, far_even, over_view(near_even, 1), over_view(far_even, 1)]
    maps = maps + [lax.ppermute(part, "plane", near) for part in maps]

    src_own = lax.dynamic_slice_in_dim(sources, own_index * local_views, local_views, 0)
    place = jnp.stack([own_index, parity]).astype(jnp.int32)
    rows = pl.pallas_call(
        assemble_kernel,
        out_shape=shape((channels * pairs, pixels), bf16),
        in_specs=[SMEM(), SMEM()] + [pl.BlockSpec()] * len(maps),
        scratch_shapes=[
            pltpu.VMEM((2, all_views, channels // 2, pixels), bf16),
            pltpu.VMEM((pixels // LANE, channels * pairs, LANE), f32),
        ],
        compiler_params=params(24),
        name="assemble",
    )(src_own, place, *maps)

    width = 2 * LANE

    def saved_shapes(count):
        one = (
            pltpu.VMEM((count, channels * pairs, width), bf16),
            pltpu.VMEM((count, G * pairs, width), bf16),
            pltpu.VMEM((count, pairs, width), f32),
            pltpu.VMEM((count, SUB, width), f32),
        )
        return one * 2

    def saved_specs(count):
        specs = []
        for index, item in enumerate(saved_shapes(count)):
            if index < 4:
                specs.append(per_plane(item.shape, lambda d: jnp.minimum(d, count - 1)))
            else:
                specs.append(per_plane(item.shape, lambda d: jnp.maximum(d - 1, 0)))
        return specs

    fixed_specs = [fixed(gates.shape), fixed(rows.shape), fixed(refx.shape), hbm]
    scratch = [
        pltpu.VMEM((2, pixels, pixels), bf16),
        pltpu.SemaphoreType.DMA((2,)),
        pltpu.VMEM((G * pairs, LANE), f32),
        pltpu.VMEM((channels * pairs, width), f32),
        pltpu.VMEM((channels * pairs, width), f32),
    ]
    inner_count = planes - 4
    load = (3,) + packed
    *edge_saved, up_load, down_load = pl.pallas_call(
        edge_kernel,
        out_shape=saved_shapes(4) + (shape(load, f32),) * 2,
        grid=(5,),
        in_specs=fixed_specs + [fixed(cot.shape)],
        out_specs=tuple(saved_specs(4)) + (fixed(load),) * 2,
        scratch_shapes=[pltpu.VMEM((4,) + packed, f32)] + scratch,
        compiler_params=params(11),
        name="forward_edge",
    )(gates, rows, refx, weights, cot)
    below = lax.ppermute(up_load, "plane", up)
    above = lax.ppermute(down_load, "plane", down)
    *inner_saved, inner_cost = pl.pallas_call(
        inner_kernel,
        out_shape=saved_shapes(inner_count) + (shape((inner_count,) + packed, f32),),
        grid=(inner_count + 1,),
        in_specs=fixed_specs,
        out_specs=tuple(saved_specs(inner_count)) + (fixed((inner_count,) + packed),),
        scratch_shapes=scratch,
        compiler_params=params(11),
        cost_estimate=pl.CostEstimate(
            flops=2 * channels * pairs * pixels * pixels * inner_count,
            bytes_accessed=40 * MIB,
            transcendentals=0,
        ),
        name="forward_inner",
    )(gates, rows, refx, weights)

    halo = (below, down_load, inner_cost, up_load, above, cot)
    inner_saved, edge_saved = [
        [pltpu.with_memory_space_constraint(item, pltpu.VMEM) for item in group]
        for group in (inner_saved, edge_saved)
    ]
    returned = (all_views, channels // 2, pixels)
    regular, keep, send = pl.pallas_call(
        backward_kernel,
        out_shape=(shape(cotangent.shape, bf16), shape(returned, f32), shape(returned, bf16)),
        grid=(planes + 1,),
        in_specs=[SMEM()] * 3
        + [fixed(gates.shape), fixed(refx.shape), hbm]
        + [fixed(item.shape) for item in halo]
        + [
            per_plane(item.shape, lambda d: jnp.minimum(d, inner_count - 1))
            for item in inner_saved
        ]
        + [
            per_plane(item.shape, lambda d: jnp.clip(d - inner_count, 0, 3))
            for item in edge_saved
        ],
        out_specs=(fixed(cotangent.shape), fixed(returned), fixed(returned)),
        scratch_shapes=[
            pltpu.VMEM((planes + 4,) + packed, f32),
            pltpu.VMEM((planes,) + packed, f32),
            pltpu.VMEM((planes + 2,) + packed, f32),
            pltpu.VMEM((planes + 2,) + packed, f32),
            pltpu.VMEM((channels * pairs // 2, pixels), bf16),
            pltpu.VMEM((channels * pairs // 2, pixels), bf16),
            pltpu.VMEM((pixels // LANE, channels * pairs, LANE), f32),
            pltpu.VMEM((pixels // LANE, channels * SUB, LANE), f32),
            pltpu.VMEM((pairs, pixels), f32),
            pltpu.VMEM((3, pixels, pixels), bf16),
            pltpu.SemaphoreType.DMA((3,)),
            pltpu.VMEM((all_views, channels, pixels), f32),
        ],
        compiler_params=params(12 + 14 * all_views * channels * pixels // MIB),
        name="backward",
    )(
        src_own,
        place,
        depth_kernel,
        gates,
        refx,
        weights,
        *halo,
        *inner_saved,
        *edge_saved,
    )

    received = lax.ppermute(send, "plane", near)
    close = quarter * local_views
    piece = (local_views, channels // 2, pixels)

    def stage(first, count, after, kind):
        even_sum, outgoing = pl.pallas_call(
            functools.partial(split_kernel, first),
            out_shape=(shape((count,) + piece[1:], f32), shape((count,) + piece[1:], bf16)),
            in_specs=[pl.BlockSpec(), pl.BlockSpec(), anywhere],
            compiler_params=params(32),
            name="split",
        )(keep, received, after)
        incoming = over_view(outgoing, 1)
        return pl.pallas_call(
            spread_kernel,
            out_shape=(shape(piece, kind),) + (shape(piece, bf16),) * (count // local_views - 1),
            compiler_params=params(32),
            name="spread",
        )(even_sum, incoming)

    away_parts = stage(close, all_views // 2 - close, received, bf16)
    total, *close_parts = stage(0, close, away_parts[0], f32)
    for index, part in enumerate(away_parts):
        total = total + over_view(part, 2 * (quarter + index)).astype(f32)
    for index, part in enumerate(close_parts):
        total = total + over_view(part, 2 * (index + 1)).astype(f32)
    rounded = total.astype(bf16)
    total = rounded.astype(f32) + lax.ppermute(rounded, "plane", far).astype(f32)
    other = lax.ppermute(total, "plane", near)
    cut = (local_views, blocks, 1, share, pixels)
    first = jnp.where(parity == 0, total, other).reshape(cut)
    second = jnp.where(parity == 0, other, total).reshape(cut)
    feature_grads = jnp.concatenate([first, second], axis=2).reshape(features.shape)
    return (regular, feature_grads)


def solution(mesh):
    in_specs = (
        P("view", None, None),
        P(),
        P("plane", None, None),
        P(),
        P(),
        P("view", "plane", None, None),
    )
    out_specs = (P("view", "plane", None, None), P("view", None, None))
    return jax.shard_map(shards, mesh=mesh, in_specs=in_specs, out_specs=out_specs, check_vma=False)
```

```python
import functools

import jax
import jax.numpy as jnp
from jax import lax
from jax.experimental import pallas as pl
from jax.experimental.pallas import tpu as pltpu
from jax.sharding import PartitionSpec as P

G = 8
GC = 4
SUB = 8
LANE = 128
MIB = 1024 * 1024
NT = (((1,), (1,)), ((), ()))


def params(mib=16):
    return pltpu.CompilerParams(vmem_limit_bytes=mib * MIB)


def low_half():
    return lax.broadcasted_iota(jnp.int32, (SUB, LANE), 0) < SUB // 2


def swap_halves(tile):
    return pltpu.roll(tile, SUB // 2, 0)


def spread(tile, half, low):
    other = swap_halves(tile)
    return jnp.where(low, tile, other) if half == 0 else jnp.where(low, other, tile)


def pack_planes(array_ref, plane, out_ref, slot):
    local_views, _, groups, pixels = array_ref.shape
    for view in range(local_views):
        for tile in range(pixels // LANE):
            first = (tile % 2) * local_views + view
            out_ref[slot, tile // 2, pl.ds(first, groups, stride=SUB), :] = array_ref[
                view, plane, :, pl.ds(tile * LANE, LANE)
            ].astype(jnp.float32)


def prep_kernel(
    gate_ref, own_hbm, cot_hbm, refx_ref, gates_ref, cot_out, own_ref, cot_ref, sems
):
    copies = [
        pltpu.make_async_copy(own_hbm, own_ref, sems.at[0]),
        pltpu.make_async_copy(cot_hbm, cot_ref, sems.at[1]),
    ]
    for copy in copies:
        copy.start()
    for copy in copies:
        copy.wait()
    local_views, channels, pixels = own_ref.shape
    for tile in range(pixels // LANE):
        for view in range(local_views):
            own = own_ref[view, :, pl.ds(tile * LANE, LANE)].astype(jnp.float32)
            for copied in range(SUB // local_views):
                first = copied * local_views + view
                refx_ref[tile, pl.ds(first, channels, stride=SUB), :] = own
    for g in range(gates_ref.shape[0]):
        gates_ref[g] = jnp.full((SUB, LANE), gate_ref[g], jnp.float32)

    def pack_one(plane, carry):
        pack_planes(cot_ref, plane, cot_out, plane)
        return carry

    lax.fori_loop(0, cot_out.shape[0], pack_one, 0)


def position(view, own_index, local_views, view_count):
    distance = (view // local_views) ^ own_index
    place = distance // 2 + (distance % 2) * (view_count // 2)
    return place * local_views + view % local_views


def assemble_kernel(src_ref, place_ref, *rest):
    *map_refs, rows_ref, maps, scratch = rest
    local_views, per_view = src_ref.shape
    tiles = scratch.shape[0]
    pairs = local_views * per_view
    view_count = maps.shape[1] // local_views
    blocks = maps.shape[2] // SUB
    own_index = place_ref[0]
    parity = place_ref[1]
    half = len(map_refs) // 2
    for side in range(2):
        first = 0
        for ref in map_refs[side * half : (side + 1) * half]:
            maps[side, first : first + ref.shape[0]] = ref[...]
            first += ref.shape[0]
    for pair in range(pairs):
        view = src_ref[pair % local_views, pair // local_views]
        slot = position(view, own_index, local_views, view_count)
        for tile in range(tiles):
            for side in range(2):
                values = maps[side, slot, :, pl.ds(tile * LANE, LANE)].astype(jnp.float32)
                held = parity if side == 0 else 1 - parity
                for block in range(blocks):
                    first = (2 * block + held) * (SUB * pairs) + pair
                    scratch[tile, pl.ds(first, SUB, stride=pairs), :] = values[
                        block * SUB : (block + 1) * SUB
                    ]
    for tile in range(tiles):
        rows_ref[:, pl.ds(tile * LANE, LANE)] = scratch[tile].astype(jnp.bfloat16)


def forward_vector(gates_ref, refx_ref, chunk, tile, plane, saved):
    warped_ref, corr_ref, sig_ref, rden_ref = saved
    pairs = sig_ref.shape[1]
    tiles = pairs // SUB
    inner = pl.ds((tile % 2) * LANE, LANE)
    lanes = pl.ds(tile * LANE, LANE)
    logits = None
    for g in range(G):
        total = None
        for j in range(0, GC, 2):
            c = g * GC + j
            span = pl.ds(c * pairs, 2 * pairs)
            both = chunk[span, inner]
            warped_ref[plane, span, lanes] = both.astype(jnp.bfloat16)
            both = both.reshape(2, tiles, SUB, LANE)
            for i in range(2):
                part = both[i] * refx_ref[tile, pl.ds((c + i) * SUB, SUB), :][None]
                total = part if total is None else total + part
        corr = total * (1.0 / GC)
        corr_ref[plane, pl.ds(g * pairs, pairs), lanes] = corr.reshape(pairs, LANE)
        part = corr * gates_ref[g][None]
        logits = part if logits is None else logits + part
    sig = jax.nn.sigmoid(logits)
    sig_ref[plane, :, lanes] = sig.reshape(pairs, LANE)
    visible = 0.5 + sig
    den = jnp.sum(visible, axis=0)
    rden = 1.0 / (den + swap_halves(den))
    rden_ref[plane, :, lanes] = rden
    costs = []
    for g in range(G):
        corr = corr_ref[plane, pl.ds(g * pairs, pairs), lanes].reshape(tiles, SUB, LANE)
        num = jnp.sum(visible * corr, axis=0)
        costs.append((num + swap_halves(num)) * rden)
    return costs


def weight_copy(w_ref, held, sems, plane, slot):
    return pltpu.make_async_copy(w_ref.at[plane], held.at[slot], sems.at[slot])


def forward_body(count, plane_of, gates_ref, rows_ref, refx_ref, w_ref, saved, cost_ref, scratch):
    held, sems, *chunks = scratch
    low = low_half()

    def matmul(index, slot):
        chunks[index][...] = lax.dot_general(
            rows_ref[...],
            held[slot, pl.ds(index * 2 * LANE, 2 * LANE), :],
            NT,
            preferred_element_type=jnp.float32,
        )

    def vector(index, at):
        costs = [
            forward_vector(
                gates_ref, refx_ref, chunks[index], 2 * index + half, plane_of(at), saved
            )
            for half in range(2)
        ]
        for g in range(G):
            cost_ref[at, index, pl.ds(g * SUB, SUB), :] = jnp.where(low, costs[0][g], costs[1][g])

    weight_copy(w_ref, held, sems, plane_of(0), 0).start()

    def one(step, carry):
        slot = lax.rem(step, 2)

        @pl.when(step + 1 < count)
        def _():
            weight_copy(w_ref, held, sems, plane_of(step + 1), 1 - slot).start()

        weight_copy(w_ref, held, sems, plane_of(step), slot).wait()
        matmul(0, slot)
        vector(1, jnp.maximum(step - 1, 0))
        matmul(1, slot)
        vector(0, step)
        return carry

    lax.fori_loop(0, count, one, 0)
    vector(1, count - 1)


def edge_plane(planes, index):
    return jnp.where(index < 2, index, planes - 4 + index)


def edge_kernel(gates_ref, rows_ref, refx_ref, w_ref, cot_ref, *rest):
    up_ref, down_ref, cost, *scratch = rest[4:]
    planes = w_ref.shape[0]
    forward_body(
        4,
        functools.partial(edge_plane, planes),
        gates_ref,
        rows_ref,
        refx_ref,
        w_ref,
        rest[:4],
        cost,
        scratch,
    )
    down_ref[0:2] = cost[0:2]
    up_ref[0:2] = cost[2:4]
    down_ref[2] = cot_ref[0]
    up_ref[2] = cot_ref[planes - 1]


def inner_kernel(gates_ref, rows_ref, refx_ref, w_ref, *rest):
    cost_ref, *scratch = rest[8:]
    forward_body(
        cost_ref.shape[0],
        lambda index: index + 2,
        gates_ref,
        rows_ref,
        refx_ref,
        w_ref,
        rest[4:8],
        cost_ref,
        scratch,
    )


def depth_conv(
    taps_ref,
    below_ref,
    down_ref,
    inner_ref,
    up_ref,
    above_ref,
    cot_ref,
    regular_ref,
    cost,
    grad_ref,
    slope,
    smooth,
):
    planes = grad_ref.shape[0]
    local_views, _, groups, pixels = regular_ref.shape
    cost[0:2] = below_ref[0:2]
    cost[2:4] = down_ref[0:2]
    cost[4:planes] = inner_ref[...]
    cost[planes : planes + 2] = up_ref[0:2]
    cost[planes + 2 : planes + 4] = above_ref[0:2]
    slope[0] = below_ref[2]
    slope[1 : planes + 1] = cot_ref[...]
    slope[planes + 1] = above_ref[2]

    def mix(source, tap):
        totals = [None] * G
        for k in range(3):
            for b in range(G):
                value = source(k, b)
                for a in range(G):
                    part = value * tap(k, a, b)
                    totals[a] = part if totals[a] is None else totals[a] + part
        return totals

    def forward_planes(index, carry):
        plane = 2 * index
        pres = mix(
            lambda k, g: cost[pl.ds(plane + k, 2), :, pl.ds(g * SUB, SUB), :],
            lambda k, o, g: taps_ref[k, o, g],
        )
        for o in range(G):
            pre = pres[o]
            rows = pl.ds(o * SUB, SUB)
            sig = jax.nn.sigmoid(pre)
            both = pl.ds(plane, 2)
            slope[both, :, rows, :] = slope[both, :, rows, :] * (sig * (1.0 + pre * (1.0 - sig)))
            smooth[both, :, rows, :] = pre * sig
        return carry

    lax.fori_loop(0, (planes + 2) // 2, forward_planes, 0)

    def backward_planes(index, carry):
        plane = 2 * index
        grads = mix(
            lambda k, o: slope[pl.ds(plane + 2 - k, 2), :, pl.ds(o * SUB, SUB), :],
            lambda k, g, o: taps_ref[k, o, g],
        )
        for g in range(G):
            grad_ref[pl.ds(plane, 2), :, pl.ds(g * SUB, SUB), :] = grads[g]
        for view in range(local_views):
            for tile in range(pixels // LANE):
                first = (tile % 2) * local_views + view
                for i in range(2):
                    regular_ref[view, plane + i, :, pl.ds(tile * LANE, LANE)] = smooth[
                        plane + i + 1, tile // 2, pl.ds(first, groups, stride=SUB), :
                    ].astype(jnp.bfloat16)
        return carry

    lax.fori_loop(0, planes // 2, backward_planes, 0)


def backward_kernel(src_ref, place_ref, taps_ref, gates_ref, refx_ref, w_ref, *rest):
    halo_refs = rest[:6]
    warped_ref, corr_ref, sig_ref, rden_ref = rest[6:10]
    regular_ref, keep_ref, send_ref = rest[10:13]
    cost, grad_ref, slope, smooth, rows_a, rows_b, acc, dref, held, sems, dense = rest[13:]
    count = w_ref.shape[0]
    pairs = sig_ref.shape[1]
    tiles = pairs // SUB
    lane_tiles = dref.shape[0]
    local_views = src_ref.shape[0]
    channels = G * GC
    low = low_half()

    def vector(plane, tile, target):
        lanes = pl.ds(tile * LANE, LANE)
        pack = tile // 2
        half = tile % 2
        rden = rden_ref[plane, :, lanes]
        sig = sig_ref[plane, :, lanes].reshape(tiles, SUB, LANE)
        num_grads = []
        mixed = None
        for g in range(G):
            rows = pl.ds(g * SUB, SUB)
            grad = grad_ref[plane, pack, rows, :]
            num_grads.append(spread(grad, half, low) * rden)
            part = grad * cost[plane + 2, pack, rows, :]
            mixed = part if mixed is None else mixed + part
        vis_grad = -(spread(mixed, half, low) * rden)[None]
        for g in range(G):
            corr = corr_ref[plane, pl.ds(g * pairs, pairs), lanes].reshape(tiles, SUB, LANE)
            vis_grad = vis_grad + num_grads[g][None] * corr
        logit_grad = vis_grad * (sig * (1.0 - sig)) * (1.0 / GC)
        visible = (0.5 + sig) * (1.0 / GC)
        for g in range(G):
            corr_grad = visible * num_grads[g][None] + logit_grad * gates_ref[g][None]
            for j in range(0, GC, 2):
                c = g * GC + j
                span = pl.ds(c * pairs, 2 * pairs)
                both = jnp.concatenate(
                    [
                        (corr_grad * refx_ref[tile, pl.ds((c + i) * SUB, SUB), :][None]).reshape(
                            pairs, LANE
                        )
                        for i in range(2)
                    ],
                    axis=0,
                )
                target[span, lanes] = both.astype(jnp.bfloat16)
                warped = (
                    warped_ref[plane, span, lanes]
                    .astype(jnp.float32)
                    .reshape(2, tiles, SUB, LANE)
                )
                for i in range(2):
                    dref[tile, pl.ds((c + i) * SUB, SUB), :] += jnp.sum(
                        corr_grad * warped[i], axis=0
                    )

    def matmul(rows, slot, index):
        product = jnp.dot(
            rows[...],
            held[slot, :, pl.ds(index * 2 * LANE, 2 * LANE)],
            preferred_element_type=jnp.float32,
        )
        for half in range(2):
            acc[2 * index + half] += product[:, half * LANE : (half + 1) * LANE]

    def fetch(plane):
        return weight_copy(w_ref, held, sems, plane, lax.rem(plane, 4))

    fetch(0).start()
    fetch(1).start()
    acc[...] = jnp.zeros_like(acc)
    dref[...] = jnp.zeros_like(dref)
    rows_b[...] = jnp.zeros_like(rows_b)
    held[3] = jnp.zeros_like(held[3])
    depth_conv(taps_ref, *halo_refs, regular_ref, cost, grad_ref, slope, smooth)

    def two_planes(turn, carry):
        first = 2 * turn
        for offset, rows, before in ((0, rows_a, rows_b), (1, rows_b, rows_a)):
            plane = first + offset
            fetch(plane).wait()

            @pl.when(plane + 2 < count)
            def _():
                fetch(plane + 2).start()

            slot = lax.rem(plane + 3, 4)
            for tile in range(lane_tiles):
                if tile % 2 == 0:
                    matmul(before, slot, tile // 2)
                vector(plane, tile, rows)
        return carry

    lax.fori_loop(0, count // 2, two_planes, 0)
    for index in range(lane_tiles // 2):
        matmul(rows_b, (count - 1) % 4, index)
    own_index = place_ref[0]
    parity = place_ref[1]
    blocks = keep_ref.shape[1] // SUB
    for target, held_side in ((dense, 1 - parity), (keep_ref, parity)):
        target[...] = jnp.zeros_like(target)
        for tile in range(lane_tiles):
            lanes = pl.ds(tile * LANE, LANE)
            for block in range(blocks):
                channel = (2 * block + held_side) * SUB
                part = pl.ds(block * SUB, SUB)
                for view in range(local_views):
                    total = None
                    for copy in range(SUB // local_views):
                        first = channel * SUB + copy * local_views + view
                        value = dref[tile, pl.ds(first, SUB, stride=SUB), :]
                        total = value if total is None else total + value
                    target[view, part, lanes] = total
        for pair in range(pairs):
            view = src_ref[pair % local_views, pair // local_views]
            slot = position(view, own_index, local_views, dense.shape[0] // local_views)
            for block in range(blocks):
                first = (2 * block + held_side) * (SUB * pairs) + pair
                part = pl.ds(block * SUB, SUB)
                for tile in range(lane_tiles):
                    target[slot, part, pl.ds(tile * LANE, LANE)] += acc[
                        tile, pl.ds(first, SUB, stride=pairs), :
                    ]
    send_ref[...] = dense[...].astype(jnp.bfloat16)


def split_kernel(first, keep_ref, received_ref, after_ref, even_ref, send_ref):
    count = even_ref.shape[0]
    half = keep_ref.shape[0] // 2
    for out_ref, start in ((even_ref, first), (send_ref, half + first)):
        span = pl.ds(start, count)
        out_ref[...] = (keep_ref[span] + received_ref[span].astype(jnp.float32)).astype(
            out_ref.dtype
        )


def spread_kernel(even_ref, received_ref, *out_refs):
    size = out_refs[0].shape[0]
    for index, out_ref in enumerate(out_refs):
        span = pl.ds(index * size, size)
        out_ref[...] = (even_ref[span] + received_ref[span].astype(jnp.float32)).astype(
            out_ref.dtype
        )


SMEM = functools.partial(pl.BlockSpec, memory_space=pltpu.SMEM)


def shards(features, sources, warp_weights, view_gate, depth_kernel, cotangent):
    view_count = lax.axis_size("view")
    plane_count = lax.axis_size("plane")
    own_index = lax.axis_index("view")
    plane_index = lax.axis_index("plane")
    local_views, channels, pixels = features.shape
    all_views, per_view = sources.shape
    pairs = local_views * per_view
    planes = warp_weights.shape[0]
    share = channels // plane_count
    blocks = plane_count // 2
    parity = plane_index % 2
    f32 = jnp.float32
    bf16 = jnp.bfloat16
    near = [(i, i ^ 1) for i in range(plane_count)]
    far = [(i, i ^ 2) for i in range(plane_count)]
    up = [(i, i + 1) for i in range(plane_count - 1)]
    down = [(i + 1, i) for i in range(plane_count - 1)]
    shape = jax.ShapeDtypeStruct

    halves = features.reshape(local_views, blocks, 2, share, pixels)
    mine = lax.dynamic_index_in_dim(halves, parity, 2, keepdims=False).reshape(
        local_views, channels // 2, pixels
    )

    def over_view(array, k):
        return lax.ppermute(array, "view", [(i, i ^ k) for i in range(view_count)])

    quarter = max(view_count // 4, 1)
    even = [mine] + [over_view(mine, k) for k in range(2, view_count, 2)]
    near_even = jnp.concatenate(even[:quarter], axis=0)
    far_even = jnp.concatenate(even[quarter:], axis=0)
    packed = (pixels // (2 * LANE), G * SUB, LANE)
    hbm = pl.BlockSpec(memory_space=pltpu.HBM)
    anywhere = pl.BlockSpec(memory_space=pl.ANY)
    weights = pltpu.with_memory_space_constraint(warp_weights, pltpu.HBM)
    refx, gates, cot = pl.pallas_call(
        prep_kernel,
        out_shape=(
            shape((pixels // LANE, channels * SUB, LANE), f32),
            shape((G, SUB, LANE), f32),
            shape((planes,) + packed, f32),
        ),
        in_specs=[SMEM(), hbm, hbm],
        scratch_shapes=[
            pltpu.VMEM(features.shape, bf16),
            pltpu.VMEM(cotangent.shape, bf16),
            pltpu.SemaphoreType.DMA((2,)),
        ],
        compiler_params=params(),
        cost_estimate=pl.CostEstimate(flops=10**9, bytes_accessed=4 * MIB, transcendentals=0),
        name="prep",
    )(
        pltpu.with_memory_space_constraint(view_gate, pltpu.HBM),
        pltpu.with_memory_space_constraint(features, pltpu.HBM),
        pltpu.with_memory_space_constraint(cotangent, pltpu.HBM),
    )
    far_even, refx, gates, cot = lax.optimization_barrier((far_even, refx, gates, cot))
    maps = [near_even, far_even, over_view(near_even, 1), over_view(far_even, 1)]
    maps = maps + [lax.ppermute(part, "plane", near) for part in maps]

    src_own = lax.dynamic_slice_in_dim(sources, own_index * local_views, local_views, 0)
    place = jnp.stack([own_index, parity]).astype(jnp.int32)
    rows = pl.pallas_call(
        assemble_kernel,
        out_shape=shape((channels * pairs, pixels), bf16),
        in_specs=[SMEM(), SMEM()] + [pl.BlockSpec()] * len(maps),
        scratch_shapes=[
            pltpu.VMEM((2, all_views, channels // 2, pixels), bf16),
            pltpu.VMEM((pixels // LANE, channels * pairs, LANE), f32),
        ],
        compiler_params=params(24),
        name="assemble",
    )(src_own, place, *maps)

    saved = (
        pltpu.VMEM((planes, channels * pairs, pixels), bf16),
        pltpu.VMEM((planes, G * pairs, pixels), f32),
        pltpu.VMEM((planes, pairs, pixels), f32),
        pltpu.VMEM((planes, SUB, pixels), f32),
    )
    on_chip = functools.partial(pltpu.with_memory_space_constraint, memory_space=pltpu.VMEM)
    vmem = pl.BlockSpec(memory_space=pltpu.VMEM)
    scratch = [
        pltpu.VMEM((2, pixels, pixels), bf16),
        pltpu.SemaphoreType.DMA((2,)),
        pltpu.VMEM((channels * pairs, 2 * LANE), f32),
        pltpu.VMEM((channels * pairs, 2 * LANE), f32),
    ]
    load = (3,) + packed
    rows, refx, gates, cot = [on_chip(item) for item in (rows, refx, gates, cot)]
    *edge_saved, up_load, down_load = pl.pallas_call(
        edge_kernel,
        out_shape=saved + (shape(load, f32),) * 2,
        in_specs=[vmem] * 3 + [hbm, vmem],
        out_specs=(vmem,) * 6,
        scratch_shapes=[pltpu.VMEM((4,) + packed, f32)] + scratch,
        compiler_params=params(8),
        name="forward_edge",
    )(gates, rows, refx, weights, cot)
    below = lax.ppermute(up_load, "plane", up)
    above = lax.ppermute(down_load, "plane", down)
    inner_count = planes - 4
    *all_saved, inner_cost = pl.pallas_call(
        inner_kernel,
        out_shape=saved + (pltpu.VMEM((inner_count,) + packed, f32),),
        in_specs=[vmem] * 3 + [hbm] + [anywhere] * 4,
        out_specs=(vmem,) * 5,
        scratch_shapes=scratch,
        input_output_aliases={4 + i: i for i in range(4)},
        compiler_params=params(8),
        cost_estimate=pl.CostEstimate(
            flops=2 * channels * pairs * pixels * pixels * inner_count,
            bytes_accessed=40 * MIB,
            transcendentals=0,
        ),
        name="forward_inner",
    )(gates, rows, refx, weights, *[on_chip(item) for item in edge_saved])

    halo = (below, down_load, inner_cost, up_load, above, cot)
    returned = (all_views, channels // 2, pixels)
    regular, keep, send = pl.pallas_call(
        backward_kernel,
        out_shape=(shape(cotangent.shape, bf16), shape(returned, f32), shape(returned, bf16)),
        in_specs=[SMEM()] * 3 + [vmem, vmem, hbm] + [vmem] * 10,
        out_specs=(vmem,) * 3,
        scratch_shapes=[
            pltpu.VMEM((planes + 4,) + packed, f32),
            pltpu.VMEM((planes,) + packed, f32),
            pltpu.VMEM((planes + 2,) + packed, f32),
            pltpu.VMEM((planes + 2,) + packed, f32),
            pltpu.VMEM((channels * pairs, pixels), bf16),
            pltpu.VMEM((channels * pairs, pixels), bf16),
            pltpu.VMEM((pixels // LANE, channels * pairs, LANE), f32),
            pltpu.VMEM((pixels // LANE, channels * SUB, LANE), f32),
            pltpu.VMEM((4, pixels, pixels), bf16),
            pltpu.SemaphoreType.DMA((4,)),
            pltpu.VMEM(returned, f32),
        ],
        compiler_params=params(14 + 5 * all_views * channels * pixels // MIB),
        name="backward",
    )(
        src_own,
        place,
        pltpu.with_memory_space_constraint(depth_kernel, pltpu.HBM),
        gates,
        refx,
        weights,
        *halo,
        *[on_chip(item) for item in all_saved],
    )

    received = lax.ppermute(send, "plane", near)
    close = quarter * local_views
    piece = (local_views, channels // 2, pixels)

    def stage(first, count, after, kind):
        even_sum, outgoing = pl.pallas_call(
            functools.partial(split_kernel, first),
            out_shape=(shape((count,) + piece[1:], f32), shape((count,) + piece[1:], bf16)),
            in_specs=[pl.BlockSpec(), pl.BlockSpec(), anywhere],
            compiler_params=params(32),
            name="split",
        )(keep, received, after)
        incoming = over_view(outgoing, 1)
        return pl.pallas_call(
            spread_kernel,
            out_shape=(shape(piece, kind),) + (shape(piece, bf16),) * (count // local_views - 1),
            compiler_params=params(32),
            name="spread",
        )(even_sum, incoming)

    away_parts = stage(close, all_views // 2 - close, received, bf16)
    total, *close_parts = stage(0, close, away_parts[0], f32)
    for index, part in enumerate(away_parts):
        total = total + over_view(part, 2 * (quarter + index)).astype(f32)
    for index, part in enumerate(close_parts):
        total = total + over_view(part, 2 * (index + 1)).astype(f32)
    rounded = total.astype(bf16)
    total = rounded.astype(f32) + lax.ppermute(rounded, "plane", far).astype(f32)
    other = lax.ppermute(total, "plane", near)
    cut = (local_views, blocks, 1, share, pixels)
    first = jnp.where(parity == 0, total, other).reshape(cut)
    second = jnp.where(parity == 0, other, total).reshape(cut)
    feature_grads = jnp.concatenate([first, second], axis=2).reshape(features.shape)
    return (regular, feature_grads)


def solution(mesh):
    in_specs = (
        P("view", None, None),
        P(),
        P("plane", None, None),
        P(),
        P(),
        P("view", "plane", None, None),
    )
    out_specs = (P("view", "plane", None, None), P("view", None, None))
    return jax.shard_map(shards, mesh=mesh, in_specs=in_specs, out_specs=out_specs, check_vma=False)
```

```python
import functools

import jax
import jax.numpy as jnp
from jax import lax
from jax.experimental import pallas as pl
from jax.experimental.pallas import tpu as pltpu
from jax.sharding import PartitionSpec as P

G = 8
GC = 4
SUB = 8
LANE = 128
MIB = 1024 * 1024
NT = (((1,), (1,)), ((), ()))


def params(mib=16):
    return pltpu.CompilerParams(vmem_limit_bytes=mib * MIB)


def low_half():
    return lax.broadcasted_iota(jnp.int32, (SUB, LANE), 0) < SUB // 2


def swap_halves(tile):
    return pltpu.roll(tile, SUB // 2, 0)


def spread(tile, half, low):
    other = swap_halves(tile)
    return jnp.where(low, tile, other) if half == 0 else jnp.where(low, other, tile)


def pack_planes(array_ref, plane, out_ref, slot):
    local_views, _, groups, pixels = array_ref.shape
    for view in range(local_views):
        for tile in range(pixels // LANE):
            first = (tile % 2) * local_views + view
            out_ref[slot, tile // 2, pl.ds(first, groups, stride=SUB), :] = array_ref[
                view, plane, :, pl.ds(tile * LANE, LANE)
            ].astype(jnp.float32)


def prep_kernel(
    gate_ref, own_hbm, cot_hbm, w_hbm, refx_ref, gates_ref, cot_out, w_ref, own_ref, cot_ref, sems
):
    weights = pltpu.make_async_copy(w_hbm, w_ref, sems.at[2])
    weights.start()
    copies = [
        pltpu.make_async_copy(own_hbm, own_ref, sems.at[0]),
        pltpu.make_async_copy(cot_hbm, cot_ref, sems.at[1]),
    ]
    for copy in copies:
        copy.start()
    for copy in copies:
        copy.wait()
    local_views, channels, pixels = own_ref.shape
    for tile in range(pixels // LANE):
        for view in range(local_views):
            own = own_ref[view, :, pl.ds(tile * LANE, LANE)].astype(jnp.float32)
            for copied in range(SUB // local_views):
                first = copied * local_views + view
                refx_ref[tile, pl.ds(first, channels, stride=SUB), :] = own
    for g in range(gates_ref.shape[0]):
        gates_ref[g] = jnp.full((SUB, LANE), gate_ref[g], jnp.float32)

    def pack_one(plane, carry):
        pack_planes(cot_ref, plane, cot_out, plane)
        return carry

    lax.fori_loop(0, cot_out.shape[0], pack_one, 0)
    weights.wait()


def position(view, own_index, local_views, view_count):
    distance = (view // local_views) ^ own_index
    place = distance // 2 + (distance % 2) * (view_count // 2)
    return place * local_views + view % local_views


def assemble_kernel(src_ref, place_ref, *rest):
    *map_refs, rows_ref, maps, scratch = rest
    local_views, per_view = src_ref.shape
    tiles = scratch.shape[0]
    pairs = local_views * per_view
    view_count = maps.shape[1] // local_views
    blocks = maps.shape[2] // SUB
    own_index = place_ref[0]
    parity = place_ref[1]
    half = len(map_refs) // 2
    for side in range(2):
        first = 0
        for ref in map_refs[side * half : (side + 1) * half]:
            maps[side, first : first + ref.shape[0]] = ref[...]
            first += ref.shape[0]
    for pair in range(pairs):
        view = src_ref[pair % local_views, pair // local_views]
        slot = position(view, own_index, local_views, view_count)
        for tile in range(tiles):
            for side in range(2):
                values = maps[side, slot, :, pl.ds(tile * LANE, LANE)].astype(jnp.float32)
                held = parity if side == 0 else 1 - parity
                for block in range(blocks):
                    first = (2 * block + held) * (SUB * pairs) + pair
                    scratch[tile, pl.ds(first, SUB, stride=pairs), :] = values[
                        block * SUB : (block + 1) * SUB
                    ]
    for tile in range(tiles):
        rows_ref[:, pl.ds(tile * LANE, LANE)] = scratch[tile].astype(jnp.bfloat16)


def forward_vector(gates_ref, refx_ref, chunk, tile, plane, saved):
    warped_ref, corr_ref, sig_ref, rden_ref = saved
    pairs = sig_ref.shape[1]
    tiles = pairs // SUB
    lanes = pl.ds(tile * LANE, LANE)
    logits = None
    for g in range(G):
        total = None
        for j in range(0, GC, 2):
            c = g * GC + j
            span = pl.ds(c * pairs, 2 * pairs)
            both = chunk[span, lanes]
            warped_ref[plane, span, lanes] = both.astype(jnp.bfloat16)
            both = both.reshape(2, tiles, SUB, LANE)
            for i in range(2):
                part = both[i] * refx_ref[tile, pl.ds((c + i) * SUB, SUB), :][None]
                total = part if total is None else total + part
        corr = total * (1.0 / GC)
        corr_ref[plane, pl.ds(g * pairs, pairs), lanes] = corr.reshape(pairs, LANE)
        part = corr * gates_ref[g][None]
        logits = part if logits is None else logits + part
    sig = jax.nn.sigmoid(logits)
    sig_ref[plane, :, lanes] = sig.reshape(pairs, LANE)
    visible = 0.5 + sig
    den = jnp.sum(visible, axis=0)
    rden = 1.0 / (den + swap_halves(den))
    rden_ref[plane, :, lanes] = rden
    costs = []
    for g in range(G):
        corr = corr_ref[plane, pl.ds(g * pairs, pairs), lanes].reshape(tiles, SUB, LANE)
        num = jnp.sum(visible * corr, axis=0)
        costs.append((num + swap_halves(num)) * rden)
    return costs


def forward_body(count, plane_of, gates_ref, rows_ref, refx_ref, w_ref, saved, cost_ref, scratch):
    low = low_half()

    def matmul(chunk, at):
        chunk[...] = lax.dot_general(
            rows_ref[...], w_ref[plane_of(at)], NT, preferred_element_type=jnp.float32
        )

    def vector(chunk, at):
        plane = plane_of(at)
        for index in range(2):
            costs = [
                forward_vector(gates_ref, refx_ref, chunk, 2 * index + half, plane, saved)
                for half in range(2)
            ]
            for g in range(G):
                cost_ref[at, index, pl.ds(g * SUB, SUB), :] = jnp.where(
                    low, costs[0][g], costs[1][g]
                )

    def two_planes(turn, carry):
        first = 2 * turn
        matmul(scratch[0], first)
        vector(scratch[1], jnp.maximum(first - 1, 0))
        matmul(scratch[1], first + 1)
        vector(scratch[0], first)
        return carry

    lax.fori_loop(0, count // 2, two_planes, 0)
    vector(scratch[1], count - 1)


def edge_plane(planes, index):
    return jnp.where(index < 2, index, planes - 4 + index)


def edge_kernel(gates_ref, rows_ref, refx_ref, w_ref, cot_ref, *rest):
    up_ref, down_ref, cost, *scratch = rest[4:]
    planes = w_ref.shape[0]
    forward_body(
        4,
        functools.partial(edge_plane, planes),
        gates_ref,
        rows_ref,
        refx_ref,
        w_ref,
        rest[:4],
        cost,
        scratch,
    )
    down_ref[0:2] = cost[0:2]
    up_ref[0:2] = cost[2:4]
    down_ref[2] = cot_ref[0]
    up_ref[2] = cot_ref[planes - 1]


def inner_kernel(gates_ref, rows_ref, refx_ref, w_ref, *rest):
    cost_ref, *scratch = rest[8:]
    forward_body(
        cost_ref.shape[0],
        lambda index: index + 2,
        gates_ref,
        rows_ref,
        refx_ref,
        w_ref,
        rest[4:8],
        cost_ref,
        scratch,
    )


def depth_conv(
    taps_ref,
    below_ref,
    down_ref,
    inner_ref,
    up_ref,
    above_ref,
    cot_ref,
    regular_ref,
    cost,
    grad_ref,
    slope,
    smooth,
):
    planes = grad_ref.shape[0]
    local_views, _, groups, pixels = regular_ref.shape
    cost[0:2] = below_ref[0:2]
    cost[2:4] = down_ref[0:2]
    cost[4:planes] = inner_ref[...]
    cost[planes : planes + 2] = up_ref[0:2]
    cost[planes + 2 : planes + 4] = above_ref[0:2]
    slope[0] = below_ref[2]
    slope[1 : planes + 1] = cot_ref[...]
    slope[planes + 1] = above_ref[2]

    def mix(source, tap):
        totals = [None] * G
        for k in range(3):
            for b in range(G):
                value = source(k, b)
                for a in range(G):
                    part = value * tap(k, a, b)
                    totals[a] = part if totals[a] is None else totals[a] + part
        return totals

    def forward_planes(index, carry):
        plane = 2 * index
        pres = mix(
            lambda k, g: cost[pl.ds(plane + k, 2), :, pl.ds(g * SUB, SUB), :],
            lambda k, o, g: taps_ref[k, o, g],
        )
        for o in range(G):
            pre = pres[o]
            rows = pl.ds(o * SUB, SUB)
            sig = jax.nn.sigmoid(pre)
            both = pl.ds(plane, 2)
            slope[both, :, rows, :] = slope[both, :, rows, :] * (sig * (1.0 + pre * (1.0 - sig)))
            smooth[both, :, rows, :] = pre * sig
        return carry

    lax.fori_loop(0, (planes + 2) // 2, forward_planes, 0)

    def backward_planes(index, carry):
        plane = 2 * index
        grads = mix(
            lambda k, o: slope[pl.ds(plane + 2 - k, 2), :, pl.ds(o * SUB, SUB), :],
            lambda k, g, o: taps_ref[k, o, g],
        )
        for g in range(G):
            grad_ref[pl.ds(plane, 2), :, pl.ds(g * SUB, SUB), :] = grads[g]
        for view in range(local_views):
            for tile in range(pixels // LANE):
                first = (tile % 2) * local_views + view
                for i in range(2):
                    regular_ref[view, plane + i, :, pl.ds(tile * LANE, LANE)] = smooth[
                        plane + i + 1, tile // 2, pl.ds(first, groups, stride=SUB), :
                    ].astype(jnp.bfloat16)
        return carry

    lax.fori_loop(0, planes // 2, backward_planes, 0)


def backward_kernel(src_ref, place_ref, taps_ref, gates_ref, refx_ref, w_ref, *rest):
    halo_refs = rest[:6]
    warped_ref, corr_ref, sig_ref, rden_ref = rest[6:10]
    regular_ref, keep_ref, send_ref = rest[10:13]
    cost, grad_ref, slope, smooth, rows_a, rows_b, acc, dref, held, sems, dense = rest[13:]
    count = w_ref.shape[0]
    pairs = sig_ref.shape[1]
    tiles = pairs // SUB
    lane_tiles = dref.shape[0]
    local_views = src_ref.shape[0]
    channels = G * GC
    low = low_half()

    def vector(plane, tile, target):
        lanes = pl.ds(tile * LANE, LANE)
        pack = tile // 2
        half = tile % 2
        rden = rden_ref[plane, :, lanes]
        sig = sig_ref[plane, :, lanes].reshape(tiles, SUB, LANE)
        num_grads = []
        mixed = None
        for g in range(G):
            rows = pl.ds(g * SUB, SUB)
            grad = grad_ref[plane, pack, rows, :]
            num_grads.append(spread(grad, half, low) * rden)
            part = grad * cost[plane + 2, pack, rows, :]
            mixed = part if mixed is None else mixed + part
        vis_grad = -(spread(mixed, half, low) * rden)[None]
        for g in range(G):
            corr = corr_ref[plane, pl.ds(g * pairs, pairs), lanes].reshape(tiles, SUB, LANE)
            vis_grad = vis_grad + num_grads[g][None] * corr
        logit_grad = vis_grad * (sig * (1.0 - sig)) * (1.0 / GC)
        visible = (0.5 + sig) * (1.0 / GC)
        for g in range(G):
            corr_grad = visible * num_grads[g][None] + logit_grad * gates_ref[g][None]
            for j in range(0, GC, 2):
                c = g * GC + j
                span = pl.ds(c * pairs, 2 * pairs)
                both = jnp.concatenate(
                    [
                        (corr_grad * refx_ref[tile, pl.ds((c + i) * SUB, SUB), :][None]).reshape(
                            pairs, LANE
                        )
                        for i in range(2)
                    ],
                    axis=0,
                )
                target[span, lanes] = both.astype(jnp.bfloat16)
                warped = (
                    warped_ref[plane, span, lanes]
                    .astype(jnp.float32)
                    .reshape(2, tiles, SUB, LANE)
                )
                for i in range(2):
                    dref[tile, pl.ds((c + i) * SUB, SUB), :] += jnp.sum(
                        corr_grad * warped[i], axis=0
                    )

    def matmul(rows, slot):
        product = jnp.dot(rows[...], held[slot], preferred_element_type=jnp.float32)
        for tile in range(lane_tiles):
            acc[tile] += product[:, tile * LANE : (tile + 1) * LANE]

    def fetch(plane):
        slot = lax.rem(plane, 4)
        return pltpu.make_async_copy(w_ref.at[plane], held.at[slot], sems.at[slot])

    fetch(0).start()
    fetch(1).start()
    acc[...] = jnp.zeros_like(acc)
    dref[...] = jnp.zeros_like(dref)
    rows_b[...] = jnp.zeros_like(rows_b)
    held[3] = jnp.zeros_like(held[3])
    depth_conv(taps_ref, *halo_refs, regular_ref, cost, grad_ref, slope, smooth)

    def two_planes(turn, carry):
        for offset, rows, before in ((0, rows_a, rows_b), (1, rows_b, rows_a)):
            plane = 2 * turn + offset
            fetch(plane).wait()

            @pl.when(plane + 2 < count)
            def _():
                fetch(plane + 2).start()

            matmul(before, lax.rem(plane + 3, 4))
            for tile in range(lane_tiles):
                vector(plane, tile, rows)
        return carry

    lax.fori_loop(0, count // 2, two_planes, 0)
    matmul(rows_b, (count - 1) % 4)
    own_index = place_ref[0]
    parity = place_ref[1]
    blocks = keep_ref.shape[1] // SUB
    for target, held_side in ((dense, 1 - parity), (keep_ref, parity)):
        target[...] = jnp.zeros_like(target)
        for tile in range(lane_tiles):
            lanes = pl.ds(tile * LANE, LANE)
            for block in range(blocks):
                channel = (2 * block + held_side) * SUB
                part = pl.ds(block * SUB, SUB)
                for view in range(local_views):
                    total = None
                    for copy in range(SUB // local_views):
                        first = channel * SUB + copy * local_views + view
                        value = dref[tile, pl.ds(first, SUB, stride=SUB), :]
                        total = value if total is None else total + value
                    target[view, part, lanes] = total
        for pair in range(pairs):
            view = src_ref[pair % local_views, pair // local_views]
            slot = position(view, own_index, local_views, dense.shape[0] // local_views)
            for block in range(blocks):
                first = (2 * block + held_side) * (SUB * pairs) + pair
                part = pl.ds(block * SUB, SUB)
                for tile in range(lane_tiles):
                    target[slot, part, pl.ds(tile * LANE, LANE)] += acc[
                        tile, pl.ds(first, SUB, stride=pairs), :
                    ]
    send_ref[...] = dense[...].astype(jnp.bfloat16)


def split_kernel(first, keep_ref, received_ref, after_ref, even_ref, send_ref):
    count = even_ref.shape[0]
    half = keep_ref.shape[0] // 2
    for out_ref, start in ((even_ref, first), (send_ref, half + first)):
        span = pl.ds(start, count)
        out_ref[...] = (keep_ref[span] + received_ref[span].astype(jnp.float32)).astype(
            out_ref.dtype
        )


def spread_kernel(even_ref, received_ref, *out_refs):
    size = out_refs[0].shape[0]
    for index, out_ref in enumerate(out_refs):
        span = pl.ds(index * size, size)
        out_ref[...] = (even_ref[span] + received_ref[span].astype(jnp.float32)).astype(
            out_ref.dtype
        )


SMEM = functools.partial(pl.BlockSpec, memory_space=pltpu.SMEM)


def shards(features, sources, warp_weights, view_gate, depth_kernel, cotangent):
    view_count = lax.axis_size("view")
    plane_count = lax.axis_size("plane")
    own_index = lax.axis_index("view")
    plane_index = lax.axis_index("plane")
    local_views, channels, pixels = features.shape
    all_views, per_view = sources.shape
    pairs = local_views * per_view
    planes = warp_weights.shape[0]
    share = channels // plane_count
    blocks = plane_count // 2
    parity = plane_index % 2
    f32 = jnp.float32
    bf16 = jnp.bfloat16
    near = [(i, i ^ 1) for i in range(plane_count)]
    far = [(i, i ^ 2) for i in range(plane_count)]
    up = [(i, i + 1) for i in range(plane_count - 1)]
    down = [(i + 1, i) for i in range(plane_count - 1)]
    shape = jax.ShapeDtypeStruct

    halves = features.reshape(local_views, blocks, 2, share, pixels)
    mine = lax.dynamic_index_in_dim(halves, parity, 2, keepdims=False).reshape(
        local_views, channels // 2, pixels
    )

    def over_view(array, k):
        return lax.ppermute(array, "view", [(i, i ^ k) for i in range(view_count)])

    quarter = max(view_count // 4, 1)
    even = [mine] + [over_view(mine, k) for k in range(2, view_count, 2)]
    near_even = jnp.concatenate(even[:quarter], axis=0)
    far_even = jnp.concatenate(even[quarter:], axis=0)
    packed = (pixels // (2 * LANE), G * SUB, LANE)
    hbm = pl.BlockSpec(memory_space=pltpu.HBM)
    anywhere = pl.BlockSpec(memory_space=pl.ANY)
    refx, gates, cot, weights = pl.pallas_call(
        prep_kernel,
        out_shape=(
            shape((pixels // LANE, channels * SUB, LANE), f32),
            shape((G, SUB, LANE), f32),
            shape((planes,) + packed, f32),
            pltpu.VMEM(warp_weights.shape, bf16),
        ),
        in_specs=[SMEM(), hbm, hbm, hbm],
        scratch_shapes=[
            pltpu.VMEM(features.shape, bf16),
            pltpu.VMEM(cotangent.shape, bf16),
            pltpu.SemaphoreType.DMA((3,)),
        ],
        compiler_params=params(),
        cost_estimate=pl.CostEstimate(flops=10**9, bytes_accessed=4 * MIB, transcendentals=0),
        name="prep",
    )(
        pltpu.with_memory_space_constraint(view_gate, pltpu.HBM),
        pltpu.with_memory_space_constraint(features, pltpu.HBM),
        pltpu.with_memory_space_constraint(cotangent, pltpu.HBM),
        pltpu.with_memory_space_constraint(warp_weights, pltpu.HBM),
    )
    far_even, refx, gates, cot = lax.optimization_barrier((far_even, refx, gates, cot))
    maps = [near_even, far_even, over_view(near_even, 1), over_view(far_even, 1)]
    maps = maps + [lax.ppermute(part, "plane", near) for part in maps]

    src_own = lax.dynamic_slice_in_dim(sources, own_index * local_views, local_views, 0)
    place = jnp.stack([own_index, parity]).astype(jnp.int32)
    rows = pl.pallas_call(
        assemble_kernel,
        out_shape=shape((channels * pairs, pixels), bf16),
        in_specs=[SMEM(), SMEM()] + [pl.BlockSpec()] * len(maps),
        scratch_shapes=[
            pltpu.VMEM((2, all_views, channels // 2, pixels), bf16),
            pltpu.VMEM((pixels // LANE, channels * pairs, LANE), f32),
        ],
        compiler_params=params(24),
        name="assemble",
    )(src_own, place, *maps)

    saved = (
        pltpu.VMEM((planes, channels * pairs, pixels), bf16),
        pltpu.VMEM((planes, G * pairs, pixels), f32),
        pltpu.VMEM((planes, pairs, pixels), f32),
        pltpu.VMEM((planes, SUB, pixels), f32),
    )
    on_chip = functools.partial(pltpu.with_memory_space_constraint, memory_space=pltpu.VMEM)
    vmem = pl.BlockSpec(memory_space=pltpu.VMEM)
    scratch = [pltpu.VMEM((channels * pairs, pixels), f32)] * 2
    load = (3,) + packed
    rows, refx, gates, cot = [on_chip(item) for item in (rows, refx, gates, cot)]
    weights = on_chip(weights)
    *edge_saved, up_load, down_load = pl.pallas_call(
        edge_kernel,
        out_shape=saved + (shape(load, f32),) * 2,
        in_specs=[vmem] * 5,
        out_specs=(vmem,) * 6,
        scratch_shapes=[pltpu.VMEM((4,) + packed, f32)] + scratch,
        compiler_params=params(8),
        name="forward_edge",
    )(gates, rows, refx, weights, cot)
    below = lax.ppermute(up_load, "plane", up)
    above = lax.ppermute(down_load, "plane", down)
    inner_count = planes - 4
    *all_saved, inner_cost = pl.pallas_call(
        inner_kernel,
        out_shape=saved + (pltpu.VMEM((inner_count,) + packed, f32),),
        in_specs=[vmem] * 4 + [anywhere] * 4,
        out_specs=(vmem,) * 5,
        scratch_shapes=scratch,
        input_output_aliases={4 + i: i for i in range(4)},
        compiler_params=params(8),
        cost_estimate=pl.CostEstimate(
            flops=2 * channels * pairs * pixels * pixels * inner_count,
            bytes_accessed=40 * MIB,
            transcendentals=0,
        ),
        name="forward_inner",
    )(gates, rows, refx, weights, *[on_chip(item) for item in edge_saved])

    halo = (below, down_load, inner_cost, up_load, above, cot)
    returned = (all_views, channels // 2, pixels)
    regular, keep, send = pl.pallas_call(
        backward_kernel,
        out_shape=(shape(cotangent.shape, bf16), shape(returned, f32), shape(returned, bf16)),
        in_specs=[SMEM()] * 3 + [vmem, vmem, hbm] + [vmem] * 10,
        out_specs=(vmem,) * 3,
        scratch_shapes=[
            pltpu.VMEM((planes + 4,) + packed, f32),
            pltpu.VMEM((planes,) + packed, f32),
            pltpu.VMEM((planes + 2,) + packed, f32),
            pltpu.VMEM((planes + 2,) + packed, f32),
            pltpu.VMEM((channels * pairs, pixels), bf16),
            pltpu.VMEM((channels * pairs, pixels), bf16),
            pltpu.VMEM((pixels // LANE, channels * pairs, LANE), f32),
            pltpu.VMEM((pixels // LANE, channels * SUB, LANE), f32),
            pltpu.VMEM((4, pixels, pixels), bf16),
            pltpu.SemaphoreType.DMA((4,)),
            pltpu.VMEM(returned, f32),
        ],
        compiler_params=params(14 + 5 * all_views * channels * pixels // MIB),
        name="backward",
    )(
        src_own,
        place,
        pltpu.with_memory_space_constraint(depth_kernel, pltpu.HBM),
        gates,
        refx,
        pltpu.with_memory_space_constraint(warp_weights, pltpu.HBM),
        *halo,
        *[on_chip(item) for item in all_saved],
    )

    received = lax.ppermute(send, "plane", near)
    close = quarter * local_views
    piece = (local_views, channels // 2, pixels)

    def stage(first, count, after, kind):
        even_sum, outgoing = pl.pallas_call(
            functools.partial(split_kernel, first),
            out_shape=(shape((count,) + piece[1:], f32), shape((count,) + piece[1:], bf16)),
            in_specs=[pl.BlockSpec(), pl.BlockSpec(), anywhere],
            compiler_params=params(32),
            name="split",
        )(keep, received, after)
        incoming = over_view(outgoing, 1)
        return pl.pallas_call(
            spread_kernel,
            out_shape=(shape(piece, kind),) + (shape(piece, bf16),) * (count // local_views - 1),
            compiler_params=params(32),
            name="spread",
        )(even_sum, incoming)

    away_parts = stage(close, all_views // 2 - close, received, bf16)
    total, *close_parts = stage(0, close, away_parts[0], f32)
    for index, part in enumerate(away_parts):
        total = total + over_view(part, 2 * (quarter + index)).astype(f32)
    for index, part in enumerate(close_parts):
        total = total + over_view(part, 2 * (index + 1)).astype(f32)
    rounded = total.astype(bf16)
    total = rounded.astype(f32) + lax.ppermute(rounded, "plane", far).astype(f32)
    other = lax.ppermute(total, "plane", near)
    cut = (local_views, blocks, 1, share, pixels)
    first = jnp.where(parity == 0, total, other).reshape(cut)
    second = jnp.where(parity == 0, other, total).reshape(cut)
    feature_grads = jnp.concatenate([first, second], axis=2).reshape(features.shape)
    return (regular, feature_grads)


def solution(mesh):
    in_specs = (
        P("view", None, None),
        P(),
        P("plane", None, None),
        P(),
        P(),
        P("view", "plane", None, None),
    )
    out_specs = (P("view", "plane", None, None), P("view", None, None))
    return jax.shard_map(shards, mesh=mesh, in_specs=in_specs, out_specs=out_specs, check_vma=False)
```

```python
import functools

import jax
import jax.numpy as jnp
from jax import lax
from jax.experimental import pallas as pl
from jax.experimental.pallas import tpu as pltpu
from jax.sharding import PartitionSpec as P

G = 8
GC = 4
SUB = 8
LANE = 128
MIB = 1024 * 1024
NT = (((1,), (1,)), ((), ()))


def params(mib=16):
    return pltpu.CompilerParams(vmem_limit_bytes=mib * MIB)


def low_half():
    return lax.broadcasted_iota(jnp.int32, (SUB, LANE), 0) < SUB // 2


def swap_halves(tile):
    return pltpu.roll(tile, SUB // 2, 0)


def spread(tile, half, low):
    other = swap_halves(tile)
    return jnp.where(low, tile, other) if half == 0 else jnp.where(low, other, tile)


def pack_planes(array_ref, plane, out_ref, slot):
    local_views, _, groups, pixels = array_ref.shape
    for view in range(local_views):
        for tile in range(pixels // LANE):
            first = (tile % 2) * local_views + view
            out_ref[slot, tile // 2, pl.ds(first, groups, stride=SUB), :] = array_ref[
                view, plane, :, pl.ds(tile * LANE, LANE)
            ].astype(jnp.float32)


def prep_kernel(
    gate_ref, own_hbm, cot_hbm, refx_ref, gates_ref, cot_out, own_ref, cot_ref, sems
):
    copies = [
        pltpu.make_async_copy(own_hbm, own_ref, sems.at[0]),
        pltpu.make_async_copy(cot_hbm, cot_ref, sems.at[1]),
    ]
    for copy in copies:
        copy.start()
    for copy in copies:
        copy.wait()
    local_views, channels, pixels = own_ref.shape
    for tile in range(pixels // LANE):
        for view in range(local_views):
            own = own_ref[view, :, pl.ds(tile * LANE, LANE)].astype(jnp.float32)
            for copied in range(SUB // local_views):
                first = copied * local_views + view
                refx_ref[tile, pl.ds(first, channels, stride=SUB), :] = own
    for g in range(gates_ref.shape[0]):
        gates_ref[g] = jnp.full((SUB, LANE), gate_ref[g], jnp.float32)

    def pack_one(plane, carry):
        pack_planes(cot_ref, plane, cot_out, plane)
        return carry

    lax.fori_loop(0, cot_out.shape[0], pack_one, 0)


def position(view, own_index, local_views, view_count):
    distance = (view // local_views) ^ own_index
    place = distance // 2 + (distance % 2) * (view_count // 2)
    return place * local_views + view % local_views


def assemble(src_ref, place_ref, map_refs, rows_ref, maps, scratch):
    local_views, per_view = src_ref.shape
    tiles = scratch.shape[0]
    pairs = local_views * per_view
    view_count = maps.shape[1] // local_views
    blocks = maps.shape[2] // SUB
    own_index = place_ref[0]
    parity = place_ref[1]
    half = len(map_refs) // 2
    for side in range(2):
        first = 0
        for ref in map_refs[side * half : (side + 1) * half]:
            maps[side, first : first + ref.shape[0]] = ref[...]
            first += ref.shape[0]
    for pair in range(pairs):
        view = src_ref[pair % local_views, pair // local_views]
        slot = position(view, own_index, local_views, view_count)
        for tile in range(tiles):
            for side in range(2):
                values = maps[side, slot, :, pl.ds(tile * LANE, LANE)].astype(jnp.float32)
                held = parity if side == 0 else 1 - parity
                for block in range(blocks):
                    first = (2 * block + held) * (SUB * pairs) + pair
                    scratch[tile, pl.ds(first, SUB, stride=pairs), :] = values[
                        block * SUB : (block + 1) * SUB
                    ]
    for tile in range(tiles):
        rows_ref[:, pl.ds(tile * LANE, LANE)] = scratch[tile].astype(jnp.bfloat16)


def forward_vector(gates_ref, refx_ref, chunk, tile, plane, saved):
    warped_ref, corr_ref, sig_ref, rden_ref = saved
    pairs = sig_ref.shape[1]
    tiles = pairs // SUB
    lanes = pl.ds(tile * LANE, LANE)
    logits = None
    for g in range(G):
        total = None
        for j in range(0, GC, 2):
            c = g * GC + j
            span = pl.ds(c * pairs, 2 * pairs)
            both = chunk[span, lanes]
            warped_ref[plane, span, lanes] = both.astype(jnp.bfloat16)
            both = both.reshape(2, tiles, SUB, LANE)
            for i in range(2):
                part = both[i] * refx_ref[tile, pl.ds((c + i) * SUB, SUB), :][None]
                total = part if total is None else total + part
        corr = total * (1.0 / GC)
        corr_ref[plane, pl.ds(g * pairs, pairs), lanes] = corr.reshape(pairs, LANE)
        part = corr * gates_ref[g][None]
        logits = part if logits is None else logits + part
    sig = jax.nn.sigmoid(logits)
    sig_ref[plane, :, lanes] = sig.reshape(pairs, LANE)
    visible = 0.5 + sig
    den = jnp.sum(visible, axis=0)
    rden = 1.0 / (den + swap_halves(den))
    rden_ref[plane, :, lanes] = rden
    costs = []
    for g in range(G):
        corr = corr_ref[plane, pl.ds(g * pairs, pairs), lanes].reshape(tiles, SUB, LANE)
        num = jnp.sum(visible * corr, axis=0)
        costs.append((num + swap_halves(num)) * rden)
    return costs


def weight_copy(w_ref, plane, held, sems, slot):
    return pltpu.make_async_copy(w_ref.at[plane], held.at[slot], sems.at[slot])


def forward_body(count, plane_of, gates_ref, rows_ref, refx_ref, w_ref, saved, cost_ref, scratch):
    held, sems, *chunks = scratch
    low = low_half()

    def fetch(at, slot):
        return weight_copy(w_ref, plane_of(jnp.minimum(at, count - 1)), held, sems, slot)

    def matmul(slot):
        chunks[slot][...] = lax.dot_general(
            rows_ref[...], held[slot], NT, preferred_element_type=jnp.float32
        )

    def vector(slot, at):
        plane = plane_of(at)
        for index in range(2):
            costs = [
                forward_vector(gates_ref, refx_ref, chunks[slot], 2 * index + half, plane, saved)
                for half in range(2)
            ]
            for g in range(G):
                cost_ref[at, index, pl.ds(g * SUB, SUB), :] = jnp.where(
                    low, costs[0][g], costs[1][g]
                )

    def two_planes(turn, carry):
        first = 2 * turn
        for slot in range(2):
            fetch(first + slot, slot).wait()
            matmul(slot)
            fetch(first + slot + 2, slot).start()
            vector(1 - slot, jnp.maximum(first + slot - 1, 0))
        return carry

    lax.fori_loop(0, count // 2, two_planes, 0)
    vector(1, count - 1)
    for slot in range(2):
        fetch(count - 1, slot).wait()


def edge_plane(planes, index):
    return jnp.where(index < 2, index, planes - 4 + index)


def edge_kernel(src_ref, place_ref, gates_ref, refx_ref, w_ref, cot_ref, *rest):
    map_refs = rest[:8]
    saved = rest[8:12]
    up_ref, down_ref, rows_ref, next_ref = rest[12:16]
    maps, gathered, cost, next_sem, *scratch = rest[16:]
    held, sems, *_ = scratch
    planes = w_ref.shape[0]
    weight_copy(w_ref, 0, held, sems, 0).start()
    weight_copy(w_ref, 1, held, sems, 1).start()
    following = pltpu.make_async_copy(w_ref.at[2], next_ref, next_sem)
    following.start()
    assemble(src_ref, place_ref, map_refs, rows_ref, maps, gathered)
    forward_body(
        4,
        functools.partial(edge_plane, planes),
        gates_ref,
        rows_ref,
        refx_ref,
        w_ref,
        saved,
        cost,
        scratch,
    )
    down_ref[0:2] = cost[0:2]
    up_ref[0:2] = cost[2:4]
    down_ref[2] = cot_ref[0]
    up_ref[2] = cot_ref[planes - 1]
    following.wait()


def inner_kernel(gates_ref, rows_ref, refx_ref, w_ref, next_ref, *rest):
    cost_ref, *scratch = rest[8:]
    held, sems, *_ = scratch
    weight_copy(w_ref, 3, held, sems, 1).start()
    first = pltpu.make_async_copy(next_ref, held.at[0], sems.at[0])
    first.start()
    forward_body(
        cost_ref.shape[0],
        lambda index: index + 2,
        gates_ref,
        rows_ref,
        refx_ref,
        w_ref,
        rest[4:8],
        cost_ref,
        scratch,
    )


def depth_conv(
    taps_ref,
    below_ref,
    down_ref,
    inner_ref,
    up_ref,
    above_ref,
    cot_ref,
    regular_ref,
    cost,
    grad_ref,
    slope,
    smooth,
):
    planes = grad_ref.shape[0]
    local_views, _, groups, pixels = regular_ref.shape
    cost[0:2] = below_ref[0:2]
    cost[2:4] = down_ref[0:2]
    cost[4:planes] = inner_ref[...]
    cost[planes : planes + 2] = up_ref[0:2]
    cost[planes + 2 : planes + 4] = above_ref[0:2]
    slope[0] = below_ref[2]
    slope[1 : planes + 1] = cot_ref[...]
    slope[planes + 1] = above_ref[2]

    def mix(source, tap):
        totals = [None] * G
        for k in range(3):
            for b in range(G):
                value = source(k, b)
                for a in range(G):
                    part = value * tap(k, a, b)
                    totals[a] = part if totals[a] is None else totals[a] + part
        return totals

    def forward_planes(index, carry):
        plane = 2 * index
        pres = mix(
            lambda k, g: cost[pl.ds(plane + k, 2), :, pl.ds(g * SUB, SUB), :],
            lambda k, o, g: taps_ref[k, o, g],
        )
        for o in range(G):
            pre = pres[o]
            rows = pl.ds(o * SUB, SUB)
            sig = jax.nn.sigmoid(pre)
            both = pl.ds(plane, 2)
            slope[both, :, rows, :] = slope[both, :, rows, :] * (sig * (1.0 + pre * (1.0 - sig)))
            smooth[both, :, rows, :] = pre * sig
        return carry

    lax.fori_loop(0, (planes + 2) // 2, forward_planes, 0)

    def backward_planes(index, carry):
        plane = 2 * index
        grads = mix(
            lambda k, o: slope[pl.ds(plane + 2 - k, 2), :, pl.ds(o * SUB, SUB), :],
            lambda k, g, o: taps_ref[k, o, g],
        )
        for g in range(G):
            grad_ref[pl.ds(plane, 2), :, pl.ds(g * SUB, SUB), :] = grads[g]
        for view in range(local_views):
            for tile in range(pixels // LANE):
                first = (tile % 2) * local_views + view
                for i in range(2):
                    regular_ref[view, plane + i, :, pl.ds(tile * LANE, LANE)] = smooth[
                        plane + i + 1, tile // 2, pl.ds(first, groups, stride=SUB), :
                    ].astype(jnp.bfloat16)
        return carry

    lax.fori_loop(0, planes // 2, backward_planes, 0)


def backward_kernel(src_ref, place_ref, taps_ref, gates_ref, refx_ref, w_ref, *rest):
    halo_refs = rest[:6]
    warped_ref, corr_ref, sig_ref, rden_ref = rest[6:10]
    regular_ref, keep_ref, send_ref = rest[10:13]
    cost, grad_ref, slope, smooth, rows, acc, dref, held, sems, dense = rest[13:]
    count = w_ref.shape[0]
    pairs = sig_ref.shape[1]
    tiles = pairs // SUB
    lane_tiles = dref.shape[0]
    pixels = sig_ref.shape[2]
    local_views = src_ref.shape[0]
    low = low_half()

    def vector(plane, tile, offset):
        lanes = pl.ds(tile * LANE, LANE)
        target = pl.ds(offset * pixels + tile * LANE, LANE)
        pack = tile // 2
        half = tile % 2
        rden = rden_ref[plane, :, lanes]
        sig = sig_ref[plane, :, lanes].reshape(tiles, SUB, LANE)
        num_grads = []
        mixed = None
        for g in range(G):
            group = pl.ds(g * SUB, SUB)
            grad = grad_ref[plane, pack, group, :]
            num_grads.append(spread(grad, half, low) * rden)
            part = grad * cost[plane + 2, pack, group, :]
            mixed = part if mixed is None else mixed + part
        vis_grad = -(spread(mixed, half, low) * rden)[None]
        for g in range(G):
            corr = corr_ref[plane, pl.ds(g * pairs, pairs), lanes].reshape(tiles, SUB, LANE)
            vis_grad = vis_grad + num_grads[g][None] * corr
        logit_grad = vis_grad * (sig * (1.0 - sig)) * (1.0 / GC)
        visible = (0.5 + sig) * (1.0 / GC)
        for g in range(G):
            corr_grad = visible * num_grads[g][None] + logit_grad * gates_ref[g][None]
            for j in range(0, GC, 2):
                c = g * GC + j
                span = pl.ds(c * pairs, 2 * pairs)
                both = jnp.concatenate(
                    [
                        (corr_grad * refx_ref[tile, pl.ds((c + i) * SUB, SUB), :][None]).reshape(
                            pairs, LANE
                        )
                        for i in range(2)
                    ],
                    axis=0,
                )
                rows[span, target] = both.astype(jnp.bfloat16)
                warped = (
                    warped_ref[plane, span, lanes]
                    .astype(jnp.float32)
                    .reshape(2, tiles, SUB, LANE)
                )
                for i in range(2):
                    dref[tile, pl.ds((c + i) * SUB, SUB), :] += jnp.sum(
                        corr_grad * warped[i], axis=0
                    )

    turns = count // 2

    def fetch(turn):
        slot = lax.rem(turn, 2)
        first = 2 * jnp.minimum(turn, turns - 1)
        return [
            pltpu.make_async_copy(
                w_ref.at[first + offset],
                held.at[slot, pl.ds(offset * pixels, pixels)],
                sems.at[slot, offset],
            )
            for offset in range(2)
        ]

    for copy in fetch(0):
        copy.start()
    acc[...] = jnp.zeros_like(acc)
    dref[...] = jnp.zeros_like(dref)
    depth_conv(taps_ref, *halo_refs, regular_ref, cost, grad_ref, slope, smooth)

    def two_planes(turn, carry):
        for copy in fetch(turn + 1):
            copy.start()
        for copy in fetch(turn):
            copy.wait()
        for offset in range(2):
            for tile in range(lane_tiles):
                vector(2 * turn + offset, tile, offset)
        product = jnp.dot(
            rows[...], held[lax.rem(turn, 2)], preferred_element_type=jnp.float32
        )
        for tile in range(lane_tiles):
            acc[tile] += product[:, tile * LANE : (tile + 1) * LANE]
        return carry

    lax.fori_loop(0, turns, two_planes, 0)
    for copy in fetch(turns):
        copy.wait()
    own_index = place_ref[0]
    parity = place_ref[1]
    blocks = keep_ref.shape[1] // SUB
    for target, held_side in ((dense, 1 - parity), (keep_ref, parity)):
        target[...] = jnp.zeros_like(target)
        for tile in range(lane_tiles):
            lanes = pl.ds(tile * LANE, LANE)
            for block in range(blocks):
                channel = (2 * block + held_side) * SUB
                part = pl.ds(block * SUB, SUB)
                for view in range(local_views):
                    total = None
                    for copy in range(SUB // local_views):
                        first = channel * SUB + copy * local_views + view
                        value = dref[tile, pl.ds(first, SUB, stride=SUB), :]
                        total = value if total is None else total + value
                    target[view, part, lanes] = total
        for pair in range(pairs):
            view = src_ref[pair % local_views, pair // local_views]
            slot = position(view, own_index, local_views, dense.shape[0] // local_views)
            for block in range(blocks):
                first = (2 * block + held_side) * (SUB * pairs) + pair
                part = pl.ds(block * SUB, SUB)
                for tile in range(lane_tiles):
                    target[slot, part, pl.ds(tile * LANE, LANE)] += acc[
                        tile, pl.ds(first, SUB, stride=pairs), :
                    ]
    send_ref[...] = dense[...].astype(jnp.bfloat16)


def split_kernel(first, keep_ref, received_ref, after_ref, even_ref, send_ref):
    count = even_ref.shape[0]
    half = keep_ref.shape[0] // 2
    for out_ref, start in ((even_ref, first), (send_ref, half + first)):
        span = pl.ds(start, count)
        out_ref[...] = (keep_ref[span] + received_ref[span].astype(jnp.float32)).astype(
            out_ref.dtype
        )


def spread_kernel(even_ref, received_ref, *out_refs):
    size = out_refs[0].shape[0]
    for index, out_ref in enumerate(out_refs):
        span = pl.ds(index * size, size)
        out_ref[...] = (even_ref[span] + received_ref[span].astype(jnp.float32)).astype(
            out_ref.dtype
        )


SMEM = functools.partial(pl.BlockSpec, memory_space=pltpu.SMEM)


def shards(features, sources, warp_weights, view_gate, depth_kernel, cotangent):
    view_count = lax.axis_size("view")
    plane_count = lax.axis_size("plane")
    own_index = lax.axis_index("view")
    plane_index = lax.axis_index("plane")
    local_views, channels, pixels = features.shape
    all_views, per_view = sources.shape
    pairs = local_views * per_view
    planes = warp_weights.shape[0]
    share = channels // plane_count
    blocks = plane_count // 2
    parity = plane_index % 2
    f32 = jnp.float32
    bf16 = jnp.bfloat16
    near = [(i, i ^ 1) for i in range(plane_count)]
    far = [(i, i ^ 2) for i in range(plane_count)]
    up = [(i, i + 1) for i in range(plane_count - 1)]
    down = [(i + 1, i) for i in range(plane_count - 1)]
    shape = jax.ShapeDtypeStruct

    halves = features.reshape(local_views, blocks, 2, share, pixels)
    mine = lax.dynamic_index_in_dim(halves, parity, 2, keepdims=False).reshape(
        local_views, channels // 2, pixels
    )

    def over_view(array, k):
        return lax.ppermute(array, "view", [(i, i ^ k) for i in range(view_count)])

    quarter = max(view_count // 4, 1)
    even = [mine] + [over_view(mine, k) for k in range(2, view_count, 2)]
    near_even = jnp.concatenate(even[:quarter], axis=0)
    far_even = jnp.concatenate(even[quarter:], axis=0)
    packed = (pixels // (2 * LANE), G * SUB, LANE)
    hbm = pl.BlockSpec(memory_space=pltpu.HBM)
    anywhere = pl.BlockSpec(memory_space=pl.ANY)
    weights = pltpu.with_memory_space_constraint(warp_weights, pltpu.HBM)
    refx, gates, cot = pl.pallas_call(
        prep_kernel,
        out_shape=(
            shape((pixels // LANE, channels * SUB, LANE), f32),
            shape((G, SUB, LANE), f32),
            shape((planes,) + packed, f32),
        ),
        in_specs=[SMEM(), hbm, hbm],
        scratch_shapes=[
            pltpu.VMEM(features.shape, bf16),
            pltpu.VMEM(cotangent.shape, bf16),
            pltpu.SemaphoreType.DMA((2,)),
        ],
        compiler_params=params(4),
        cost_estimate=pl.CostEstimate(flops=10**9, bytes_accessed=4 * MIB, transcendentals=0),
        name="prep",
    )(
        pltpu.with_memory_space_constraint(view_gate, pltpu.HBM),
        pltpu.with_memory_space_constraint(features, pltpu.HBM),
        pltpu.with_memory_space_constraint(cotangent, pltpu.HBM),
    )
    far_even, refx, gates, cot = lax.optimization_barrier((far_even, refx, gates, cot))
    maps = [near_even, far_even, over_view(near_even, 1), over_view(far_even, 1)]
    maps = maps + [lax.ppermute(part, "plane", near) for part in maps]

    src_own = lax.dynamic_slice_in_dim(sources, own_index * local_views, local_views, 0)
    place = jnp.stack([own_index, parity]).astype(jnp.int32)
    saved = (
        pltpu.VMEM((planes, channels * pairs, pixels), bf16),
        pltpu.VMEM((planes, G * pairs, pixels), f32),
        pltpu.VMEM((planes, pairs, pixels), f32),
        pltpu.VMEM((planes, SUB, pixels), f32),
    )
    on_chip = functools.partial(pltpu.with_memory_space_constraint, memory_space=pltpu.VMEM)
    vmem = pl.BlockSpec(memory_space=pltpu.VMEM)
    scratch = [
        pltpu.VMEM((2, pixels, pixels), bf16),
        pltpu.SemaphoreType.DMA((2,)),
        pltpu.VMEM((channels * pairs, pixels), f32),
        pltpu.VMEM((channels * pairs, pixels), f32),
    ]
    load = (3,) + packed
    refx, gates, cot = [on_chip(item) for item in (refx, gates, cot)]
    *edge_saved, up_load, down_load, rows, following = pl.pallas_call(
        edge_kernel,
        out_shape=saved
        + (shape(load, f32),) * 2
        + (
            pltpu.VMEM((channels * pairs, pixels), bf16),
            pltpu.VMEM((pixels, pixels), bf16),
        ),
        in_specs=[SMEM()] * 2 + [vmem] * 2 + [hbm, vmem] + [vmem] * len(maps),
        out_specs=(vmem,) * 8,
        scratch_shapes=[
            pltpu.VMEM((2, all_views, channels // 2, pixels), bf16),
            pltpu.VMEM((pixels // LANE, channels * pairs, LANE), f32),
            pltpu.VMEM((4,) + packed, f32),
            pltpu.SemaphoreType.DMA,
        ]
        + scratch,
        compiler_params=params(12 + 4 * all_views * channels * pixels // MIB),
        name="forward_edge",
    )(src_own, place, gates, refx, weights, cot, *maps)
    rows, following = on_chip(rows), on_chip(following)
    below = lax.ppermute(up_load, "plane", up)
    above = lax.ppermute(down_load, "plane", down)
    inner_count = planes - 4
    *all_saved, inner_cost = pl.pallas_call(
        inner_kernel,
        out_shape=saved + (pltpu.VMEM((inner_count,) + packed, f32),),
        in_specs=[vmem] * 3 + [hbm, vmem] + [anywhere] * 4,
        out_specs=(vmem,) * 5,
        scratch_shapes=scratch,
        input_output_aliases={5 + i: i for i in range(4)},
        compiler_params=params(9),
        cost_estimate=pl.CostEstimate(
            flops=2 * channels * pairs * pixels * pixels * inner_count,
            bytes_accessed=40 * MIB,
            transcendentals=0,
        ),
        name="forward_inner",
    )(gates, rows, refx, weights, following, *[on_chip(item) for item in edge_saved])

    halo = (below, down_load, inner_cost, up_load, above, cot)
    returned = (all_views, channels // 2, pixels)
    regular, keep, send = pl.pallas_call(
        backward_kernel,
        out_shape=(shape(cotangent.shape, bf16), shape(returned, f32), shape(returned, bf16)),
        in_specs=[SMEM()] * 3 + [vmem, vmem, hbm] + [vmem] * 10,
        out_specs=(vmem,) * 3,
        scratch_shapes=[
            pltpu.VMEM((planes + 4,) + packed, f32),
            pltpu.VMEM((planes,) + packed, f32),
            pltpu.VMEM((planes + 2,) + packed, f32),
            pltpu.VMEM((planes + 2,) + packed, f32),
            pltpu.VMEM((channels * pairs, 2 * pixels), bf16),
            pltpu.VMEM((pixels // LANE, channels * pairs, LANE), f32),
            pltpu.VMEM((pixels // LANE, channels * SUB, LANE), f32),
            pltpu.VMEM((2, 2 * pixels, pixels), bf16),
            pltpu.SemaphoreType.DMA((2, 2)),
            pltpu.VMEM(returned, f32),
        ],
        compiler_params=params(14 + 5 * all_views * channels * pixels // MIB),
        name="backward",
    )(
        src_own,
        place,
        pltpu.with_memory_space_constraint(depth_kernel, pltpu.HBM),
        gates,
        refx,
        weights,
        *halo,
        *[on_chip(item) for item in all_saved],
    )

    received = lax.ppermute(send, "plane", near)
    close = quarter * local_views
    piece = (local_views, channels // 2, pixels)

    def stage(first, count, after, kind):
        even_sum, outgoing = pl.pallas_call(
            functools.partial(split_kernel, first),
            out_shape=(shape((count,) + piece[1:], f32), shape((count,) + piece[1:], bf16)),
            in_specs=[pl.BlockSpec(), pl.BlockSpec(), anywhere],
            compiler_params=params(32),
            name="split",
        )(keep, received, after)
        incoming = over_view(outgoing, 1)
        return pl.pallas_call(
            spread_kernel,
            out_shape=(shape(piece, kind),) + (shape(piece, bf16),) * (count // local_views - 1),
            compiler_params=params(32),
            name="spread",
        )(even_sum, incoming)

    away_parts = stage(close, all_views // 2 - close, received, bf16)
    total, *close_parts = stage(0, close, away_parts[0], f32)
    for index, part in enumerate(away_parts):
        total = total + over_view(part, 2 * (quarter + index)).astype(f32)
    for index, part in enumerate(close_parts):
        total = total + over_view(part, 2 * (index + 1)).astype(f32)
    rounded = total.astype(bf16)
    total = rounded.astype(f32) + lax.ppermute(rounded, "plane", far).astype(f32)
    other = lax.ppermute(total, "plane", near)
    cut = (local_views, blocks, 1, share, pixels)
    first = jnp.where(parity == 0, total, other).reshape(cut)
    second = jnp.where(parity == 0, other, total).reshape(cut)
    feature_grads = jnp.concatenate([first, second], axis=2).reshape(features.shape)
    return (regular, feature_grads)


def solution(mesh):
    in_specs = (
        P("view", None, None),
        P(),
        P("plane", None, None),
        P(),
        P(),
        P("view", "plane", None, None),
    )
    out_specs = (P("view", "plane", None, None), P("view", None, None))
    return jax.shard_map(shards, mesh=mesh, in_specs=in_specs, out_specs=out_specs, check_vma=False)
```

```python
import functools

import jax
import jax.numpy as jnp
from jax import lax
from jax.experimental import pallas as pl
from jax.experimental.pallas import tpu as pltpu
from jax.sharding import PartitionSpec as P

G = 8
GC = 4
SUB = 8
LANE = 128
MIB = 1024 * 1024
NT = (((1,), (1,)), ((), ()))


def params(mib=16):
    return pltpu.CompilerParams(vmem_limit_bytes=mib * MIB)


def low_half():
    return lax.broadcasted_iota(jnp.int32, (SUB, LANE), 0) < SUB // 2


def swap_halves(tile):
    return pltpu.roll(tile, SUB // 2, 0)


def spread(tile, half, low):
    other = swap_halves(tile)
    return jnp.where(low, tile, other) if half == 0 else jnp.where(low, other, tile)


def pack_planes(array_ref, plane, out_ref, slot):
    local_views, _, groups, pixels = array_ref.shape
    for view in range(local_views):
        for tile in range(pixels // LANE):
            first = (tile % 2) * local_views + view
            out_ref[slot, tile // 2, pl.ds(first, groups, stride=SUB), :] = array_ref[
                view, plane, :, pl.ds(tile * LANE, LANE)
            ].astype(jnp.float32)


def prep_kernel(
    gate_ref, own_hbm, cot_hbm, refx_ref, gates_ref, cot_out, own_ref, cot_ref, sems
):
    copies = [
        pltpu.make_async_copy(own_hbm, own_ref, sems.at[0]),
        pltpu.make_async_copy(cot_hbm, cot_ref, sems.at[1]),
    ]
    for copy in copies:
        copy.start()
    for copy in copies:
        copy.wait()
    local_views, channels, pixels = own_ref.shape
    for tile in range(pixels // LANE):
        for view in range(local_views):
            own = own_ref[view, :, pl.ds(tile * LANE, LANE)].astype(jnp.float32)
            for copied in range(SUB // local_views):
                first = copied * local_views + view
                refx_ref[tile, pl.ds(first, channels, stride=SUB), :] = own
    for g in range(gates_ref.shape[0]):
        gates_ref[g] = jnp.full((SUB, LANE), gate_ref[g], jnp.float32)

    def pack_one(plane, carry):
        pack_planes(cot_ref, plane, cot_out, plane)
        return carry

    lax.fori_loop(0, cot_out.shape[0], pack_one, 0)


def position(view, own_index, local_views, view_count):
    distance = (view // local_views) ^ own_index
    place = distance // 2 + (distance % 2) * (view_count // 2)
    return place * local_views + view % local_views


def assemble(src_ref, place_ref, map_refs, rows_ref, maps, scratch):
    local_views, per_view = src_ref.shape
    tiles = scratch.shape[0]
    pairs = local_views * per_view
    view_count = maps.shape[1] // local_views
    blocks = maps.shape[2] // SUB
    own_index = place_ref[0]
    parity = place_ref[1]
    half = len(map_refs) // 2
    for side in range(2):
        first = 0
        for ref in map_refs[side * half : (side + 1) * half]:
            maps[side, first : first + ref.shape[0]] = ref[...]
            first += ref.shape[0]
    for pair in range(pairs):
        view = src_ref[pair % local_views, pair // local_views]
        slot = position(view, own_index, local_views, view_count)
        for tile in range(tiles):
            for side in range(2):
                values = maps[side, slot, :, pl.ds(tile * LANE, LANE)].astype(jnp.float32)
                held = parity if side == 0 else 1 - parity
                for block in range(blocks):
                    first = (2 * block + held) * (SUB * pairs) + pair
                    scratch[tile, pl.ds(first, SUB, stride=pairs), :] = values[
                        block * SUB : (block + 1) * SUB
                    ]
    for tile in range(tiles):
        rows_ref[:, pl.ds(tile * LANE, LANE)] = scratch[tile].astype(jnp.bfloat16)


def forward_vector(gates_ref, refx_ref, chunk, tile, plane, saved):
    warped_ref, corr_ref, sig_ref, rden_ref = saved
    pairs = sig_ref.shape[1]
    tiles = pairs // SUB
    lanes = pl.ds(tile * LANE, LANE)
    logits = None
    for g in range(G):
        total = None
        for j in range(0, GC, 2):
            c = g * GC + j
            span = pl.ds(c * pairs, 2 * pairs)
            both = chunk[span, lanes]
            warped_ref[plane, span, lanes] = both.astype(jnp.bfloat16)
            both = both.reshape(2, tiles, SUB, LANE)
            for i in range(2):
                part = both[i] * refx_ref[tile, pl.ds((c + i) * SUB, SUB), :][None]
                total = part if total is None else total + part
        corr = total * (1.0 / GC)
        corr_ref[plane, pl.ds(g * pairs, pairs), lanes] = corr.reshape(pairs, LANE)
        part = corr * gates_ref[g][None]
        logits = part if logits is None else logits + part
    sig = jax.nn.sigmoid(logits)
    sig_ref[plane, :, lanes] = sig.reshape(pairs, LANE)
    visible = 0.5 + sig
    den = jnp.sum(visible, axis=0)
    rden = 1.0 / (den + swap_halves(den))
    rden_ref[plane, :, lanes] = rden
    costs = []
    for g in range(G):
        corr = corr_ref[plane, pl.ds(g * pairs, pairs), lanes].reshape(tiles, SUB, LANE)
        num = jnp.sum(visible * corr, axis=0)
        costs.append((num + swap_halves(num)) * rden)
    return costs


def weight_copy(w_ref, plane, held, sems, slot):
    return pltpu.make_async_copy(w_ref.at[plane], held.at[slot], sems.at[slot])


def forward_body(count, plane_of, gates_ref, rows_ref, refx_ref, w_ref, saved, cost_ref, scratch):
    held, sems, *chunks = scratch
    low = low_half()

    def fetch(at, slot):
        return weight_copy(w_ref, plane_of(jnp.minimum(at, count - 1)), held, sems, slot)

    def matmul(slot):
        chunks[slot][...] = lax.dot_general(
            rows_ref[...], held[slot], NT, preferred_element_type=jnp.float32
        )

    def vector(slot, at):
        plane = plane_of(at)
        for index in range(2):
            costs = [
                forward_vector(gates_ref, refx_ref, chunks[slot], 2 * index + half, plane, saved)
                for half in range(2)
            ]
            for g in range(G):
                cost_ref[at, index, pl.ds(g * SUB, SUB), :] = jnp.where(
                    low, costs[0][g], costs[1][g]
                )

    def two_planes(turn, carry):
        first = 2 * turn
        for slot in range(2):
            fetch(first + slot, slot).wait()
            matmul(slot)
            fetch(first + slot + 2, slot).start()
            vector(1 - slot, jnp.maximum(first + slot - 1, 0))
        return carry

    lax.fori_loop(0, count // 2, two_planes, 0)
    vector(1, count - 1)
    for slot in range(2):
        fetch(count - 1, slot).wait()


def edge_plane(planes, index):
    return jnp.where(index < 2, index, planes - 4 + index)


def edge_kernel(src_ref, place_ref, gates_ref, refx_ref, w_ref, cot_ref, *rest):
    map_refs = rest[:8]
    saved = rest[8:12]
    up_ref, down_ref, rows_ref, next_ref = rest[12:16]
    maps, gathered, cost, next_sem, *scratch = rest[16:]
    held, sems, *_ = scratch
    planes = w_ref.shape[0]
    weight_copy(w_ref, 0, held, sems, 0).start()
    weight_copy(w_ref, 1, held, sems, 1).start()
    following = pltpu.make_async_copy(w_ref.at[2], next_ref, next_sem)
    following.start()
    assemble(src_ref, place_ref, map_refs, rows_ref, maps, gathered)
    forward_body(
        4,
        functools.partial(edge_plane, planes),
        gates_ref,
        rows_ref,
        refx_ref,
        w_ref,
        saved,
        cost,
        scratch,
    )
    down_ref[0:2] = cost[0:2]
    up_ref[0:2] = cost[2:4]
    down_ref[2] = cot_ref[0]
    up_ref[2] = cot_ref[planes - 1]
    following.wait()


def inner_kernel(gates_ref, rows_ref, refx_ref, w_ref, next_ref, *rest):
    cost_ref, *scratch = rest[8:]
    held, sems, *_ = scratch
    weight_copy(w_ref, 3, held, sems, 1).start()
    first = pltpu.make_async_copy(next_ref, held.at[0], sems.at[0])
    first.start()
    forward_body(
        cost_ref.shape[0],
        lambda index: index + 2,
        gates_ref,
        rows_ref,
        refx_ref,
        w_ref,
        rest[4:8],
        cost_ref,
        scratch,
    )


def depth_conv(
    taps_ref,
    below_ref,
    down_ref,
    inner_ref,
    up_ref,
    above_ref,
    cot_ref,
    regular_ref,
    cost,
    grad_ref,
    slope,
    smooth,
):
    planes = grad_ref.shape[0]
    local_views, _, groups, pixels = regular_ref.shape
    cost[0:2] = below_ref[0:2]
    cost[2:4] = down_ref[0:2]
    cost[4:planes] = inner_ref[...]
    cost[planes : planes + 2] = up_ref[0:2]
    cost[planes + 2 : planes + 4] = above_ref[0:2]
    slope[0] = below_ref[2]
    slope[1 : planes + 1] = cot_ref[...]
    slope[planes + 1] = above_ref[2]

    def mix(source, tap):
        totals = [None] * G
        for k in range(3):
            for b in range(G):
                value = source(k, b)
                for a in range(G):
                    part = value * tap(k, a, b)
                    totals[a] = part if totals[a] is None else totals[a] + part
        return totals

    def forward_planes(index, carry):
        plane = 2 * index
        pres = mix(
            lambda k, g: cost[pl.ds(plane + k, 2), :, pl.ds(g * SUB, SUB), :],
            lambda k, o, g: taps_ref[k, o, g],
        )
        for o in range(G):
            pre = pres[o]
            rows = pl.ds(o * SUB, SUB)
            sig = jax.nn.sigmoid(pre)
            both = pl.ds(plane, 2)
            slope[both, :, rows, :] = slope[both, :, rows, :] * (sig * (1.0 + pre * (1.0 - sig)))
            smooth[both, :, rows, :] = pre * sig
        return carry

    lax.fori_loop(0, (planes + 2) // 2, forward_planes, 0)

    def backward_planes(index, carry):
        plane = 2 * index
        grads = mix(
            lambda k, o: slope[pl.ds(plane + 2 - k, 2), :, pl.ds(o * SUB, SUB), :],
            lambda k, g, o: taps_ref[k, o, g],
        )
        for g in range(G):
            grad_ref[pl.ds(plane, 2), :, pl.ds(g * SUB, SUB), :] = grads[g]
        for view in range(local_views):
            for tile in range(pixels // LANE):
                first = (tile % 2) * local_views + view
                for i in range(2):
                    regular_ref[view, plane + i, :, pl.ds(tile * LANE, LANE)] = smooth[
                        plane + i + 1, tile // 2, pl.ds(first, groups, stride=SUB), :
                    ].astype(jnp.bfloat16)
        return carry

    lax.fori_loop(0, planes // 2, backward_planes, 0)


def backward_kernel(src_ref, place_ref, taps_ref, gates_ref, refx_ref, w_ref, *rest):
    halo_refs = rest[:6]
    warped_ref, corr_ref, sig_ref, rden_ref = rest[6:10]
    regular_ref, keep_ref, send_ref = rest[10:13]
    cost, grad_ref, slope, smooth, rows, acc, column, dref, held, sems, dense = rest[13:]
    count = w_ref.shape[0]
    pairs = sig_ref.shape[1]
    tiles = pairs // SUB
    lane_tiles = dref.shape[0]
    pixels = sig_ref.shape[2]
    local_views = src_ref.shape[0]
    low = low_half()

    def vector(plane, tile, offset):
        lanes = pl.ds(tile * LANE, LANE)
        target = pl.ds(pl.multiple_of(offset * pixels + tile * LANE, LANE), LANE)
        pack = tile // 2
        half = tile % 2
        rden = rden_ref[plane, :, lanes]
        sig = sig_ref[plane, :, lanes].reshape(tiles, SUB, LANE)
        num_grads = []
        mixed = None
        for g in range(G):
            group = pl.ds(g * SUB, SUB)
            grad = grad_ref[plane, pack, group, :]
            num_grads.append(spread(grad, half, low) * rden)
            part = grad * cost[plane + 2, pack, group, :]
            mixed = part if mixed is None else mixed + part
        vis_grad = -(spread(mixed, half, low) * rden)[None]
        for g in range(G):
            corr = corr_ref[plane, pl.ds(g * pairs, pairs), lanes].reshape(tiles, SUB, LANE)
            vis_grad = vis_grad + num_grads[g][None] * corr
        logit_grad = vis_grad * (sig * (1.0 - sig)) * (1.0 / GC)
        visible = (0.5 + sig) * (1.0 / GC)
        for g in range(G):
            corr_grad = visible * num_grads[g][None] + logit_grad * gates_ref[g][None]
            for j in range(0, GC, 2):
                c = g * GC + j
                span = pl.ds(c * pairs, 2 * pairs)
                both = jnp.concatenate(
                    [
                        (corr_grad * refx_ref[tile, pl.ds((c + i) * SUB, SUB), :][None]).reshape(
                            pairs, LANE
                        )
                        for i in range(2)
                    ],
                    axis=0,
                )
                rows[span, target] = both.astype(jnp.bfloat16)
                warped = (
                    warped_ref[plane, span, lanes]
                    .astype(jnp.float32)
                    .reshape(2, tiles, SUB, LANE)
                )
                for i in range(2):
                    dref[tile, pl.ds((c + i) * SUB, SUB), :] += jnp.sum(
                        corr_grad * warped[i], axis=0
                    )

    group = rows.shape[1] // pixels

    def fetch(turn, offset):
        return pltpu.make_async_copy(
            w_ref.at[turn * group + offset],
            held.at[pl.ds(offset * pixels, pixels)],
            sems.at[offset],
        )

    acc[...] = jnp.zeros_like(acc)
    dref[...] = jnp.zeros_like(dref)
    depth_conv(taps_ref, *halo_refs, regular_ref, cost, grad_ref, slope, smooth)

    def one_turn(turn, carry):
        for offset in range(group):
            fetch(turn, offset).start()

        def one_plane(offset, carry):
            for tile in range(lane_tiles):
                vector(turn * group + offset, tile, offset)
            return carry

        lax.fori_loop(0, group, one_plane, 0)
        for offset in range(group):
            fetch(turn, offset).wait()
        for first in range(0, pixels, 2 * LANE):
            lanes = pl.ds(first, 2 * LANE)
            acc[:, lanes] += jnp.dot(
                rows[...], held[:, lanes], preferred_element_type=jnp.float32
            )
        return carry

    lax.fori_loop(0, count // group, one_turn, 0)
    own_index = place_ref[0]
    parity = place_ref[1]
    blocks = keep_ref.shape[1] // SUB
    sides = ((dense, 1 - parity), (keep_ref, parity))
    for target, held_side in sides:
        target[...] = jnp.zeros_like(target)
    for tile in range(lane_tiles):
        lanes = pl.ds(tile * LANE, LANE)
        column[...] = acc[:, lanes]
        for target, held_side in sides:
            for block in range(blocks):
                channel = (2 * block + held_side) * SUB
                part = pl.ds(block * SUB, SUB)
                for view in range(local_views):
                    total = None
                    for copy in range(SUB // local_views):
                        first = channel * SUB + copy * local_views + view
                        value = dref[tile, pl.ds(first, SUB, stride=SUB), :]
                        total = value if total is None else total + value
                    target[view, part, lanes] = total
                for pair in range(pairs):
                    view = src_ref[pair % local_views, pair // local_views]
                    slot = position(view, own_index, local_views, dense.shape[0] // local_views)
                    target[slot, part, lanes] += column[
                        pl.ds(channel * pairs + pair, SUB, stride=pairs), :
                    ]
    send_ref[...] = dense[...].astype(jnp.bfloat16)


def split_kernel(first, keep_ref, received_ref, after_ref, even_ref, send_ref):
    count = even_ref.shape[0]
    half = keep_ref.shape[0] // 2
    for out_ref, start in ((even_ref, first), (send_ref, half + first)):
        span = pl.ds(start, count)
        out_ref[...] = (keep_ref[span] + received_ref[span].astype(jnp.float32)).astype(
            out_ref.dtype
        )


def spread_kernel(even_ref, received_ref, *out_refs):
    size = out_refs[0].shape[0]
    for index, out_ref in enumerate(out_refs):
        span = pl.ds(index * size, size)
        out_ref[...] = (even_ref[span] + received_ref[span].astype(jnp.float32)).astype(
            out_ref.dtype
        )


def join_kernel(place_ref, mine_ref, other_ref, out_ref):
    parity = place_ref[1]
    for ref, side in ((mine_ref, parity), (other_ref, 1 - parity)):
        for block in range(ref.shape[1] // SUB):
            first = pl.multiple_of((2 * block + side) * SUB, SUB)
            out_ref[:, pl.ds(first, SUB), :] = ref[:, block * SUB : (block + 1) * SUB, :]


SMEM = functools.partial(pl.BlockSpec, memory_space=pltpu.SMEM)


def shards(features, sources, warp_weights, view_gate, depth_kernel, cotangent):
    view_count = lax.axis_size("view")
    plane_count = lax.axis_size("plane")
    own_index = lax.axis_index("view")
    plane_index = lax.axis_index("plane")
    local_views, channels, pixels = features.shape
    all_views, per_view = sources.shape
    pairs = local_views * per_view
    planes = warp_weights.shape[0]
    share = channels // plane_count
    blocks = plane_count // 2
    parity = plane_index % 2
    f32 = jnp.float32
    bf16 = jnp.bfloat16
    near = [(i, i ^ 1) for i in range(plane_count)]
    far = [(i, i ^ 2) for i in range(plane_count)]
    up = [(i, i + 1) for i in range(plane_count - 1)]
    down = [(i + 1, i) for i in range(plane_count - 1)]
    shape = jax.ShapeDtypeStruct

    halves = features.reshape(local_views, blocks, 2, share, pixels)
    mine = lax.dynamic_index_in_dim(halves, parity, 2, keepdims=False).reshape(
        local_views, channels // 2, pixels
    )

    def over_view(array, k):
        return lax.ppermute(array, "view", [(i, i ^ k) for i in range(view_count)])

    quarter = max(view_count // 4, 1)
    even = [mine] + [over_view(mine, k) for k in range(2, view_count, 2)]
    near_even = jnp.concatenate(even[:quarter], axis=0)
    far_even = jnp.concatenate(even[quarter:], axis=0)
    packed = (pixels // (2 * LANE), G * SUB, LANE)
    hbm = pl.BlockSpec(memory_space=pltpu.HBM)
    anywhere = pl.BlockSpec(memory_space=pl.ANY)
    weights = pltpu.with_memory_space_constraint(warp_weights, pltpu.HBM)
    refx, gates, cot = pl.pallas_call(
        prep_kernel,
        out_shape=(
            shape((pixels // LANE, channels * SUB, LANE), f32),
            shape((G, SUB, LANE), f32),
            shape((planes,) + packed, f32),
        ),
        in_specs=[SMEM(), hbm, hbm],
        scratch_shapes=[
            pltpu.VMEM(features.shape, bf16),
            pltpu.VMEM(cotangent.shape, bf16),
            pltpu.SemaphoreType.DMA((2,)),
        ],
        compiler_params=params(4),
        cost_estimate=pl.CostEstimate(flops=10**9, bytes_accessed=4 * MIB, transcendentals=0),
        name="prep",
    )(
        pltpu.with_memory_space_constraint(view_gate, pltpu.HBM),
        pltpu.with_memory_space_constraint(features, pltpu.HBM),
        pltpu.with_memory_space_constraint(cotangent, pltpu.HBM),
    )
    far_even, refx, gates, cot = lax.optimization_barrier((far_even, refx, gates, cot))
    maps = [near_even, far_even, over_view(near_even, 1), over_view(far_even, 1)]
    maps = maps + [lax.ppermute(part, "plane", near) for part in maps]

    src_own = lax.dynamic_slice_in_dim(sources, own_index * local_views, local_views, 0)
    place = jnp.stack([own_index, parity]).astype(jnp.int32)
    saved = (
        pltpu.VMEM((planes, channels * pairs, pixels), bf16),
        pltpu.VMEM((planes, G * pairs, pixels), f32),
        pltpu.VMEM((planes, pairs, pixels), f32),
        pltpu.VMEM((planes, SUB, pixels), f32),
    )
    on_chip = functools.partial(pltpu.with_memory_space_constraint, memory_space=pltpu.VMEM)
    vmem = pl.BlockSpec(memory_space=pltpu.VMEM)
    scratch = [
        pltpu.VMEM((2, pixels, pixels), bf16),
        pltpu.SemaphoreType.DMA((2,)),
        pltpu.VMEM((channels * pairs, pixels), f32),
        pltpu.VMEM((channels * pairs, pixels), f32),
    ]
    load = (3,) + packed
    refx, gates, cot = [on_chip(item) for item in (refx, gates, cot)]
    *edge_saved, up_load, down_load, rows, following = pl.pallas_call(
        edge_kernel,
        out_shape=saved
        + (shape(load, f32),) * 2
        + (
            pltpu.VMEM((channels * pairs, pixels), bf16),
            pltpu.VMEM((pixels, pixels), bf16),
        ),
        in_specs=[SMEM()] * 2 + [vmem] * 2 + [hbm, vmem] + [vmem] * len(maps),
        out_specs=(vmem,) * 8,
        scratch_shapes=[
            pltpu.VMEM((2, all_views, channels // 2, pixels), bf16),
            pltpu.VMEM((pixels // LANE, channels * pairs, LANE), f32),
            pltpu.VMEM((4,) + packed, f32),
            pltpu.SemaphoreType.DMA,
        ]
        + scratch,
        compiler_params=params(12 + 4 * all_views * channels * pixels // MIB),
        name="forward_edge",
    )(src_own, place, gates, refx, weights, cot, *maps)
    rows, following = on_chip(rows), on_chip(following)
    below = lax.ppermute(up_load, "plane", up)
    above = lax.ppermute(down_load, "plane", down)
    inner_count = planes - 4
    *all_saved, inner_cost = pl.pallas_call(
        inner_kernel,
        out_shape=saved + (pltpu.VMEM((inner_count,) + packed, f32),),
        in_specs=[vmem] * 3 + [hbm, vmem] + [anywhere] * 4,
        out_specs=(vmem,) * 5,
        scratch_shapes=scratch,
        input_output_aliases={5 + i: i for i in range(4)},
        compiler_params=params(9),
        cost_estimate=pl.CostEstimate(
            flops=2 * channels * pairs * pixels * pixels * inner_count,
            bytes_accessed=40 * MIB,
            transcendentals=0,
        ),
        name="forward_inner",
    )(gates, rows, refx, weights, following, *[on_chip(item) for item in edge_saved])

    halo = (below, down_load, inner_cost, up_load, above, cot)
    returned = (all_views, channels // 2, pixels)
    group = max(size for size in (4, 2, 1) if planes % size == 0)
    regular, keep, send = pl.pallas_call(
        backward_kernel,
        out_shape=(shape(cotangent.shape, bf16), shape(returned, f32), shape(returned, bf16)),
        in_specs=[SMEM()] * 3 + [vmem, vmem, hbm] + [vmem] * 10,
        out_specs=(vmem,) * 3,
        scratch_shapes=[
            pltpu.VMEM((planes + 4,) + packed, f32),
            pltpu.VMEM((planes,) + packed, f32),
            pltpu.VMEM((planes + 2,) + packed, f32),
            pltpu.VMEM((planes + 2,) + packed, f32),
            pltpu.VMEM((channels * pairs, group * pixels), bf16),
            pltpu.VMEM((channels * pairs, pixels), f32),
            pltpu.VMEM((channels * pairs, LANE), f32),
            pltpu.VMEM((pixels // LANE, channels * SUB, LANE), f32),
            pltpu.VMEM((group * pixels, pixels), bf16),
            pltpu.SemaphoreType.DMA((group,)),
            pltpu.VMEM(returned, f32),
        ],
        compiler_params=params(16 + 9 * all_views * channels * pixels // MIB),
        name="backward",
    )(
        src_own,
        place,
        pltpu.with_memory_space_constraint(depth_kernel, pltpu.HBM),
        gates,
        refx,
        weights,
        *halo,
        *[on_chip(item) for item in all_saved],
    )

    received = lax.ppermute(send, "plane", near)
    close = quarter * local_views
    piece = (local_views, channels // 2, pixels)

    def stage(first, count, after, kind):
        even_sum, outgoing = pl.pallas_call(
            functools.partial(split_kernel, first),
            out_shape=(shape((count,) + piece[1:], f32), shape((count,) + piece[1:], bf16)),
            in_specs=[pl.BlockSpec(), pl.BlockSpec(), anywhere],
            compiler_params=params(32),
            name="split",
        )(keep, received, after)
        incoming = over_view(outgoing, 1)
        return pl.pallas_call(
            spread_kernel,
            out_shape=(shape(piece, kind),) + (shape(piece, bf16),) * (count // local_views - 1),
            compiler_params=params(32),
            name="spread",
        )(even_sum, incoming)

    away_parts = stage(close, all_views // 2 - close, received, bf16)
    total, *close_parts = stage(0, close, away_parts[0], f32)
    for index, part in enumerate(away_parts):
        total = total + over_view(part, 2 * (quarter + index)).astype(f32)
    for index, part in enumerate(close_parts):
        total = total + over_view(part, 2 * (index + 1)).astype(f32)
    rounded = total.astype(bf16)
    total = rounded.astype(f32) + lax.ppermute(rounded, "plane", far).astype(f32)
    other = lax.ppermute(total, "plane", near)
    feature_grads = pl.pallas_call(
        join_kernel,
        out_shape=shape(features.shape, f32),
        in_specs=[SMEM(), vmem, vmem],
        compiler_params=params(4),
        name="join",
    )(place, total, other)
    return (regular, feature_grads)


def solution(mesh):
    in_specs = (
        P("view", None, None),
        P(),
        P("plane", None, None),
        P(),
        P(),
        P("view", "plane", None, None),
    )
    out_specs = (P("view", "plane", None, None), P("view", None, None))
    return jax.shard_map(shards, mesh=mesh, in_specs=in_specs, out_specs=out_specs, check_vma=False)
```

```python
import functools

import jax
import jax.numpy as jnp
from jax import lax
from jax.experimental import pallas as pl
from jax.experimental.pallas import tpu as pltpu
from jax.sharding import PartitionSpec as P

G = 8
GC = 4
SUB = 8
LANE = 128
MIB = 1024 * 1024
NT = (((1,), (1,)), ((), ()))


def params(mib=16):
    return pltpu.CompilerParams(vmem_limit_bytes=mib * MIB)


def low_half():
    return lax.broadcasted_iota(jnp.int32, (SUB, LANE), 0) < SUB // 2


def swap_halves(tile):
    return pltpu.roll(tile, SUB // 2, 0)


def spread(tile, half, low):
    other = swap_halves(tile)
    return jnp.where(low, tile, other) if half == 0 else jnp.where(low, other, tile)


def pack_planes(array_ref, plane, out_ref, slot):
    local_views, _, groups, pixels = array_ref.shape
    for view in range(local_views):
        for tile in range(pixels // LANE):
            first = (tile % 2) * local_views + view
            out_ref[slot, tile // 2, pl.ds(first, groups, stride=SUB), :] = array_ref[
                view, plane, :, pl.ds(tile * LANE, LANE)
            ].astype(jnp.float32)


def prep_kernel(
    gate_ref, own_hbm, cot_hbm, refx_ref, gates_ref, cot_out, own_ref, cot_ref, sems
):
    copies = [
        pltpu.make_async_copy(own_hbm, own_ref, sems.at[0]),
        pltpu.make_async_copy(cot_hbm, cot_ref, sems.at[1]),
    ]
    for copy in copies:
        copy.start()
    for copy in copies:
        copy.wait()
    local_views, channels, pixels = own_ref.shape
    for tile in range(pixels // LANE):
        for view in range(local_views):
            own = own_ref[view, :, pl.ds(tile * LANE, LANE)].astype(jnp.float32)
            for copied in range(SUB // local_views):
                first = copied * local_views + view
                refx_ref[tile, pl.ds(first, channels, stride=SUB), :] = own
    for g in range(gates_ref.shape[0]):
        gates_ref[g] = jnp.full((SUB, LANE), gate_ref[g], jnp.float32)

    def pack_one(plane, carry):
        pack_planes(cot_ref, plane, cot_out, plane)
        return carry

    lax.fori_loop(0, cot_out.shape[0], pack_one, 0)


def position(view, own_index, local_views, view_count):
    distance = (view // local_views) ^ own_index
    place = distance // 2 + (distance % 2) * (view_count // 2)
    return place * local_views + view % local_views


def assemble(src_ref, place_ref, map_refs, rows_ref, maps, scratch):
    local_views, per_view = src_ref.shape
    tiles = scratch.shape[0]
    pairs = local_views * per_view
    view_count = maps.shape[1] // local_views
    blocks = maps.shape[2] // SUB
    own_index = place_ref[0]
    parity = place_ref[1]
    half = len(map_refs) // 2
    for side in range(2):
        first = 0
        for ref in map_refs[side * half : (side + 1) * half]:
            maps[side, first : first + ref.shape[0]] = ref[...]
            first += ref.shape[0]
    for pair in range(pairs):
        view = src_ref[pair % local_views, pair // local_views]
        slot = position(view, own_index, local_views, view_count)
        for tile in range(tiles):
            for side in range(2):
                values = maps[side, slot, :, pl.ds(tile * LANE, LANE)].astype(jnp.float32)
                held = parity if side == 0 else 1 - parity
                for block in range(blocks):
                    first = (2 * block + held) * (SUB * pairs) + pair
                    scratch[tile, pl.ds(first, SUB, stride=pairs), :] = values[
                        block * SUB : (block + 1) * SUB
                    ]
    for tile in range(tiles):
        rows_ref[:, pl.ds(tile * LANE, LANE)] = scratch[tile].astype(jnp.bfloat16)


def forward_vector(gates_ref, refx_ref, chunk, tile, plane, saved):
    warped_ref, corr_ref, sig_ref, rden_ref = saved
    pairs = sig_ref.shape[1]
    tiles = pairs // SUB
    lanes = pl.ds(tile * LANE, LANE)
    logits = None
    for g in range(G):
        total = None
        for j in range(0, GC, 2):
            c = g * GC + j
            span = pl.ds(c * pairs, 2 * pairs)
            both = chunk[span, lanes]
            warped_ref[plane, span, lanes] = both.astype(jnp.bfloat16)
            both = both.reshape(2, tiles, SUB, LANE)
            for i in range(2):
                part = both[i] * refx_ref[tile, pl.ds((c + i) * SUB, SUB), :][None]
                total = part if total is None else total + part
        corr = total * (1.0 / GC)
        corr_ref[plane, pl.ds(g * pairs, pairs), lanes] = corr.reshape(pairs, LANE)
        part = corr * gates_ref[g][None]
        logits = part if logits is None else logits + part
    sig = jax.nn.sigmoid(logits)
    sig_ref[plane, :, lanes] = sig.reshape(pairs, LANE)
    visible = 0.5 + sig
    den = jnp.sum(visible, axis=0)
    rden = 1.0 / (den + swap_halves(den))
    rden_ref[plane, :, lanes] = rden
    costs = []
    for g in range(G):
        corr = corr_ref[plane, pl.ds(g * pairs, pairs), lanes].reshape(tiles, SUB, LANE)
        num = jnp.sum(visible * corr, axis=0)
        costs.append((num + swap_halves(num)) * rden)
    return costs


def weight_copy(w_ref, plane, held, sems, slot):
    return pltpu.make_async_copy(w_ref.at[plane], held.at[slot], sems.at[slot])


def forward_body(count, plane_of, gates_ref, rows_ref, refx_ref, w_ref, saved, cost_ref, scratch):
    held, sems, *chunks = scratch
    low = low_half()

    def fetch(at, slot):
        return weight_copy(w_ref, plane_of(jnp.minimum(at, count - 1)), held, sems, slot)

    def matmul(slot):
        chunks[slot][...] = lax.dot_general(
            rows_ref[...], held[slot], NT, preferred_element_type=jnp.float32
        )

    def vector(slot, at):
        plane = plane_of(at)
        for index in range(2):
            costs = [
                forward_vector(gates_ref, refx_ref, chunks[slot], 2 * index + half, plane, saved)
                for half in range(2)
            ]
            for g in range(G):
                cost_ref[at, index, pl.ds(g * SUB, SUB), :] = jnp.where(
                    low, costs[0][g], costs[1][g]
                )

    def two_planes(turn, carry):
        first = 2 * turn
        for slot in range(2):
            fetch(first + slot, slot).wait()
            matmul(slot)
            fetch(first + slot + 2, slot).start()
            vector(1 - slot, jnp.maximum(first + slot - 1, 0))
        return carry

    lax.fori_loop(0, count // 2, two_planes, 0)
    vector(1, count - 1)
    for slot in range(2):
        fetch(count - 1, slot).wait()


def edge_plane(planes, index):
    return jnp.where(index < 2, index, planes - 4 + index)


def edge_kernel(src_ref, place_ref, gates_ref, refx_ref, w_ref, cot_ref, *rest):
    map_refs = rest[:8]
    saved = rest[8:12]
    up_ref, down_ref, rows_ref, next_ref = rest[12:16]
    maps, gathered, cost, next_sem, *scratch = rest[16:]
    held, sems, *_ = scratch
    planes = w_ref.shape[0]
    weight_copy(w_ref, 0, held, sems, 0).start()
    weight_copy(w_ref, 1, held, sems, 1).start()
    following = pltpu.make_async_copy(w_ref.at[2], next_ref, next_sem)
    following.start()
    assemble(src_ref, place_ref, map_refs, rows_ref, maps, gathered)
    forward_body(
        4,
        functools.partial(edge_plane, planes),
        gates_ref,
        rows_ref,
        refx_ref,
        w_ref,
        saved,
        cost,
        scratch,
    )
    down_ref[0:2] = cost[0:2]
    up_ref[0:2] = cost[2:4]
    down_ref[2] = cot_ref[0]
    up_ref[2] = cot_ref[planes - 1]
    following.wait()


def inner_kernel(gates_ref, rows_ref, refx_ref, w_ref, next_ref, *rest):
    cost_ref, *scratch = rest[8:]
    held, sems, *_ = scratch
    weight_copy(w_ref, 3, held, sems, 1).start()
    first = pltpu.make_async_copy(next_ref, held.at[0], sems.at[0])
    first.start()
    forward_body(
        cost_ref.shape[0],
        lambda index: index + 2,
        gates_ref,
        rows_ref,
        refx_ref,
        w_ref,
        rest[4:8],
        cost_ref,
        scratch,
    )


def depth_conv(
    taps_ref,
    below_ref,
    down_ref,
    inner_ref,
    up_ref,
    above_ref,
    cot_ref,
    regular_ref,
    cost,
    slope,
    smooth,
):
    local_views, planes, groups, pixels = regular_ref.shape
    cost[0:2] = below_ref[0:2]
    cost[2:4] = down_ref[0:2]
    cost[4:planes] = inner_ref[...]
    cost[planes : planes + 2] = up_ref[0:2]
    cost[planes + 2 : planes + 4] = above_ref[0:2]
    slope[0] = below_ref[2]
    slope[1 : planes + 1] = cot_ref[...]
    slope[planes + 1] = above_ref[2]

    def mix(source, tap):
        totals = [None] * G
        for k in range(3):
            for b in range(G):
                value = source(k, b)
                for a in range(G):
                    part = value * tap(k, a, b)
                    totals[a] = part if totals[a] is None else totals[a] + part
        return totals

    def forward_planes(index, carry):
        plane = 2 * index
        pres = mix(
            lambda k, g: cost[pl.ds(plane + k, 2), :, pl.ds(g * SUB, SUB), :],
            lambda k, o, g: taps_ref[k, o, g],
        )
        for o in range(G):
            pre = pres[o]
            rows = pl.ds(o * SUB, SUB)
            sig = jax.nn.sigmoid(pre)
            both = pl.ds(plane, 2)
            slope[both, :, rows, :] = slope[both, :, rows, :] * (sig * (1.0 + pre * (1.0 - sig)))
            smooth[:, :, rows, :] = pre * sig
        for view in range(local_views):
            for tile in range(pixels // LANE):
                first = (tile % 2) * local_views + view
                for i, at in ((1, jnp.minimum(plane, planes - 1)), (0, jnp.abs(plane - 1))):
                    kept = smooth[i, tile // 2, pl.ds(first, groups, stride=SUB), :]
                    regular_ref[view, at, :, pl.ds(tile * LANE, LANE)] = kept.astype(jnp.bfloat16)
        return carry

    lax.fori_loop(0, (planes + 2) // 2, forward_planes, 0)

    def backward_planes(index, carry):
        plane = 2 * index
        grads = mix(
            lambda k, o: slope[pl.ds(plane + 2 - k, 2), :, pl.ds(o * SUB, SUB), :],
            lambda k, g, o: taps_ref[k, o, g],
        )
        for g in range(G):
            slope[pl.ds(plane, 2), :, pl.ds(g * SUB, SUB), :] = grads[g]
        return carry

    lax.fori_loop(0, planes // 2, backward_planes, 0)


def backward_kernel(src_ref, place_ref, taps_ref, gates_ref, refx_ref, w_ref, *rest):
    halo_refs = rest[:6]
    warped_ref, corr_ref, sig_ref, rden_ref = rest[6:10]
    regular_ref, keep_ref, send_ref = rest[10:13]
    cost, grad_ref, smooth, rows, acc, dref, held, sems, dense = rest[13:]
    count = w_ref.shape[0]
    pairs = sig_ref.shape[1]
    tiles = pairs // SUB
    lane_tiles = dref.shape[0]
    pixels = sig_ref.shape[2]
    local_views = src_ref.shape[0]
    low = low_half()

    def vector(plane, tile, offset):
        lanes = pl.ds(tile * LANE, LANE)
        target = pl.ds(offset * pixels + tile * LANE, LANE)
        pack = tile // 2
        half = tile % 2
        rden = rden_ref[plane, :, lanes]
        sig = sig_ref[plane, :, lanes].reshape(tiles, SUB, LANE)
        num_grads = []
        mixed = None
        for g in range(G):
            group = pl.ds(g * SUB, SUB)
            grad = grad_ref[plane, pack, group, :]
            num_grads.append(spread(grad, half, low) * rden)
            part = grad * cost[plane + 2, pack, group, :]
            mixed = part if mixed is None else mixed + part
        vis_grad = -(spread(mixed, half, low) * rden)[None]
        for g in range(G):
            corr = corr_ref[plane, pl.ds(g * pairs, pairs), lanes].reshape(tiles, SUB, LANE)
            vis_grad = vis_grad + num_grads[g][None] * corr
        logit_grad = vis_grad * (sig * (1.0 - sig)) * (1.0 / GC)
        visible = (0.5 + sig) * (1.0 / GC)
        for g in range(G):
            corr_grad = visible * num_grads[g][None] + logit_grad * gates_ref[g][None]
            for j in range(0, GC, 2):
                c = g * GC + j
                span = pl.ds(c * pairs, 2 * pairs)
                both = jnp.concatenate(
                    [
                        (corr_grad * refx_ref[tile, pl.ds((c + i) * SUB, SUB), :][None]).reshape(
                            pairs, LANE
                        )
                        for i in range(2)
                    ],
                    axis=0,
                )
                rows[span, target] = both.astype(jnp.bfloat16)
                warped = (
                    warped_ref[plane, span, lanes]
                    .astype(jnp.float32)
                    .reshape(2, tiles, SUB, LANE)
                )
                for i in range(2):
                    dref[tile, pl.ds((c + i) * SUB, SUB), :] += jnp.sum(
                        corr_grad * warped[i], axis=0
                    )

    group = rows.shape[1] // pixels

    def fetch(turn, offset):
        return pltpu.make_async_copy(
            w_ref.at[turn * group + offset],
            held.at[pl.ds(offset * pixels, pixels)],
            sems.at[offset],
        )

    acc[...] = jnp.zeros_like(acc)
    dref[...] = jnp.zeros_like(dref)
    depth_conv(taps_ref, *halo_refs, regular_ref, cost, grad_ref, smooth)

    def one_turn(turn, carry):
        for offset in range(group):
            fetch(turn, offset).start()
        for offset in range(group):
            for tile in range(lane_tiles):
                vector(turn * group + offset, tile, offset)
        for offset in range(group):
            fetch(turn, offset).wait()
        product = jnp.dot(rows[...], held[...], preferred_element_type=jnp.float32)
        for tile in range(lane_tiles):
            acc[tile] += product[:, tile * LANE : (tile + 1) * LANE]
        return carry

    lax.fori_loop(0, count // group, one_turn, 0)
    own_index = place_ref[0]
    parity = place_ref[1]
    blocks = keep_ref.shape[1] // SUB
    for target, held_side in ((dense, 1 - parity), (keep_ref, parity)):
        target[...] = jnp.zeros_like(target)
        for tile in range(lane_tiles):
            lanes = pl.ds(tile * LANE, LANE)
            for block in range(blocks):
                channel = (2 * block + held_side) * SUB
                part = pl.ds(block * SUB, SUB)
                for view in range(local_views):
                    total = None
                    for copy in range(SUB // local_views):
                        first = channel * SUB + copy * local_views + view
                        value = dref[tile, pl.ds(first, SUB, stride=SUB), :]
                        total = value if total is None else total + value
                    target[view, part, lanes] = total
        for pair in range(pairs):
            view = src_ref[pair % local_views, pair // local_views]
            slot = position(view, own_index, local_views, dense.shape[0] // local_views)
            for block in range(blocks):
                first = (2 * block + held_side) * (SUB * pairs) + pair
                part = pl.ds(block * SUB, SUB)
                for tile in range(lane_tiles):
                    target[slot, part, pl.ds(tile * LANE, LANE)] += acc[
                        tile, pl.ds(first, SUB, stride=pairs), :
                    ]
    send_ref[...] = dense[...].astype(jnp.bfloat16)


def split_kernel(first, keep_ref, received_ref, after_ref, even_ref, send_ref):
    count = even_ref.shape[0]
    half = keep_ref.shape[0] // 2
    for out_ref, start in ((even_ref, first), (send_ref, half + first)):
        span = pl.ds(start, count)
        out_ref[...] = (keep_ref[span] + received_ref[span].astype(jnp.float32)).astype(
            out_ref.dtype
        )


def spread_kernel(even_ref, received_ref, *out_refs):
    size = out_refs[0].shape[0]
    for index, out_ref in enumerate(out_refs):
        span = pl.ds(index * size, size)
        out_ref[...] = (even_ref[span] + received_ref[span].astype(jnp.float32)).astype(
            out_ref.dtype
        )


def join_kernel(place_ref, mine_ref, other_ref, out_ref):
    parity = place_ref[1]
    for ref, side in ((mine_ref, parity), (other_ref, 1 - parity)):
        for block in range(ref.shape[1] // SUB):
            first = pl.multiple_of((2 * block + side) * SUB, SUB)
            out_ref[:, pl.ds(first, SUB), :] = ref[:, block * SUB : (block + 1) * SUB, :]


SMEM = functools.partial(pl.BlockSpec, memory_space=pltpu.SMEM)


def shards(features, sources, warp_weights, view_gate, depth_kernel, cotangent):
    view_count = lax.axis_size("view")
    plane_count = lax.axis_size("plane")
    own_index = lax.axis_index("view")
    plane_index = lax.axis_index("plane")
    local_views, channels, pixels = features.shape
    all_views, per_view = sources.shape
    pairs = local_views * per_view
    planes = warp_weights.shape[0]
    share = channels // plane_count
    blocks = plane_count // 2
    parity = plane_index % 2
    f32 = jnp.float32
    bf16 = jnp.bfloat16
    near = [(i, i ^ 1) for i in range(plane_count)]
    far = [(i, i ^ 2) for i in range(plane_count)]
    up = [(i, i + 1) for i in range(plane_count - 1)]
    down = [(i + 1, i) for i in range(plane_count - 1)]
    shape = jax.ShapeDtypeStruct

    halves = features.reshape(local_views, blocks, 2, share, pixels)
    mine = lax.dynamic_index_in_dim(halves, parity, 2, keepdims=False).reshape(
        local_views, channels // 2, pixels
    )

    def over_view(array, k):
        return lax.ppermute(array, "view", [(i, i ^ k) for i in range(view_count)])

    quarter = max(view_count // 4, 1)
    even = [mine] + [over_view(mine, k) for k in range(2, view_count, 2)]
    near_even = jnp.concatenate(even[:quarter], axis=0)
    far_even = jnp.concatenate(even[quarter:], axis=0)
    packed = (pixels // (2 * LANE), G * SUB, LANE)
    hbm = pl.BlockSpec(memory_space=pltpu.HBM)
    anywhere = pl.BlockSpec(memory_space=pl.ANY)
    weights = pltpu.with_memory_space_constraint(warp_weights, pltpu.HBM)
    refx, gates, cot = pl.pallas_call(
        prep_kernel,
        out_shape=(
            shape((pixels // LANE, channels * SUB, LANE), f32),
            shape((G, SUB, LANE), f32),
            shape((planes,) + packed, f32),
        ),
        in_specs=[SMEM(), hbm, hbm],
        scratch_shapes=[
            pltpu.VMEM(features.shape, bf16),
            pltpu.VMEM(cotangent.shape, bf16),
            pltpu.SemaphoreType.DMA((2,)),
        ],
        compiler_params=params(4),
        cost_estimate=pl.CostEstimate(flops=10**9, bytes_accessed=4 * MIB, transcendentals=0),
        name="prep",
    )(
        pltpu.with_memory_space_constraint(view_gate, pltpu.HBM),
        pltpu.with_memory_space_constraint(features, pltpu.HBM),
        pltpu.with_memory_space_constraint(cotangent, pltpu.HBM),
    )
    far_even, refx, gates, cot = lax.optimization_barrier((far_even, refx, gates, cot))
    maps = [near_even, far_even, over_view(near_even, 1), over_view(far_even, 1)]
    maps = maps + [lax.ppermute(part, "plane", near) for part in maps]

    src_own = lax.dynamic_slice_in_dim(sources, own_index * local_views, local_views, 0)
    place = jnp.stack([own_index, parity]).astype(jnp.int32)
    saved = (
        pltpu.VMEM((planes, channels * pairs, pixels), bf16),
        pltpu.VMEM((planes, G * pairs, pixels), f32),
        pltpu.VMEM((planes, pairs, pixels), f32),
        pltpu.VMEM((planes, SUB, pixels), f32),
    )
    on_chip = functools.partial(pltpu.with_memory_space_constraint, memory_space=pltpu.VMEM)
    vmem = pl.BlockSpec(memory_space=pltpu.VMEM)
    scratch = [
        pltpu.VMEM((2, pixels, pixels), bf16),
        pltpu.SemaphoreType.DMA((2,)),
        pltpu.VMEM((channels * pairs, pixels), f32),
        pltpu.VMEM((channels * pairs, pixels), f32),
    ]
    load = (3,) + packed
    refx, gates, cot = [on_chip(item) for item in (refx, gates, cot)]
    *edge_saved, up_load, down_load, rows, following = pl.pallas_call(
        edge_kernel,
        out_shape=saved
        + (shape(load, f32),) * 2
        + (
            pltpu.VMEM((channels * pairs, pixels), bf16),
            pltpu.VMEM((pixels, pixels), bf16),
        ),
        in_specs=[SMEM()] * 2 + [vmem] * 2 + [hbm, vmem] + [vmem] * len(maps),
        out_specs=(vmem,) * 8,
        scratch_shapes=[
            pltpu.VMEM((2, all_views, channels // 2, pixels), bf16),
            pltpu.VMEM((pixels // LANE, channels * pairs, LANE), f32),
            pltpu.VMEM((4,) + packed, f32),
            pltpu.SemaphoreType.DMA,
        ]
        + scratch,
        compiler_params=params(12 + 4 * all_views * channels * pixels // MIB),
        name="forward_edge",
    )(src_own, place, gates, refx, weights, cot, *maps)
    rows, following = on_chip(rows), on_chip(following)
    below = lax.ppermute(up_load, "plane", up)
    above = lax.ppermute(down_load, "plane", down)
    inner_count = planes - 4
    *all_saved, inner_cost = pl.pallas_call(
        inner_kernel,
        out_shape=saved + (pltpu.VMEM((inner_count,) + packed, f32),),
        in_specs=[vmem] * 3 + [hbm, vmem] + [anywhere] * 4,
        out_specs=(vmem,) * 5,
        scratch_shapes=scratch,
        input_output_aliases={5 + i: i for i in range(4)},
        compiler_params=params(9),
        cost_estimate=pl.CostEstimate(
            flops=2 * channels * pairs * pixels * pixels * inner_count,
            bytes_accessed=40 * MIB,
            transcendentals=0,
        ),
        name="forward_inner",
    )(gates, rows, refx, weights, following, *[on_chip(item) for item in edge_saved])

    halo = (below, down_load, inner_cost, up_load, above, cot)
    returned = (all_views, channels // 2, pixels)
    group = max(size for size in (3, 2, 1) if planes % size == 0)
    regular, keep, send = pl.pallas_call(
        backward_kernel,
        out_shape=(shape(cotangent.shape, bf16), shape(returned, f32), shape(returned, bf16)),
        in_specs=[SMEM()] * 3 + [vmem, vmem, hbm] + [vmem] * 10,
        out_specs=(vmem,) * 3,
        scratch_shapes=[
            pltpu.VMEM((planes + 4,) + packed, f32),
            pltpu.VMEM((planes + 2,) + packed, f32),
            pltpu.VMEM((2,) + packed, f32),
            pltpu.VMEM((channels * pairs, group * pixels), bf16),
            pltpu.VMEM((pixels // LANE, channels * pairs, LANE), f32),
            pltpu.VMEM((pixels // LANE, channels * SUB, LANE), f32),
            pltpu.VMEM((group * pixels, pixels), bf16),
            pltpu.SemaphoreType.DMA((group,)),
            pltpu.VMEM(returned, f32),
        ],
        compiler_params=params(14 + 5 * all_views * channels * pixels // MIB),
        name="backward",
    )(
        src_own,
        place,
        pltpu.with_memory_space_constraint(depth_kernel, pltpu.HBM),
        gates,
        refx,
        weights,
        *halo,
        *[on_chip(item) for item in all_saved],
    )

    received = lax.ppermute(send, "plane", near)
    close = quarter * local_views
    piece = (local_views, channels // 2, pixels)

    def stage(first, count, after, kind):
        even_sum, outgoing = pl.pallas_call(
            functools.partial(split_kernel, first),
            out_shape=(shape((count,) + piece[1:], f32), shape((count,) + piece[1:], bf16)),
            in_specs=[pl.BlockSpec(), pl.BlockSpec(), anywhere],
            compiler_params=params(32),
            name="split",
        )(keep, received, after)
        incoming = over_view(outgoing, 1)
        return pl.pallas_call(
            spread_kernel,
            out_shape=(shape(piece, kind),) + (shape(piece, bf16),) * (count // local_views - 1),
            compiler_params=params(32),
            name="spread",
        )(even_sum, incoming)

    away_parts = stage(close, all_views // 2 - close, received, bf16)
    total, *close_parts = stage(0, close, away_parts[0], f32)
    for index, part in enumerate(away_parts):
        total = total + over_view(part, 2 * (quarter + index)).astype(f32)
    for index, part in enumerate(close_parts):
        total = total + over_view(part, 2 * (index + 1)).astype(f32)
    rounded = total.astype(bf16)
    total = rounded.astype(f32) + lax.ppermute(rounded, "plane", far).astype(f32)
    other = lax.ppermute(total, "plane", near)
    feature_grads = pl.pallas_call(
        join_kernel,
        out_shape=shape(features.shape, f32),
        in_specs=[SMEM(), vmem, vmem],
        compiler_params=params(4),
        name="join",
    )(place, total, other)
    return (regular, feature_grads)


def solution(mesh):
    in_specs = (
        P("view", None, None),
        P(),
        P("plane", None, None),
        P(),
        P(),
        P("view", "plane", None, None),
    )
    out_specs = (P("view", "plane", None, None), P("view", None, None))
    return jax.shard_map(shards, mesh=mesh, in_specs=in_specs, out_specs=out_specs, check_vma=False)
```

```python
import functools

import jax
import jax.numpy as jnp
from jax import lax
from jax.experimental import pallas as pl
from jax.experimental.pallas import tpu as pltpu
from jax.sharding import PartitionSpec as P

G = 8
GC = 4
SUB = 8
LANE = 128
MIB = 1024 * 1024
NT = (((1,), (1,)), ((), ()))


def params(mib=16):
    return pltpu.CompilerParams(vmem_limit_bytes=mib * MIB)


def low_half():
    return lax.broadcasted_iota(jnp.int32, (SUB, LANE), 0) < SUB // 2


def swap_halves(tile):
    return pltpu.roll(tile, SUB // 2, 0)


def spread(tile, half, low):
    other = swap_halves(tile)
    return jnp.where(low, tile, other) if half == 0 else jnp.where(low, other, tile)


def pack_planes(array_ref, plane, out_ref, slot):
    local_views, _, groups, pixels = array_ref.shape
    for view in range(local_views):
        for tile in range(pixels // LANE):
            first = (tile % 2) * local_views + view
            out_ref[slot, tile // 2, pl.ds(first, groups, stride=SUB), :] = array_ref[
                view, plane, :, pl.ds(tile * LANE, LANE)
            ].astype(jnp.float32)


def prep_kernel(
    gate_ref, own_hbm, cot_hbm, refx_ref, gates_ref, cot_out, own_ref, cot_ref, sems
):
    copies = [
        pltpu.make_async_copy(own_hbm, own_ref, sems.at[0]),
        pltpu.make_async_copy(cot_hbm, cot_ref, sems.at[1]),
    ]
    for copy in copies:
        copy.start()
    for copy in copies:
        copy.wait()
    local_views, channels, pixels = own_ref.shape
    for tile in range(pixels // LANE):
        for view in range(local_views):
            own = own_ref[view, :, pl.ds(tile * LANE, LANE)].astype(jnp.float32)
            for copied in range(SUB // local_views):
                first = copied * local_views + view
                refx_ref[tile, pl.ds(first, channels, stride=SUB), :] = own
    for g in range(gates_ref.shape[0]):
        gates_ref[g] = jnp.full((SUB, LANE), gate_ref[g], jnp.float32)

    def pack_one(plane, carry):
        pack_planes(cot_ref, plane, cot_out, plane)
        return carry

    lax.fori_loop(0, cot_out.shape[0], pack_one, 0)


def position(view, own_index, local_views, view_count):
    distance = (view // local_views) ^ own_index
    place = distance // 2 + (distance % 2) * (view_count // 2)
    return place * local_views + view % local_views


def assemble(src_ref, place_ref, map_refs, rows_ref, maps, scratch):
    local_views, per_view = src_ref.shape
    tiles = scratch.shape[0]
    pairs = local_views * per_view
    view_count = maps.shape[1] // local_views
    blocks = maps.shape[2] // SUB
    own_index = place_ref[0]
    parity = place_ref[1]
    half = len(map_refs) // 2
    for side in range(2):
        first = 0
        for ref in map_refs[side * half : (side + 1) * half]:
            maps[side, first : first + ref.shape[0]] = ref[...]
            first += ref.shape[0]
    for pair in range(pairs):
        view = src_ref[pair % local_views, pair // local_views]
        slot = position(view, own_index, local_views, view_count)
        for tile in range(tiles):
            for side in range(2):
                values = maps[side, slot, :, pl.ds(tile * LANE, LANE)].astype(jnp.float32)
                held = parity if side == 0 else 1 - parity
                for block in range(blocks):
                    first = (2 * block + held) * (SUB * pairs) + pair
                    scratch[tile, pl.ds(first, SUB, stride=pairs), :] = values[
                        block * SUB : (block + 1) * SUB
                    ]
    for tile in range(tiles):
        rows_ref[:, pl.ds(tile * LANE, LANE)] = scratch[tile].astype(jnp.bfloat16)


def forward_vector(gates_ref, refx_ref, chunk, tile, plane, saved):
    warped_ref, corr_ref, sig_ref, rden_ref = saved
    pairs = sig_ref.shape[1]
    tiles = pairs // SUB
    lanes = pl.ds(tile * LANE, LANE)
    logits = None
    for g in range(G):
        total = None
        for j in range(0, GC, 2):
            c = g * GC + j
            span = pl.ds(c * pairs, 2 * pairs)
            both = chunk[span, lanes]
            warped_ref[plane, span, lanes] = both.astype(jnp.bfloat16)
            both = both.reshape(2, tiles, SUB, LANE)
            for i in range(2):
                part = both[i] * refx_ref[tile, pl.ds((c + i) * SUB, SUB), :][None]
                total = part if total is None else total + part
        corr = total * (1.0 / GC)
        corr_ref[plane, pl.ds(g * pairs, pairs), lanes] = corr.reshape(pairs, LANE)
        part = corr * gates_ref[g][None]
        logits = part if logits is None else logits + part
    sig = jax.nn.sigmoid(logits)
    sig_ref[plane, :, lanes] = sig.reshape(pairs, LANE)
    visible = 0.5 + sig
    den = jnp.sum(visible, axis=0)
    rden = 1.0 / (den + swap_halves(den))
    rden_ref[plane, :, lanes] = rden
    costs = []
    for g in range(G):
        corr = corr_ref[plane, pl.ds(g * pairs, pairs), lanes].reshape(tiles, SUB, LANE)
        num = jnp.sum(visible * corr, axis=0)
        costs.append((num + swap_halves(num)) * rden)
    return costs


def weight_copy(w_ref, plane, held, sems, slot):
    return pltpu.make_async_copy(w_ref.at[plane], held.at[slot], sems.at[slot])


def forward_body(count, plane_of, gates_ref, rows_ref, refx_ref, w_ref, saved, cost_ref, scratch):
    held, sems, *chunks = scratch
    low = low_half()

    def fetch(at, slot):
        return weight_copy(w_ref, plane_of(jnp.minimum(at, count - 1)), held, sems, slot)

    def matmul(slot):
        chunks[slot][...] = lax.dot_general(
            rows_ref[...], held[slot], NT, preferred_element_type=jnp.float32
        )

    def vector(slot, at):
        plane = plane_of(at)
        for index in range(2):
            costs = [
                forward_vector(gates_ref, refx_ref, chunks[slot], 2 * index + half, plane, saved)
                for half in range(2)
            ]
            for g in range(G):
                cost_ref[at, index, pl.ds(g * SUB, SUB), :] = jnp.where(
                    low, costs[0][g], costs[1][g]
                )

    def two_planes(turn, carry):
        first = 2 * turn
        for slot in range(2):
            fetch(first + slot, slot).wait()
            matmul(slot)
            fetch(first + slot + 2, slot).start()
            vector(1 - slot, jnp.maximum(first + slot - 1, 0))
        return carry

    lax.fori_loop(0, count // 2, two_planes, 0)
    vector(1, count - 1)
    for slot in range(2):
        fetch(count - 1, slot).wait()


def edge_plane(planes, index):
    return jnp.where(index < 2, index, planes - 4 + index)


def edge_kernel(src_ref, place_ref, gates_ref, refx_ref, w_ref, cot_ref, *rest):
    map_refs = rest[:8]
    saved = rest[8:12]
    up_ref, down_ref, rows_ref, next_ref = rest[12:16]
    maps, gathered, cost, next_sem, *scratch = rest[16:]
    held, sems, *_ = scratch
    planes = w_ref.shape[0]
    weight_copy(w_ref, 0, held, sems, 0).start()
    weight_copy(w_ref, 1, held, sems, 1).start()
    following = pltpu.make_async_copy(w_ref.at[2], next_ref, next_sem)
    following.start()
    assemble(src_ref, place_ref, map_refs, rows_ref, maps, gathered)
    forward_body(
        4,
        functools.partial(edge_plane, planes),
        gates_ref,
        rows_ref,
        refx_ref,
        w_ref,
        saved,
        cost,
        scratch,
    )
    down_ref[0:2] = cost[0:2]
    up_ref[0:2] = cost[2:4]
    down_ref[2] = cot_ref[0]
    up_ref[2] = cot_ref[planes - 1]
    following.wait()


def inner_kernel(gates_ref, rows_ref, refx_ref, w_ref, next_ref, *rest):
    cost_ref, *scratch = rest[8:]
    held, sems, *_ = scratch
    weight_copy(w_ref, 3, held, sems, 1).start()
    first = pltpu.make_async_copy(next_ref, held.at[0], sems.at[0])
    first.start()
    forward_body(
        cost_ref.shape[0],
        lambda index: index + 2,
        gates_ref,
        rows_ref,
        refx_ref,
        w_ref,
        rest[4:8],
        cost_ref,
        scratch,
    )


def depth_conv(
    taps_ref,
    below_ref,
    down_ref,
    inner_ref,
    up_ref,
    above_ref,
    cot_ref,
    regular_ref,
    cost,
    slope,
    smooth,
):
    local_views, planes, groups, pixels = regular_ref.shape
    cost[0:2] = below_ref[0:2]
    cost[2:4] = down_ref[0:2]
    cost[4:planes] = inner_ref[...]
    cost[planes : planes + 2] = up_ref[0:2]
    cost[planes + 2 : planes + 4] = above_ref[0:2]
    slope[0] = below_ref[2]
    slope[1 : planes + 1] = cot_ref[...]
    slope[planes + 1] = above_ref[2]

    def mix(source, tap):
        totals = [None] * G
        for k in range(3):
            for b in range(G):
                value = source(k, b)
                for a in range(G):
                    part = value * tap(k, a, b)
                    totals[a] = part if totals[a] is None else totals[a] + part
        return totals

    def forward_planes(index, carry):
        plane = 2 * index
        pres = mix(
            lambda k, g: cost[pl.ds(plane + k, 2), :, pl.ds(g * SUB, SUB), :],
            lambda k, o, g: taps_ref[k, o, g],
        )
        for o in range(G):
            pre = pres[o]
            rows = pl.ds(o * SUB, SUB)
            sig = jax.nn.sigmoid(pre)
            both = pl.ds(plane, 2)
            slope[both, :, rows, :] = slope[both, :, rows, :] * (sig * (1.0 + pre * (1.0 - sig)))
            smooth[:, :, rows, :] = pre * sig
        for view in range(local_views):
            for tile in range(pixels // LANE):
                first = (tile % 2) * local_views + view
                for i, at in ((1, jnp.minimum(plane, planes - 1)), (0, jnp.abs(plane - 1))):
                    kept = smooth[i, tile // 2, pl.ds(first, groups, stride=SUB), :]
                    regular_ref[view, at, :, pl.ds(tile * LANE, LANE)] = kept.astype(jnp.bfloat16)
        return carry

    lax.fori_loop(0, (planes + 2) // 2, forward_planes, 0)

    def backward_planes(index, carry):
        plane = 2 * index
        grads = mix(
            lambda k, o: slope[pl.ds(plane + 2 - k, 2), :, pl.ds(o * SUB, SUB), :],
            lambda k, g, o: taps_ref[k, o, g],
        )
        for g in range(G):
            slope[pl.ds(plane, 2), :, pl.ds(g * SUB, SUB), :] = grads[g]
        return carry

    lax.fori_loop(0, planes // 2, backward_planes, 0)


def backward_kernel(src_ref, place_ref, taps_ref, gates_ref, refx_ref, w_ref, *rest):
    halo_refs = rest[:6]
    warped_ref, corr_ref, sig_ref, rden_ref = rest[6:10]
    regular_ref, keep_ref, send_ref = rest[10:13]
    cost, grad_ref, smooth, rows, acc, dref, held, sems = rest[13:]
    count = w_ref.shape[0]
    pairs = sig_ref.shape[1]
    tiles = pairs // SUB
    lane_tiles = dref.shape[0]
    pixels = sig_ref.shape[2]
    local_views = src_ref.shape[0]
    low = low_half()

    def vector(plane, tile, offset, side):
        lanes = pl.ds(tile * LANE, LANE)
        target = pl.ds(offset * pixels + tile * LANE, LANE)
        pack = tile // 2
        half = tile % 2
        rden = rden_ref[plane, :, lanes]
        sig = sig_ref[plane, :, lanes].reshape(tiles, SUB, LANE)
        num_grads = []
        mixed = None
        for g in range(G):
            group = pl.ds(g * SUB, SUB)
            grad = grad_ref[plane, pack, group, :]
            num_grads.append(spread(grad, half, low) * rden)
            part = grad * cost[plane + 2, pack, group, :]
            mixed = part if mixed is None else mixed + part
        vis_grad = -(spread(mixed, half, low) * rden)[None]
        for g in range(G):
            corr = corr_ref[plane, pl.ds(g * pairs, pairs), lanes].reshape(tiles, SUB, LANE)
            vis_grad = vis_grad + num_grads[g][None] * corr
        logit_grad = vis_grad * (sig * (1.0 - sig)) * (1.0 / GC)
        visible = (0.5 + sig) * (1.0 / GC)
        for g in range(G):
            corr_grad = visible * num_grads[g][None] + logit_grad * gates_ref[g][None]
            for j in range(0, GC, 2):
                c = g * GC + j
                span = pl.ds(c * pairs, 2 * pairs)
                both = jnp.concatenate(
                    [
                        (corr_grad * refx_ref[tile, pl.ds((c + i) * SUB, SUB), :][None]).reshape(
                            pairs, LANE
                        )
                        for i in range(2)
                    ],
                    axis=0,
                )
                rows[side, span, target] = both.astype(jnp.bfloat16)
                warped = (
                    warped_ref[plane, span, lanes]
                    .astype(jnp.float32)
                    .reshape(2, tiles, SUB, LANE)
                )
                for i in range(2):
                    dref[tile, pl.ds((c + i) * SUB, SUB), :] += jnp.sum(
                        corr_grad * warped[i], axis=0
                    )

    turns = count // 2

    def fetch(turn):
        slot = lax.rem(turn, 2)
        first = 2 * jnp.minimum(turn, turns - 1)
        return [
            pltpu.make_async_copy(
                w_ref.at[first + offset],
                held.at[slot, pl.ds(offset * pixels, pixels)],
                sems.at[slot, offset],
            )
            for offset in range(2)
        ]

    def matmul(side):
        product = jnp.dot(rows[side], held[side], preferred_element_type=jnp.float32)
        for tile in range(lane_tiles):
            acc[tile] += product[:, tile * LANE : (tile + 1) * LANE]

    for copy in fetch(0):
        copy.start()
    acc[...] = jnp.zeros_like(acc)
    dref[...] = jnp.zeros_like(dref)
    rows[1] = jnp.zeros_like(rows[1])
    held[1] = jnp.zeros_like(held[1])
    depth_conv(taps_ref, *halo_refs, regular_ref, cost, grad_ref, smooth)

    def two_planes(turn, carry):
        side = lax.rem(turn, 2)
        matmul(1 - side)
        for copy in fetch(turn + 1):
            copy.start()
        for offset in range(2):
            for tile in range(lane_tiles):
                vector(2 * turn + offset, tile, offset, side)
        for copy in fetch(turn):
            copy.wait()
        return carry

    lax.fori_loop(0, turns, two_planes, 0)
    matmul((turns - 1) % 2)
    for copy in fetch(turns):
        copy.wait()
    own_index = place_ref[0]
    parity = place_ref[1]
    blocks = keep_ref.shape[1] // SUB
    target = keep_ref
    for held_side in (1 - parity, parity):
        target[...] = jnp.zeros_like(target)
        for tile in range(lane_tiles):
            lanes = pl.ds(tile * LANE, LANE)
            for block in range(blocks):
                channel = (2 * block + held_side) * SUB
                part = pl.ds(block * SUB, SUB)
                for view in range(local_views):
                    total = None
                    for copy in range(SUB // local_views):
                        first = channel * SUB + copy * local_views + view
                        value = dref[tile, pl.ds(first, SUB, stride=SUB), :]
                        total = value if total is None else total + value
                    target[view, part, lanes] = total
        for pair in range(pairs):
            view = src_ref[pair % local_views, pair // local_views]
            slot = position(view, own_index, local_views, keep_ref.shape[0] // local_views)
            for block in range(blocks):
                first = (2 * block + held_side) * (SUB * pairs) + pair
                part = pl.ds(block * SUB, SUB)
                for tile in range(lane_tiles):
                    target[slot, part, pl.ds(tile * LANE, LANE)] += acc[
                        tile, pl.ds(first, SUB, stride=pairs), :
                    ]
        if held_side is not parity:
            send_ref[...] = target[...].astype(jnp.bfloat16)


def split_kernel(first, keep_ref, received_ref, after_ref, even_ref, send_ref):
    count = even_ref.shape[0]
    half = keep_ref.shape[0] // 2
    for out_ref, start in ((even_ref, first), (send_ref, half + first)):
        span = pl.ds(start, count)
        out_ref[...] = (keep_ref[span] + received_ref[span].astype(jnp.float32)).astype(
            out_ref.dtype
        )


def spread_kernel(even_ref, received_ref, *out_refs):
    size = out_refs[0].shape[0]
    for index, out_ref in enumerate(out_refs):
        span = pl.ds(index * size, size)
        out_ref[...] = (even_ref[span] + received_ref[span].astype(jnp.float32)).astype(
            out_ref.dtype
        )


SMEM = functools.partial(pl.BlockSpec, memory_space=pltpu.SMEM)


def shards(features, sources, warp_weights, view_gate, depth_kernel, cotangent):
    view_count = lax.axis_size("view")
    plane_count = lax.axis_size("plane")
    own_index = lax.axis_index("view")
    plane_index = lax.axis_index("plane")
    local_views, channels, pixels = features.shape
    all_views, per_view = sources.shape
    pairs = local_views * per_view
    planes = warp_weights.shape[0]
    share = channels // plane_count
    blocks = plane_count // 2
    parity = plane_index % 2
    f32 = jnp.float32
    bf16 = jnp.bfloat16
    near = [(i, i ^ 1) for i in range(plane_count)]
    far = [(i, i ^ 2) for i in range(plane_count)]
    up = [(i, i + 1) for i in range(plane_count - 1)]
    down = [(i + 1, i) for i in range(plane_count - 1)]
    shape = jax.ShapeDtypeStruct

    halves = features.reshape(local_views, blocks, 2, share, pixels)
    mine = lax.dynamic_index_in_dim(halves, parity, 2, keepdims=False).reshape(
        local_views, channels // 2, pixels
    )

    def over_view(array, k):
        return lax.ppermute(array, "view", [(i, i ^ k) for i in range(view_count)])

    quarter = max(view_count // 4, 1)
    even = [mine] + [over_view(mine, k) for k in range(2, view_count, 2)]
    near_even = jnp.concatenate(even[:quarter], axis=0)
    far_even = jnp.concatenate(even[quarter:], axis=0)
    packed = (pixels // (2 * LANE), G * SUB, LANE)
    hbm = pl.BlockSpec(memory_space=pltpu.HBM)
    anywhere = pl.BlockSpec(memory_space=pl.ANY)
    weights = pltpu.with_memory_space_constraint(warp_weights, pltpu.HBM)
    refx, gates, cot = pl.pallas_call(
        prep_kernel,
        out_shape=(
            shape((pixels // LANE, channels * SUB, LANE), f32),
            shape((G, SUB, LANE), f32),
            shape((planes,) + packed, f32),
        ),
        in_specs=[SMEM(), hbm, hbm],
        scratch_shapes=[
            pltpu.VMEM(features.shape, bf16),
            pltpu.VMEM(cotangent.shape, bf16),
            pltpu.SemaphoreType.DMA((2,)),
        ],
        compiler_params=params(4),
        cost_estimate=pl.CostEstimate(flops=10**9, bytes_accessed=4 * MIB, transcendentals=0),
        name="prep",
    )(
        pltpu.with_memory_space_constraint(view_gate, pltpu.HBM),
        pltpu.with_memory_space_constraint(features, pltpu.HBM),
        pltpu.with_memory_space_constraint(cotangent, pltpu.HBM),
    )
    far_even, refx, gates, cot = lax.optimization_barrier((far_even, refx, gates, cot))
    maps = [near_even, far_even, over_view(near_even, 1), over_view(far_even, 1)]
    maps = maps + [lax.ppermute(part, "plane", near) for part in maps]

    src_own = lax.dynamic_slice_in_dim(sources, own_index * local_views, local_views, 0)
    place = jnp.stack([own_index, parity]).astype(jnp.int32)
    saved = (
        pltpu.VMEM((planes, channels * pairs, pixels), bf16),
        pltpu.VMEM((planes, G * pairs, pixels), f32),
        pltpu.VMEM((planes, pairs, pixels), f32),
        pltpu.VMEM((planes, SUB, pixels), f32),
    )
    on_chip = functools.partial(pltpu.with_memory_space_constraint, memory_space=pltpu.VMEM)
    vmem = pl.BlockSpec(memory_space=pltpu.VMEM)
    scratch = [
        pltpu.VMEM((2, pixels, pixels), bf16),
        pltpu.SemaphoreType.DMA((2,)),
        pltpu.VMEM((channels * pairs, pixels), f32),
        pltpu.VMEM((channels * pairs, pixels), f32),
    ]
    load = (3,) + packed
    refx, gates, cot = [on_chip(item) for item in (refx, gates, cot)]
    *edge_saved, up_load, down_load, rows, following = pl.pallas_call(
        edge_kernel,
        out_shape=saved
        + (shape(load, f32),) * 2
        + (
            pltpu.VMEM((channels * pairs, pixels), bf16),
            pltpu.VMEM((pixels, pixels), bf16),
        ),
        in_specs=[SMEM()] * 2 + [vmem] * 2 + [hbm, vmem] + [vmem] * len(maps),
        out_specs=(vmem,) * 8,
        scratch_shapes=[
            pltpu.VMEM((2, all_views, channels // 2, pixels), bf16),
            pltpu.VMEM((pixels // LANE, channels * pairs, LANE), f32),
            pltpu.VMEM((4,) + packed, f32),
            pltpu.SemaphoreType.DMA,
        ]
        + scratch,
        compiler_params=params(12 + 4 * all_views * channels * pixels // MIB),
        name="forward_edge",
    )(src_own, place, gates, refx, weights, cot, *maps)
    rows, following = on_chip(rows), on_chip(following)
    below = lax.ppermute(up_load, "plane", up)
    above = lax.ppermute(down_load, "plane", down)
    inner_count = planes - 4
    *all_saved, inner_cost = pl.pallas_call(
        inner_kernel,
        out_shape=saved + (pltpu.VMEM((inner_count,) + packed, f32),),
        in_specs=[vmem] * 3 + [hbm, vmem] + [anywhere] * 4,
        out_specs=(vmem,) * 5,
        scratch_shapes=scratch,
        input_output_aliases={5 + i: i for i in range(4)},
        compiler_params=params(9),
        cost_estimate=pl.CostEstimate(
            flops=2 * channels * pairs * pixels * pixels * inner_count,
            bytes_accessed=40 * MIB,
            transcendentals=0,
        ),
        name="forward_inner",
    )(gates, rows, refx, weights, following, *[on_chip(item) for item in edge_saved])

    halo = (below, down_load, inner_cost, up_load, above, cot)
    returned = (all_views, channels // 2, pixels)
    regular, keep, send = pl.pallas_call(
        backward_kernel,
        out_shape=(shape(cotangent.shape, bf16), shape(returned, f32), shape(returned, bf16)),
        in_specs=[SMEM()] * 3 + [vmem, vmem, hbm] + [vmem] * 10,
        out_specs=(vmem,) * 3,
        scratch_shapes=[
            pltpu.VMEM((planes + 4,) + packed, f32),
            pltpu.VMEM((planes + 2,) + packed, f32),
            pltpu.VMEM((2,) + packed, f32),
            pltpu.VMEM((2, channels * pairs, 2 * pixels), bf16),
            pltpu.VMEM((pixels // LANE, channels * pairs, LANE), f32),
            pltpu.VMEM((pixels // LANE, channels * SUB, LANE), f32),
            pltpu.VMEM((2, 2 * pixels, pixels), bf16),
            pltpu.SemaphoreType.DMA((2, 2)),
        ],
        compiler_params=params(16 + 5 * all_views * channels * pixels // MIB),
        name="backward",
    )(
        src_own,
        place,
        pltpu.with_memory_space_constraint(depth_kernel, pltpu.HBM),
        gates,
        refx,
        weights,
        *halo,
        *[on_chip(item) for item in all_saved],
    )

    received = lax.ppermute(send, "plane", near)
    close = quarter * local_views
    piece = (local_views, channels // 2, pixels)

    def stage(first, count, after, kind):
        even_sum, outgoing = pl.pallas_call(
            functools.partial(split_kernel, first),
            out_shape=(shape((count,) + piece[1:], f32), shape((count,) + piece[1:], bf16)),
            in_specs=[pl.BlockSpec(), pl.BlockSpec(), anywhere],
            compiler_params=params(32),
            name="split",
        )(keep, received, after)
        incoming = over_view(outgoing, 1)
        return pl.pallas_call(
            spread_kernel,
            out_shape=(shape(piece, kind),) + (shape(piece, bf16),) * (count // local_views - 1),
            compiler_params=params(32),
            name="spread",
        )(even_sum, incoming)

    away_parts = stage(close, all_views // 2 - close, received, bf16)
    total, *close_parts = stage(0, close, away_parts[0], f32)
    for index, part in enumerate(away_parts):
        total = total + over_view(part, 2 * (quarter + index)).astype(f32)
    for index, part in enumerate(close_parts):
        total = total + over_view(part, 2 * (index + 1)).astype(f32)
    rounded = total.astype(bf16)
    total = rounded.astype(f32) + lax.ppermute(rounded, "plane", far).astype(f32)
    other = lax.ppermute(total, "plane", near)
    cut = (local_views, blocks, 1, share, pixels)
    is_mine = jnp.arange(2).reshape(1, 1, 2, 1, 1) == parity
    feature_grads = jnp.where(is_mine, total.reshape(cut), other.reshape(cut))
    return (regular, feature_grads.reshape(features.shape))


def solution(mesh):
    in_specs = (
        P("view", None, None),
        P(),
        P("plane", None, None),
        P(),
        P(),
        P("view", "plane", None, None),
    )
    out_specs = (P("view", "plane", None, None), P("view", None, None))
    return jax.shard_map(shards, mesh=mesh, in_specs=in_specs, out_specs=out_specs, check_vma=False)
```

```python
import functools

import jax
import jax.numpy as jnp
from jax import lax
from jax.experimental import pallas as pl
from jax.experimental.pallas import tpu as pltpu
from jax.sharding import PartitionSpec as P

G = 8
GC = 4
SUB = 8
LANE = 128
MIB = 1024 * 1024
NT = (((1,), (1,)), ((), ()))


def params(mib=16):
    return pltpu.CompilerParams(vmem_limit_bytes=mib * MIB)


def low_half():
    return lax.broadcasted_iota(jnp.int32, (SUB, LANE), 0) < SUB // 2


def swap_halves(tile):
    return pltpu.roll(tile, SUB // 2, 0)


def spread(tile, half, low):
    other = swap_halves(tile)
    return jnp.where(low, tile, other) if half == 0 else jnp.where(low, other, tile)


def pack_planes(array_ref, plane, out_ref, slot):
    local_views, _, groups, pixels = array_ref.shape
    for view in range(local_views):
        for tile in range(pixels // LANE):
            first = (tile % 2) * local_views + view
            out_ref[slot, tile // 2, pl.ds(first, groups, stride=SUB), :] = array_ref[
                view, plane, :, pl.ds(tile * LANE, LANE)
            ].astype(jnp.float32)


def prep_kernel(
    gate_ref, own_hbm, cot_hbm, refx_ref, gates_ref, cot_out, own_ref, cot_ref, sems
):
    copies = [
        pltpu.make_async_copy(own_hbm, own_ref, sems.at[0]),
        pltpu.make_async_copy(cot_hbm, cot_ref, sems.at[1]),
    ]
    for copy in copies:
        copy.start()
    for copy in copies:
        copy.wait()
    local_views, channels, pixels = own_ref.shape
    for tile in range(pixels // LANE):
        for view in range(local_views):
            own = own_ref[view, :, pl.ds(tile * LANE, LANE)].astype(jnp.float32)
            for copied in range(SUB // local_views):
                first = copied * local_views + view
                refx_ref[tile, pl.ds(first, channels, stride=SUB), :] = own
    for g in range(gates_ref.shape[0]):
        gates_ref[g] = jnp.full((SUB, LANE), gate_ref[g], jnp.float32)

    def pack_one(plane, carry):
        pack_planes(cot_ref, plane, cot_out, plane)
        return carry

    lax.fori_loop(0, cot_out.shape[0], pack_one, 0)


def position(view, own_index, local_views, view_count):
    distance = (view // local_views) ^ own_index
    place = distance // 2 + (distance % 2) * (view_count // 2)
    return place * local_views + view % local_views


def assemble(src_ref, place_ref, map_refs, rows_ref, maps, scratch):
    local_views, per_view = src_ref.shape
    tiles = scratch.shape[0]
    pairs = local_views * per_view
    view_count = maps.shape[1] // local_views
    blocks = maps.shape[2] // SUB
    own_index = place_ref[0]
    parity = place_ref[1]
    half = len(map_refs) // 2
    for side in range(2):
        first = 0
        for ref in map_refs[side * half : (side + 1) * half]:
            maps[side, first : first + ref.shape[0]] = ref[...]
            first += ref.shape[0]
    for pair in range(pairs):
        view = src_ref[pair % local_views, pair // local_views]
        slot = position(view, own_index, local_views, view_count)
        for tile in range(tiles):
            for side in range(2):
                values = maps[side, slot, :, pl.ds(tile * LANE, LANE)].astype(jnp.float32)
                held = parity if side == 0 else 1 - parity
                for block in range(blocks):
                    first = (2 * block + held) * (SUB * pairs) + pair
                    scratch[tile, pl.ds(first, SUB, stride=pairs), :] = values[
                        block * SUB : (block + 1) * SUB
                    ]
    for tile in range(tiles):
        rows_ref[:, pl.ds(tile * LANE, LANE)] = scratch[tile].astype(jnp.bfloat16)


def forward_vector(gates_ref, refx_ref, chunk, tile, plane, saved):
    warped_ref, corr_ref, sig_ref, rden_ref = saved
    pairs = sig_ref.shape[1]
    tiles = pairs // SUB
    lanes = pl.ds(tile * LANE, LANE)
    logits = None
    for g in range(G):
        total = None
        for j in range(0, GC, 2):
            c = g * GC + j
            span = pl.ds(c * pairs, 2 * pairs)
            both = chunk[span, lanes]
            warped_ref[plane, span, lanes] = both.astype(jnp.bfloat16)
            both = both.reshape(2, tiles, SUB, LANE)
            for i in range(2):
                part = both[i] * refx_ref[tile, pl.ds((c + i) * SUB, SUB), :][None]
                total = part if total is None else total + part
        corr = total * (1.0 / GC)
        corr_ref[plane, pl.ds(g * pairs, pairs), lanes] = corr.reshape(pairs, LANE)
        part = corr * gates_ref[g][None]
        logits = part if logits is None else logits + part
    sig = jax.nn.sigmoid(logits)
    sig_ref[plane, :, lanes] = sig.reshape(pairs, LANE)
    visible = 0.5 + sig
    den = jnp.sum(visible, axis=0)
    rden = 1.0 / (den + swap_halves(den))
    rden_ref[plane, :, lanes] = rden
    costs = []
    for g in range(G):
        corr = corr_ref[plane, pl.ds(g * pairs, pairs), lanes].reshape(tiles, SUB, LANE)
        num = jnp.sum(visible * corr, axis=0)
        costs.append((num + swap_halves(num)) * rden)
    return costs


def weight_copy(w_ref, plane, held, sems, slot):
    return pltpu.make_async_copy(w_ref.at[plane], held.at[slot], sems.at[slot])


def forward_body(count, plane_of, gates_ref, rows_ref, refx_ref, w_ref, saved, cost_ref, scratch):
    held, sems, *chunks = scratch
    low = low_half()

    def fetch(at, slot):
        return weight_copy(w_ref, plane_of(jnp.minimum(at, count - 1)), held, sems, slot)

    def matmul(slot):
        chunks[slot][...] = lax.dot_general(
            rows_ref[...], held[slot], NT, preferred_element_type=jnp.float32
        )

    def vector(slot, at):
        plane = plane_of(at)
        for index in range(2):
            costs = [
                forward_vector(gates_ref, refx_ref, chunks[slot], 2 * index + half, plane, saved)
                for half in range(2)
            ]
            for g in range(G):
                cost_ref[at, index, pl.ds(g * SUB, SUB), :] = jnp.where(
                    low, costs[0][g], costs[1][g]
                )

    def two_planes(turn, carry):
        first = 2 * turn
        for slot in range(2):
            fetch(first + slot, slot).wait()
            matmul(slot)
            fetch(first + slot + 2, slot).start()
            vector(1 - slot, jnp.maximum(first + slot - 1, 0))
        return carry

    lax.fori_loop(0, count // 2, two_planes, 0)
    vector(1, count - 1)
    for slot in range(2):
        fetch(count - 1, slot).wait()


def edge_plane(planes, index):
    return jnp.where(index < 2, index, planes - 4 + index)


def edge_kernel(src_ref, place_ref, gates_ref, refx_ref, w_ref, cot_ref, *rest):
    map_refs = rest[:8]
    saved = rest[8:12]
    up_ref, down_ref, rows_ref, next_ref = rest[12:16]
    maps, gathered, cost, next_sem, *scratch = rest[16:]
    held, sems, *_ = scratch
    planes = w_ref.shape[0]
    weight_copy(w_ref, 0, held, sems, 0).start()
    weight_copy(w_ref, 1, held, sems, 1).start()
    following = pltpu.make_async_copy(w_ref.at[2], next_ref, next_sem)
    following.start()
    assemble(src_ref, place_ref, map_refs, rows_ref, maps, gathered)
    forward_body(
        4,
        functools.partial(edge_plane, planes),
        gates_ref,
        rows_ref,
        refx_ref,
        w_ref,
        saved,
        cost,
        scratch,
    )
    down_ref[0:2] = cost[0:2]
    up_ref[0:2] = cost[2:4]
    down_ref[2] = cot_ref[0]
    up_ref[2] = cot_ref[planes - 1]
    following.wait()


def inner_kernel(gates_ref, rows_ref, refx_ref, w_ref, next_ref, *rest):
    cost_ref, *scratch = rest[8:]
    held, sems, *_ = scratch
    weight_copy(w_ref, 3, held, sems, 1).start()
    first = pltpu.make_async_copy(next_ref, held.at[0], sems.at[0])
    first.start()
    forward_body(
        cost_ref.shape[0],
        lambda index: index + 2,
        gates_ref,
        rows_ref,
        refx_ref,
        w_ref,
        rest[4:8],
        cost_ref,
        scratch,
    )


def depth_conv(
    taps_ref,
    below_ref,
    down_ref,
    inner_ref,
    up_ref,
    above_ref,
    cot_ref,
    regular_ref,
    cost,
    grad_ref,
    slope,
    smooth,
):
    planes = grad_ref.shape[0]
    local_views, _, groups, pixels = regular_ref.shape
    cost[0:2] = below_ref[0:2]
    cost[2:4] = down_ref[0:2]
    cost[4:planes] = inner_ref[...]
    cost[planes : planes + 2] = up_ref[0:2]
    cost[planes + 2 : planes + 4] = above_ref[0:2]
    slope[0] = below_ref[2]
    slope[1 : planes + 1] = cot_ref[...]
    slope[planes + 1] = above_ref[2]

    def mix(source, tap):
        totals = [None] * G
        for k in range(3):
            for b in range(G):
                value = source(k, b)
                for a in range(G):
                    part = value * tap(k, a, b)
                    totals[a] = part if totals[a] is None else totals[a] + part
        return totals

    def forward_planes(index, carry):
        plane = 2 * index
        pres = mix(
            lambda k, g: cost[pl.ds(plane + k, 2), :, pl.ds(g * SUB, SUB), :],
            lambda k, o, g: taps_ref[k, o, g],
        )
        for o in range(G):
            pre = pres[o]
            rows = pl.ds(o * SUB, SUB)
            sig = jax.nn.sigmoid(pre)
            both = pl.ds(plane, 2)
            slope[both, :, rows, :] = slope[both, :, rows, :] * (sig * (1.0 + pre * (1.0 - sig)))
            smooth[both, :, rows, :] = pre * sig
        return carry

    lax.fori_loop(0, (planes + 2) // 2, forward_planes, 0)

    def backward_planes(index, carry):
        plane = 2 * index
        grads = mix(
            lambda k, o: slope[pl.ds(plane + 2 - k, 2), :, pl.ds(o * SUB, SUB), :],
            lambda k, g, o: taps_ref[k, o, g],
        )
        for g in range(G):
            grad_ref[pl.ds(plane, 2), :, pl.ds(g * SUB, SUB), :] = grads[g]
        for view in range(local_views):
            for tile in range(pixels // LANE):
                first = (tile % 2) * local_views + view
                for i in range(2):
                    regular_ref[view, plane + i, :, pl.ds(tile * LANE, LANE)] = smooth[
                        plane + i + 1, tile // 2, pl.ds(first, groups, stride=SUB), :
                    ].astype(jnp.bfloat16)
        return carry

    lax.fori_loop(0, planes // 2, backward_planes, 0)


def backward_kernel(src_ref, place_ref, taps_ref, gates_ref, refx_ref, w_ref, *rest):
    halo_refs = rest[:6]
    warped_ref, corr_ref, sig_ref, rden_ref = rest[6:10]
    regular_ref, keep_ref, send_ref = rest[10:13]
    cost, grad_ref, slope, smooth, rows, acc, dref, held, sems = rest[13:]
    count = w_ref.shape[0]
    pairs = sig_ref.shape[1]
    tiles = pairs // SUB
    lane_tiles = dref.shape[0]
    pixels = sig_ref.shape[2]
    local_views = src_ref.shape[0]
    low = low_half()

    def vector(plane, tile, offset):
        lanes = pl.ds(tile * LANE, LANE)
        target = pl.ds(offset * pixels + tile * LANE, LANE)
        pack = tile // 2
        half = tile % 2
        rden = rden_ref[plane, :, lanes]
        sig = sig_ref[plane, :, lanes].reshape(tiles, SUB, LANE)
        num_grads = []
        mixed = None
        for g in range(G):
            group = pl.ds(g * SUB, SUB)
            grad = grad_ref[plane, pack, group, :]
            num_grads.append(spread(grad, half, low) * rden)
            part = grad * cost[plane + 2, pack, group, :]
            mixed = part if mixed is None else mixed + part
        vis_grad = -(spread(mixed, half, low) * rden)[None]
        for g in range(G):
            corr = corr_ref[plane, pl.ds(g * pairs, pairs), lanes].reshape(tiles, SUB, LANE)
            vis_grad = vis_grad + num_grads[g][None] * corr
        logit_grad = vis_grad * (sig * (1.0 - sig)) * (1.0 / GC)
        visible = (0.5 + sig) * (1.0 / GC)
        for g in range(G):
            corr_grad = visible * num_grads[g][None] + logit_grad * gates_ref[g][None]
            for j in range(0, GC, 2):
                c = g * GC + j
                span = pl.ds(c * pairs, 2 * pairs)
                both = jnp.concatenate(
                    [
                        (corr_grad * refx_ref[tile, pl.ds((c + i) * SUB, SUB), :][None]).reshape(
                            pairs, LANE
                        )
                        for i in range(2)
                    ],
                    axis=0,
                )
                rows[span, target] = both.astype(jnp.bfloat16)
                warped = (
                    warped_ref[plane, span, lanes]
                    .astype(jnp.float32)
                    .reshape(2, tiles, SUB, LANE)
                )
                for i in range(2):
                    dref[tile, pl.ds((c + i) * SUB, SUB), :] += jnp.sum(
                        corr_grad * warped[i], axis=0
                    )

    group = rows.shape[1] // pixels

    def fetch(turn, offset):
        return pltpu.make_async_copy(
            w_ref.at[turn * group + offset],
            held.at[pl.ds(offset * pixels, pixels)],
            sems.at[offset],
        )

    acc[...] = jnp.zeros_like(acc)
    dref[...] = jnp.zeros_like(dref)
    depth_conv(taps_ref, *halo_refs, regular_ref, cost, grad_ref, slope, smooth)

    def one_turn(turn, carry):
        for offset in range(group):
            fetch(turn, offset).start()
        for offset in range(group):
            for tile in range(lane_tiles):
                vector(turn * group + offset, tile, offset)
        for offset in range(group):
            fetch(turn, offset).wait()
        product = jnp.dot(rows[...], held[...], preferred_element_type=jnp.float32)
        for tile in range(lane_tiles):
            acc[tile] += product[:, tile * LANE : (tile + 1) * LANE]
        return carry

    lax.fori_loop(0, count // group, one_turn, 0)
    own_index = place_ref[0]
    parity = place_ref[1]
    blocks = keep_ref.shape[1] // SUB
    target = keep_ref
    for held_side in (1 - parity, parity):
        target[...] = jnp.zeros_like(target)
        for tile in range(lane_tiles):
            lanes = pl.ds(tile * LANE, LANE)
            for block in range(blocks):
                channel = (2 * block + held_side) * SUB
                part = pl.ds(block * SUB, SUB)
                for view in range(local_views):
                    total = None
                    for copy in range(SUB // local_views):
                        first = channel * SUB + copy * local_views + view
                        value = dref[tile, pl.ds(first, SUB, stride=SUB), :]
                        total = value if total is None else total + value
                    target[view, part, lanes] = total
        for pair in range(pairs):
            view = src_ref[pair % local_views, pair // local_views]
            slot = position(view, own_index, local_views, keep_ref.shape[0] // local_views)
            for block in range(blocks):
                first = (2 * block + held_side) * (SUB * pairs) + pair
                part = pl.ds(block * SUB, SUB)
                for tile in range(lane_tiles):
                    target[slot, part, pl.ds(tile * LANE, LANE)] += acc[
                        tile, pl.ds(first, SUB, stride=pairs), :
                    ]
        if held_side is not parity:
            send_ref[...] = target[...].astype(jnp.bfloat16)


def split_kernel(first, keep_ref, received_ref, after_ref, even_ref, send_ref):
    count = even_ref.shape[0]
    half = keep_ref.shape[0] // 2
    for out_ref, start in ((even_ref, first), (send_ref, half + first)):
        span = pl.ds(start, count)
        out_ref[...] = (keep_ref[span] + received_ref[span].astype(jnp.float32)).astype(
            out_ref.dtype
        )


def spread_kernel(even_ref, received_ref, *out_refs):
    size = out_refs[0].shape[0]
    for index, out_ref in enumerate(out_refs):
        span = pl.ds(index * size, size)
        out_ref[...] = (even_ref[span] + received_ref[span].astype(jnp.float32)).astype(
            out_ref.dtype
        )


SMEM = functools.partial(pl.BlockSpec, memory_space=pltpu.SMEM)


def shards(features, sources, warp_weights, view_gate, depth_kernel, cotangent):
    view_count = lax.axis_size("view")
    plane_count = lax.axis_size("plane")
    own_index = lax.axis_index("view")
    plane_index = lax.axis_index("plane")
    local_views, channels, pixels = features.shape
    all_views, per_view = sources.shape
    pairs = local_views * per_view
    planes = warp_weights.shape[0]
    share = channels // plane_count
    blocks = plane_count // 2
    parity = plane_index % 2
    f32 = jnp.float32
    bf16 = jnp.bfloat16
    near = [(i, i ^ 1) for i in range(plane_count)]
    far = [(i, i ^ 2) for i in range(plane_count)]
    up = [(i, i + 1) for i in range(plane_count - 1)]
    down = [(i + 1, i) for i in range(plane_count - 1)]
    shape = jax.ShapeDtypeStruct

    halves = features.reshape(local_views, blocks, 2, share, pixels)
    mine = lax.dynamic_index_in_dim(halves, parity, 2, keepdims=False).reshape(
        local_views, channels // 2, pixels
    )

    def over_view(array, k):
        return lax.ppermute(array, "view", [(i, i ^ k) for i in range(view_count)])

    quarter = max(view_count // 4, 1)
    even = [mine] + [over_view(mine, k) for k in range(2, view_count, 2)]
    near_even = jnp.concatenate(even[:quarter], axis=0)
    far_even = jnp.concatenate(even[quarter:], axis=0)
    packed = (pixels // (2 * LANE), G * SUB, LANE)
    hbm = pl.BlockSpec(memory_space=pltpu.HBM)
    anywhere = pl.BlockSpec(memory_space=pl.ANY)
    weights = pltpu.with_memory_space_constraint(warp_weights, pltpu.HBM)
    refx, gates, cot = pl.pallas_call(
        prep_kernel,
        out_shape=(
            shape((pixels // LANE, channels * SUB, LANE), f32),
            shape((G, SUB, LANE), f32),
            shape((planes,) + packed, f32),
        ),
        in_specs=[SMEM(), hbm, hbm],
        scratch_shapes=[
            pltpu.VMEM(features.shape, bf16),
            pltpu.VMEM(cotangent.shape, bf16),
            pltpu.SemaphoreType.DMA((2,)),
        ],
        compiler_params=params(4),
        cost_estimate=pl.CostEstimate(flops=10**9, bytes_accessed=4 * MIB, transcendentals=0),
        name="prep",
    )(
        pltpu.with_memory_space_constraint(view_gate, pltpu.HBM),
        pltpu.with_memory_space_constraint(features, pltpu.HBM),
        pltpu.with_memory_space_constraint(cotangent, pltpu.HBM),
    )
    far_even, refx, gates, cot = lax.optimization_barrier((far_even, refx, gates, cot))
    maps = [near_even, far_even, over_view(near_even, 1), over_view(far_even, 1)]
    maps = maps + [lax.ppermute(part, "plane", near) for part in maps]

    src_own = lax.dynamic_slice_in_dim(sources, own_index * local_views, local_views, 0)
    place = jnp.stack([own_index, parity]).astype(jnp.int32)
    saved = (
        pltpu.VMEM((planes, channels * pairs, pixels), bf16),
        pltpu.VMEM((planes, G * pairs, pixels), f32),
        pltpu.VMEM((planes, pairs, pixels), f32),
        pltpu.VMEM((planes, SUB, pixels), f32),
    )
    on_chip = functools.partial(pltpu.with_memory_space_constraint, memory_space=pltpu.VMEM)
    vmem = pl.BlockSpec(memory_space=pltpu.VMEM)
    scratch = [
        pltpu.VMEM((2, pixels, pixels), bf16),
        pltpu.SemaphoreType.DMA((2,)),
        pltpu.VMEM((channels * pairs, pixels), f32),
        pltpu.VMEM((channels * pairs, pixels), f32),
    ]
    load = (3,) + packed
    refx, gates, cot = [on_chip(item) for item in (refx, gates, cot)]
    *edge_saved, up_load, down_load, rows, following = pl.pallas_call(
        edge_kernel,
        out_shape=saved
        + (shape(load, f32),) * 2
        + (
            pltpu.VMEM((channels * pairs, pixels), bf16),
            pltpu.VMEM((pixels, pixels), bf16),
        ),
        in_specs=[SMEM()] * 2 + [vmem] * 2 + [hbm, vmem] + [vmem] * len(maps),
        out_specs=(vmem,) * 8,
        scratch_shapes=[
            pltpu.VMEM((2, all_views, channels // 2, pixels), bf16),
            pltpu.VMEM((pixels // LANE, channels * pairs, LANE), f32),
            pltpu.VMEM((4,) + packed, f32),
            pltpu.SemaphoreType.DMA,
        ]
        + scratch,
        compiler_params=params(12 + 4 * all_views * channels * pixels // MIB),
        name="forward_edge",
    )(src_own, place, gates, refx, weights, cot, *maps)
    rows, following = on_chip(rows), on_chip(following)
    below = lax.ppermute(up_load, "plane", up)
    above = lax.ppermute(down_load, "plane", down)
    inner_count = planes - 4
    *all_saved, inner_cost = pl.pallas_call(
        inner_kernel,
        out_shape=saved + (pltpu.VMEM((inner_count,) + packed, f32),),
        in_specs=[vmem] * 3 + [hbm, vmem] + [anywhere] * 4,
        out_specs=(vmem,) * 5,
        scratch_shapes=scratch,
        input_output_aliases={5 + i: i for i in range(4)},
        compiler_params=params(9),
        cost_estimate=pl.CostEstimate(
            flops=2 * channels * pairs * pixels * pixels * inner_count,
            bytes_accessed=40 * MIB,
            transcendentals=0,
        ),
        name="forward_inner",
    )(gates, rows, refx, weights, following, *[on_chip(item) for item in edge_saved])

    halo = (below, down_load, inner_cost, up_load, above, cot)
    returned = (all_views, channels // 2, pixels)
    group = max(size for size in (3, 2, 1) if planes % size == 0)
    regular, keep, send = pl.pallas_call(
        backward_kernel,
        out_shape=(shape(cotangent.shape, bf16), shape(returned, f32), shape(returned, bf16)),
        in_specs=[SMEM()] * 3 + [vmem, vmem, hbm] + [vmem] * 10,
        out_specs=(vmem,) * 3,
        scratch_shapes=[
            pltpu.VMEM((planes + 4,) + packed, f32),
            pltpu.VMEM((planes,) + packed, f32),
            pltpu.VMEM((planes + 2,) + packed, f32),
            pltpu.VMEM((planes + 2,) + packed, f32),
            pltpu.VMEM((channels * pairs, group * pixels), bf16),
            pltpu.VMEM((pixels // LANE, channels * pairs, LANE), f32),
            pltpu.VMEM((pixels // LANE, channels * SUB, LANE), f32),
            pltpu.VMEM((group * pixels, pixels), bf16),
            pltpu.SemaphoreType.DMA((group,)),
        ],
        compiler_params=params(14 + 5 * all_views * channels * pixels // MIB),
        name="backward",
    )(
        src_own,
        place,
        pltpu.with_memory_space_constraint(depth_kernel, pltpu.HBM),
        gates,
        refx,
        weights,
        *halo,
        *[on_chip(item) for item in all_saved],
    )

    received = lax.ppermute(send, "plane", near)
    close = quarter * local_views
    piece = (local_views, channels // 2, pixels)

    def stage(first, count, after, kind):
        even_sum, outgoing = pl.pallas_call(
            functools.partial(split_kernel, first),
            out_shape=(shape((count,) + piece[1:], f32), shape((count,) + piece[1:], bf16)),
            in_specs=[pl.BlockSpec(), pl.BlockSpec(), anywhere],
            compiler_params=params(32),
            name="split",
        )(keep, received, after)
        incoming = over_view(outgoing, 1)
        return pl.pallas_call(
            spread_kernel,
            out_shape=(shape(piece, kind),) + (shape(piece, bf16),) * (count // local_views - 1),
            compiler_params=params(32),
            name="spread",
        )(even_sum, incoming)

    away_parts = stage(close, all_views // 2 - close, received, bf16)
    total, *close_parts = stage(0, close, away_parts[0], f32)
    for index, part in enumerate(away_parts):
        total = total + over_view(part, 2 * (quarter + index)).astype(f32)
    for index, part in enumerate(close_parts):
        total = total + over_view(part, 2 * (index + 1)).astype(f32)
    rounded = total.astype(bf16)
    total = rounded.astype(f32) + lax.ppermute(rounded, "plane", far).astype(f32)
    other = lax.ppermute(total, "plane", near)
    cut = (local_views, blocks, 1, share, pixels)
    first = jnp.where(parity == 0, total, other).reshape(cut)
    second = jnp.where(parity == 0, other, total).reshape(cut)
    feature_grads = jnp.concatenate([first, second], axis=2).reshape(features.shape)
    return (regular, feature_grads)


def solution(mesh):
    in_specs = (
        P("view", None, None),
        P(),
        P("plane", None, None),
        P(),
        P(),
        P("view", "plane", None, None),
    )
    out_specs = (P("view", "plane", None, None), P("view", None, None))
    return jax.shard_map(shards, mesh=mesh, in_specs=in_specs, out_specs=out_specs, check_vma=False)
```
